256 devices in a mesh: seq: 64 (over y, z, core), dp: 4 (over x).
Axes of the slice: x: 4, y: 4, z: 8, core: 2. Of those that a mesh axis runs over, the one named last changes fastest.
Arguments:
- tokens: bfloat16 [4, 8192, 768], P('dp', 'seq'), may hold values from -6 to 6
- cotangent: bfloat16 [4, 8192, 768], P('dp', 'seq'), may hold values from -6 to 6
- qkv_weight: bfloat16 [2304, 768], replicated, may hold values from -0.21875 to 0.21875
- out_weight: bfloat16 [768, 768], replicated, may hold values from -0.21875 to 0.21875
- logit_scale: float32 [12], replicated, may hold values from 4 to 24
- near_offsets: int32 [12], replicated, may hold values from 0 to 7
- far_offsets: int32 [12], replicated, may hold values from 0 to 63
Outputs:
- branch: bfloat16 [4, 8192, 768], P('dp', 'seq')
- grad_tokens: bfloat16 [4, 8192, 768], P('dp', 'seq')
- qkv_grad: float32 [2304, 768], P(('seq', 'dp'))
- out_grad: float32 [768, 768], P(('seq', 'dp'))
The draws below stay inside these ranges and needn't reach their ends.
All inputs are finite; a program needn't handle non-finite values.
Results may differ from the reference program's by a relative error of at most 0.014.
Values may be sent and summed in bfloat16 or wider, within the bound.
A program may use at most 128 MiB of HBM per device.

```python
import math
import jax
import jax.numpy as jnp
from jax import lax

HEADS = 12
D = 768
TOK_DEV = 128
SPAN = 8
LENGTH = 8192
BATCH = 4
N_SEQ = 64


def plant(array, stream_key, least, largest):
    longest = array.shape.index(max(array.shape))
    spots = []
    for shift in (0, 1):
        where = [jax.random.randint(jax.random.fold_in(stream_key, axis), (), 0, length) for axis, length in enumerate(array.shape)]
        where[longest] = (where[longest] + shift) % array.shape[longest]
        spots.append(tuple(where))
    return array.at[spots[0]].set(least).at[spots[1]].set(largest)


def steps_of(key, shape, shards, low, top_value):
    gain = 1.0
    for position, parts in shards:
        steps = jax.random.uniform(jax.random.fold_in(jax.random.fold_in(key, 6), position), (parts,), jnp.float32, low / len(shards), top_value / len(shards))
        gain = gain * jnp.repeat(jnp.exp(steps), shape[position] // parts).reshape((-1,) + (1,) * (len(shape) - 1 - position))
    return gain


def scatter_about(key, dims, scale, reach, split=(), held_as=jnp.bfloat16):
    entries = scale * jax.random.normal(key, dims, jnp.float32)
    if split:
        entries = entries * steps_of(key, dims, split, -0.22, 0.18)
    return jnp.clip(entries, -reach, reach).astype(held_as)


def setup_inputs(seed: int = 0) -> dict:
    seeds = jax.random.split(jax.random.key(seed), 8)
    return {
        "tokens": scatter_about(seeds[0], (BATCH, LENGTH, D), 1.0, 6.0, ((0, 4), (1, 64))),
        "cotangent": scatter_about(seeds[1], (BATCH, LENGTH, D), 1.0, 6.0, ((0, 4), (1, 64))),
        "qkv_weight": scatter_about(seeds[2], (3 * D, D), D ** -0.5, 0.21875),
        "out_weight": scatter_about(seeds[3], (D, D), D ** -0.5, 0.21875),
        "logit_scale": jnp.clip(jnp.exp(jax.random.uniform(seeds[4], (HEADS,), jnp.float32, math.log(4.0), math.log(24.0))), 4.0, 24.0),
        "near_offsets": plant(jax.random.randint(seeds[5], (HEADS,), 0, SPAN), jax.random.fold_in(seeds[5], 1), 0, SPAN - 1).astype(jnp.int32),
        "far_offsets": plant(jax.random.randint(seeds[6], (HEADS,), 0, N_SEQ), jax.random.fold_in(seeds[6], 1), 0, N_SEQ - 1).astype(jnp.int32),
    }


EPS = 1e-06

def level_mask(offsets, dilation):
    return jnp.arange(dilation, dtype=jnp.int32)[:, None] == offsets[None, :].astype(jnp.int32)

def dilate(values, pick_mask):
    dilation = pick_mask.shape[0]
    shaped = values.reshape((values.shape[0] // dilation, dilation) + values.shape[1:])
    pick = pick_mask.reshape(pick_mask.shape + (1,) * (values.ndim - 2))
    return lax.optimization_barrier(jnp.sum(jnp.where(pick[None], shaped, jnp.zeros((), values.dtype)), axis=1)).astype(values.dtype)

def undilate(values, pick_mask):
    dilation = pick_mask.shape[0]
    pick = pick_mask.reshape(pick_mask.shape + (1,) * (values.ndim - 2))
    spread = jnp.where(pick[None], values[:, None], jnp.zeros((), values.dtype))
    return spread.reshape((values.shape[0] * dilation,) + values.shape[1:])

def widen(values):
    return values.astype(jnp.float32)

def rounded(values):
    return lax.optimization_barrier(values.astype(jnp.bfloat16)).astype(jnp.float32)

def block_forward(query_rows, key_rows, value_rows, logit_scale):
    scores = jnp.einsum('qhe,khe->hqk', widen(query_rows), widen(key_rows)) * logit_scale[:, None, None]
    weights = jnp.exp(scores)
    denominator = lax.optimization_barrier(jnp.sum(weights, axis=2)).T
    numerator = jnp.einsum('hqk,khe->qhe', rounded(weights), widen(value_rows))
    return (numerator, denominator)

def block_backward(query_rows, key_rows, value_rows, grad_rows, row_delta, inverse_den, logit_scale):
    scores = jnp.einsum('qhe,khe->hqk', widen(query_rows), widen(key_rows)) * logit_scale[:, None, None]
    probs = jnp.exp(scores) * inverse_den.T[:, :, None]
    grad_probs = jnp.einsum('qhe,khe->hqk', widen(grad_rows), widen(value_rows))
    grad_scores = rounded(logit_scale[:, None, None] * probs * (grad_probs - row_delta.T[:, :, None]))
    grad_query = jnp.einsum('hqk,khe->qhe', grad_scores, widen(key_rows))
    grad_key = jnp.einsum('hqk,qhe->khe', grad_scores, widen(query_rows))
    grad_value = jnp.einsum('hqk,qhe->khe', rounded(probs), widen(grad_rows))
    return (grad_query, grad_key, grad_value)

def normalize(rows):
    wide = rows.astype(jnp.float32)
    inverse = lax.rsqrt(lax.optimization_barrier(jnp.sum(wide * wide, axis=-1)) + EPS)
    return (inverse, wide * inverse[..., None])

def unnormalize(inverse, unit, grad_unit):
    return inverse[..., None] * (grad_unit - unit * lax.optimization_barrier(jnp.sum(unit * grad_unit, axis=-1, keepdims=True)))

def sequence(tokens, cotangent, qkv_weight, out_weight, logit_scale, levels):
    length, width = tokens.shape
    head_count = logit_scale.shape[0]
    head_size = width // head_count
    qkv = jnp.dot(tokens, qkv_weight.T, preferred_element_type=jnp.float32).astype(jnp.bfloat16)
    query = qkv[:, :width].reshape(length, head_count, head_size)
    key = qkv[:, width:2 * width].reshape(length, head_count, head_size)
    value = qkv[:, 2 * width:].reshape(length, head_count, head_size)
    query_inverse, query_unit = normalize(query)
    key_inverse, key_unit = normalize(key)
    query_norm = query_unit.astype(jnp.bfloat16)
    key_norm = key_unit.astype(jnp.bfloat16)
    numerator = jnp.zeros((length, head_count, head_size), jnp.float32)
    denominator = jnp.zeros((length, head_count), jnp.float32)
    for dilation, offsets in levels:
        pick_mask = level_mask(offsets, dilation)
        segments = length // (dilation * TOK_DEV)

        def split_rows(values):
            picked = dilate(values, pick_mask)
            return picked.reshape((segments, TOK_DEV) + picked.shape[1:])

        def forward_segment(triple):
            return block_forward(triple[0], triple[1], triple[2], logit_scale)
        seg_num, seg_den = lax.map(forward_segment, (split_rows(query_norm), split_rows(key_norm), split_rows(value)))
        numerator = numerator + undilate(seg_num.reshape((-1, head_count, head_size)), pick_mask)
        denominator = denominator + undilate(seg_den.reshape((-1, head_count)), pick_mask)
    attn = (numerator / denominator[..., None]).astype(jnp.bfloat16)
    attn_flat = attn.reshape(length, width)
    branch = jnp.dot(attn_flat, out_weight, preferred_element_type=jnp.float32).astype(jnp.bfloat16)
    grad_attn = jnp.dot(cotangent, out_weight.T, preferred_element_type=jnp.float32).astype(jnp.bfloat16)
    grad_attn = grad_attn.reshape(length, head_count, head_size)
    row_delta = lax.optimization_barrier(jnp.sum(grad_attn.astype(jnp.float32) * attn.astype(jnp.float32), axis=-1))
    inverse_den = 1.0 / denominator
    grad_qn = jnp.zeros((length, head_count, head_size), jnp.float32)
    grad_kn = jnp.zeros((length, head_count, head_size), jnp.float32)
    grad_value = jnp.zeros((length, head_count, head_size), jnp.float32)
    for dilation, offsets in levels:
        pick_mask = level_mask(offsets, dilation)
        segments = length // (dilation * TOK_DEV)

        def split_rows(values):
            picked = dilate(values, pick_mask)
            return picked.reshape((segments, TOK_DEV) + picked.shape[1:])

        def backward_segment(inputs):
            return block_backward(inputs[0], inputs[1], inputs[2], inputs[3], inputs[4], inputs[5], logit_scale)
        seg_q, seg_k, seg_v = lax.map(backward_segment, (split_rows(query_norm), split_rows(key_norm), split_rows(value), split_rows(grad_attn), split_rows(row_delta), split_rows(inverse_den)))
        grad_qn = grad_qn + undilate(seg_q.reshape((-1, head_count, head_size)), pick_mask)
        grad_kn = grad_kn + undilate(seg_k.reshape((-1, head_count, head_size)), pick_mask)
        grad_value = grad_value + undilate(seg_v.reshape((-1, head_count, head_size)), pick_mask)
    grad_query = unnormalize(query_inverse, query_unit, grad_qn)
    grad_key = unnormalize(key_inverse, key_unit, grad_kn)
    grad_qkv = jnp.concatenate([grad_query.reshape(length, width), grad_key.reshape(length, width), grad_value.reshape(length, width)], axis=1).astype(jnp.bfloat16)
    grad_tokens = jnp.dot(grad_qkv, qkv_weight, preferred_element_type=jnp.float32).astype(jnp.bfloat16)
    qkv_term = jnp.dot(grad_qkv.T, tokens, preferred_element_type=jnp.float32)
    out_term = jnp.dot(attn_flat.T, cotangent, preferred_element_type=jnp.float32)
    return (branch, grad_tokens, qkv_term, out_term)

def reference(tokens, cotangent, qkv_weight, out_weight, logit_scale, near_offsets, far_offsets):
    levels = ((1, jnp.zeros_like(near_offsets)), (SPAN, near_offsets), (N_SEQ, far_offsets))

    def one_sequence(pair):
        return sequence(pair[0], pair[1], qkv_weight, out_weight, logit_scale, levels)
    branch, grad_tokens, qkv_terms, out_terms = lax.map(one_sequence, (tokens, cotangent))
    return (branch, grad_tokens, lax.optimization_barrier(jnp.sum(qkv_terms, axis=0)), lax.optimization_barrier(jnp.sum(out_terms, axis=0)))
```

```python
import jax
import jax.numpy as jnp
import numpy as np
from jax import lax
from jax.experimental import pallas as pl
from jax.experimental.pallas import tpu as pltpu
from jax.sharding import PartitionSpec as P

BF = jnp.bfloat16
F32 = jnp.float32
MESH = pl.DeviceIdType.MESH
EPS = 1e-06

NY, NZ, NX = 4, 8, 4
TOK = 128
WIDTH = 768
HEADS = 12
HEAD = 64
GROUP = 4
LANES = GROUP * HEAD
GROUPS = HEADS // GROUP
SPAN = 8
NEAR = TOK // SPAN
FAR = 2
PACK = 4 * FAR * WIDTH // 128
HALF = WIDTH // 2
QROWS = 3 * WIDTH // NY
OROWS = WIDTH // NY
PIECE = QROWS + OROWS
QZ, OZ = QROWS // NZ, OROWS // NZ
ZROWS = QZ + OZ


def nn(a, b):
    return lax.dot_general(a, b, (((1,), (0,)), ((), ())), preferred_element_type=F32)


def nt(a, b):
    return lax.dot_general(a, b, (((1,), (1,)), ((), ())), preferred_element_type=F32)


def tn(a, b):
    return lax.dot_general(a, b, (((0,), (0,)), ((), ())), preferred_element_type=F32)


def split(x):
    high = x.astype(BF)
    return high, (x - high.astype(F32)).astype(BF)


def iota(shape, dim):
    return lax.broadcasted_iota(jnp.int32, shape, dim)


def place():
    seq = lax.axis_index("seq")
    return seq, lax.rem(seq, 2), lax.rem(seq // 2, NZ), seq // (2 * NZ)


def at(y, z, core):
    return {"seq": (y * NZ + z) * 2 + core}


def remote(src, dst, send, recv, device):
    return pltpu.make_async_remote_copy(
        src_ref=src, dst_ref=dst, send_sem=send, recv_sem=recv, device_id=device, device_id_type=MESH
    )


def greet(devices):
    barrier = pltpu.get_barrier_semaphore()
    for device in devices:
        pl.semaphore_signal(barrier, inc=1, device_id=device, device_id_type=MESH)
    pl.semaphore_wait(barrier, len(devices))


def lanes_of(b):
    return slice(b * LANES, (b + 1) * LANES)


def attention(
    scale_ref, near_ref, far_ref, tok_ref, cot_ref, wqkv_ref, wout_ref, block_ref, compact_ref, order_ref,
    branch_ref, attn_ref, dqkv_ref,
    qkv, qn, kn, gr, inv_q, inv_k, p_loc, p_near, p_far, num, den, dq, dk, dv, pack,
    near_kv, near_qg, near_s, far_z, far_kv, far_qg, far_sz, far_s,
    s_nkv, r_nkv, s_nqg, r_nqg, s_ns, r_ns, s_fz, r_fz, s_fsz, r_fsz,
    s_fkv, r_fkv, s_fqg, r_fqg, s_fs, r_fs, s_ckv, r_ckv, s_cqg, r_cqg, s_cs, r_cs,
):
    seq, core, z, y = place()
    mine = lax.rem(seq, SPAN)
    base = seq - mine
    other = 1 - core
    near_peers = [lax.rem(mine + d, SPAN) for d in range(1, SPAN)]
    z_peers = [lax.rem(z + d, NZ) for d in range(1, NZ)]
    y_peers = [lax.rem(y + d, NY) for d in range(1, NY)]
    quad = mine // 2
    greet(
        [at(y, t, core) for t in z_peers]
        + [{"seq": base + 2 * lax.rem(quad + d, SPAN // 2) + other} for d in range(SPAN // 2)]
        + [at(t, z, core) for t in y_peers]
    )
    sent = []

    def send(src, dst, ssem, rsem, device):
        copy = remote(src, dst, ssem, rsem, device)
        copy.start()
        sent.append(copy)

    def arrived(ref, ssem, rsem):
        remote(ref, ref, ssem, rsem, {"seq": seq}).wait_recv()

    head_lane = iota((1, LANES), 1) // HEAD
    picks_f = [(head_lane == h).astype(F32) for h in range(GROUP)]
    picks = [m.astype(BF) for m in picks_f]

    def spread(x):
        return jnp.concatenate([x * m for m in picks], axis=0)

    def fold(x):
        rows = x.shape[0] // GROUP
        return sum(x[h * rows : (h + 1) * rows] * picks_f[h] for h in range(GROUP))

    def norms(columns):
        wide = columns.astype(F32)
        high, low = split(wide * wide)
        inverse = lax.rsqrt(nn(high, block_ref[...]) + nn(low, block_ref[...]) + EPS)
        return inverse, wide * inverse

    tok = tok_ref[...]
    cot = cot_ref[...]
    for b in range(3 * GROUPS):
        qkv[:, lanes_of(b)] = nt(tok, wqkv_ref[lanes_of(b), :]).astype(BF)
    for b in range(GROUPS):
        gr[:, lanes_of(b)] = nt(cot, wout_ref[lanes_of(b), :]).astype(BF)
        inverse, unit = norms(qkv[:, lanes_of(b)])
        inv_q[:, lanes_of(b)] = inverse
        qn[:, lanes_of(b)] = unit.astype(BF)
        inverse, unit = norms(qkv[:, lanes_of(GROUPS + b)])
        inv_k[:, lanes_of(b)] = inverse
        kn[:, lanes_of(b)] = unit.astype(BF)

    wide_head = iota((1, WIDTH), 1) // HEAD
    slim_head = iota((1, 128), 1)
    slim_head = jnp.where(slim_head >= HEADS, slim_head - HEADS, slim_head)
    near_row, far_row = jnp.zeros((1, WIDTH), jnp.int32), jnp.zeros((1, WIDTH), jnp.int32)
    near_slim, far_slim = jnp.zeros((1, 128), jnp.int32), jnp.zeros((1, 128), jnp.int32)
    for h in range(HEADS):
        near_row = jnp.where(wide_head == h, near_ref[h], near_row)
        far_row = jnp.where(wide_head == h, far_ref[h], far_row)
        near_slim = jnp.where(slim_head == h, near_ref[h], near_slim)
        far_slim = jnp.where(slim_head == h, far_ref[h], far_slim)
    near_mask = ((iota((TOK, WIDTH), 0) & (SPAN - 1)) == near_row).astype(F32)
    far_mask = ((iota((TOK, WIDTH), 0) & (TOK // FAR - 1)) == far_row).astype(F32)
    near_bf, far_bf = near_mask.astype(BF), far_mask.astype(BF)
    near_slim = ((iota((TOK, 128), 0) & (SPAN - 1)) == near_slim).astype(F32).astype(BF)
    far_slim = ((iota((TOK, 128), 0) & (TOK // FAR - 1)) == far_slim).astype(F32).astype(BF)
    row, token = iota((NEAR, TOK), 0), iota((NEAR, TOK), 1)
    take_near = (token // SPAN == row).astype(F32).astype(BF)
    take_far = (token // (TOK // FAR) == row).astype(F32).astype(BF)
    take_far_z = ((row // FAR == z) & (token // (TOK // FAR) == (row & 1))).astype(F32).astype(BF)

    def unnear(x, b):
        return jnp.broadcast_to(x[:, None, :], (NEAR, SPAN, LANES)).reshape(TOK, LANES) * near_mask[:, lanes_of(b)]

    def unfar(x, b):
        rows = [jnp.broadcast_to(x[i : i + 1], (TOK // FAR, LANES)) for i in range(FAR)]
        return jnp.concatenate(rows, axis=0) * far_mask[:, lanes_of(b)]

    value = qkv[:, 2 * WIDTH :]
    rows = [kn[...], value, qn[...], gr[...]]
    far_rows = []
    for i, x in enumerate(rows):
        into = near_kv if i < 2 else near_qg
        into[mine, i % 2] = nn(take_near, x * near_bf).astype(BF)
        picked = nn(take_far, x * far_bf)
        far_rows.append(picked.astype(BF))
        for r in range(FAR):
            for t in range(WIDTH // 128):
                at_row = (i * FAR + r) * (WIDTH // 128) + t
                pack[at_row : at_row + 1, :] = picked[r : r + 1, 128 * t : 128 * (t + 1)]
    far_z[z] = pack[...].astype(BF)
    for n, t in enumerate(z_peers):
        send(far_z.at[z], far_z.at[z], s_fz.at[n], r_fz.at[z], at(y, t, core))
    for n, t in enumerate(near_peers):
        send(near_kv.at[mine], near_kv.at[mine], s_nkv.at[n], r_nkv.at[mine], {"seq": base + t})
    for n, t in enumerate(near_peers):
        send(near_qg.at[mine], near_qg.at[mine], s_nqg.at[n], r_nqg.at[mine], {"seq": base + t})

    ones = spread(jnp.ones((TOK, LANES), BF))
    for b in range(GROUPS):
        s = nt(spread(qn[:, lanes_of(b)]), kn[:, lanes_of(b)])
        ps = []
        for h in range(GROUP):
            p = jnp.exp(s[h * TOK : (h + 1) * TOK] * scale_ref[GROUP * b + h])
            p_loc[(GROUP * b + h) * TOK : (GROUP * b + h + 1) * TOK, :] = p
            ps.append(p.astype(BF))
        ps = jnp.concatenate(ps, axis=1)
        num[:, lanes_of(b)] = nn(ps, spread(qkv[:, lanes_of(2 * GROUPS + b)]))
        den[:, lanes_of(b)] = nn(ps, ones)

    for t in z_peers:
        arrived(far_z.at[t], s_fz.at[0], r_fz.at[t])
    ordered = nn(order_ref[...], far_z[...].reshape(NZ * PACK, 128)).astype(BF)
    for i in range(4):
        into = far_kv if i < 2 else far_qg
        for t in range(WIDTH // 128):
            first = (i * (WIDTH // 128) + t) * 16
            into[core, y, i % 2, :, 128 * t : 128 * (t + 1)] = ordered[first : first + 16, :]
    for n, t in enumerate(y_peers):
        send(far_kv.at[core, y], far_kv.at[core, y], s_fkv.at[n], r_fkv.at[y], at(t, z, core))
    for n, t in enumerate(y_peers):
        send(far_qg.at[core, y], far_qg.at[core, y], s_fqg.at[n], r_fqg.at[y], at(t, z, core))

    def forward(queries, keys, values, p_ref):
        results = []
        for b in range(GROUPS):
            s = nt(spread(queries[:, lanes_of(b)]), keys(b))
            ps = []
            for h in range(GROUP):
                ps.append(jnp.exp(s[h * 16 : (h + 1) * 16] * scale_ref[GROUP * b + h]))
            p = jnp.concatenate(ps, axis=0)
            p_ref[b] = p
            total = jnp.broadcast_to(jnp.sum(p, axis=1, keepdims=True), (GROUP * 16, LANES))
            results.append((fold(nn(p.astype(BF), values(b))), fold(total)))
        return results

    def near_rows(ref, i):
        return lambda b: jnp.concatenate([ref[s, i, :, lanes_of(b)] for s in range(SPAN)], axis=0)

    def far_rows_of(ref, i):
        return lambda b: jnp.concatenate(
            [ref[s, t, i, :, lanes_of(b)] for s in range(2) for t in range(NY)], axis=0
        )

    for t in near_peers:
        arrived(near_kv.at[t], s_nkv.at[0], r_nkv.at[t])
    near_q, near_g = near_qg[mine, 0], near_qg[mine, 1]
    for b, (n_part, d_part) in enumerate(forward(near_q, near_rows(near_kv, 0), near_rows(near_kv, 1), p_near)):
        num[:, lanes_of(b)] += unnear(n_part, b)
        den[:, lanes_of(b)] += unnear(d_part, b)

    partner = at(y, z, other)
    for t in y_peers:
        arrived(far_kv.at[core, t], s_fkv.at[0], r_fkv.at[t])
    send(far_kv.at[core], far_kv.at[core], s_ckv, r_ckv, partner)
    for t in y_peers:
        arrived(far_qg.at[core, t], s_fqg.at[0], r_fqg.at[t])
    send(far_qg.at[core], far_qg.at[core], s_cqg, r_cqg, partner)
    arrived(far_kv.at[other], s_ckv, r_ckv)
    far_k, far_v, far_q, far_g = far_rows
    for b, (n_part, d_part) in enumerate(forward(far_q, far_rows_of(far_kv, 0), far_rows_of(far_kv, 1), p_far)):
        num[:, lanes_of(b)] += unfar(n_part, b)
        den[:, lanes_of(b)] += unfar(d_part, b)

    inverse = 1.0 / den[...]
    attn = (num[...] * inverse).astype(BF)
    attn_ref[...] = attn
    high, low = split(inverse)
    slim = nn(high, compact_ref[:, :128]) + nn(low, compact_ref[:, :128])
    high, low = split(gr[...].astype(F32) * attn.astype(F32))
    slim = slim + nn(high, compact_ref[:, 128:]) + nn(low, compact_ref[:, 128:])
    high, low = split(slim)

    def take(selection, mask):
        return nn(selection, high * mask) + nn(selection, low * mask)

    near_slim_rows = take(take_near, near_slim)
    far_slim_rows = take(take_far, far_slim)
    near_s[mine] = near_slim_rows
    far_sz[z] = take(take_far_z, far_slim)
    for n, t in enumerate(z_peers):
        send(far_sz.at[z], far_sz.at[z], s_fsz.at[n], r_fsz.at[z], at(y, t, core))
    for n, t in enumerate(near_peers):
        send(near_s.at[mine], near_s.at[mine], s_ns.at[n], r_ns.at[mine], {"seq": base + t})
    branch_ref[...] = nn(attn, wout_ref[...]).astype(BF)

    for b in range(GROUPS):
        g = spread(gr[:, lanes_of(b)])
        grad_p = nt(g, qkv[:, lanes_of(2 * GROUPS + b)])
        ps, ds = [], []
        for h in range(GROUP):
            n = GROUP * b + h
            p = p_loc[n * TOK : (n + 1) * TOK, :] * slim[:, n : n + 1]
            d = scale_ref[n] * p * (grad_p[h * TOK : (h + 1) * TOK] - slim[:, HEADS + n : HEADS + n + 1])
            ps.append(p.astype(BF))
            ds.append(d.astype(BF))
        dq[:, lanes_of(b)] = nn(jnp.concatenate(ds, axis=1), spread(kn[:, lanes_of(b)]))
        dk[:, lanes_of(b)] = tn(jnp.concatenate(ds, axis=0), spread(qn[:, lanes_of(b)]))
        dv[:, lanes_of(b)] = tn(jnp.concatenate(ps, axis=0), g)

    for t in z_peers:
        arrived(far_sz.at[t], s_fsz.at[0], r_fsz.at[t])
    far_s[core, y] = jnp.sum(far_sz[...], axis=0)
    for n, t in enumerate(y_peers):
        send(far_s.at[core, y], far_s.at[core, y], s_fs.at[n], r_fs.at[y], at(t, z, core))

    def query_side(grads, keys, values, p_ref, slim_rows, b):
        grad_p = nt(spread(grads[:, lanes_of(b)]), values(b))
        ds = []
        for h in range(GROUP):
            n = GROUP * b + h
            p = p_ref[b, h * 16 : (h + 1) * 16, :] * slim_rows[:, n : n + 1]
            ds.append(
                scale_ref[n] * p * (grad_p[h * 16 : (h + 1) * 16] - slim_rows[:, HEADS + n : HEADS + n + 1])
            )
        return fold(nn(jnp.concatenate(ds, axis=0).astype(BF), keys(b)))

    for b in range(GROUPS):
        near_part = query_side(near_g, near_rows(near_kv, 0), near_rows(near_kv, 1), p_near, near_slim_rows, b)
        far_part = query_side(far_g, far_rows_of(far_kv, 0), far_rows_of(far_kv, 1), p_far, far_slim_rows, b)
        dq[:, lanes_of(b)] += unnear(near_part, b) + unfar(far_part, b)

    for t in y_peers:
        arrived(far_s.at[core, t], s_fs.at[0], r_fs.at[t])
    send(far_s.at[core], far_s.at[core], s_cs, r_cs, partner)

    def key_side(keys, values, queries, grads, columns, b):
        q, g = queries(b), grads(b)
        s = nt(spread(keys[:, lanes_of(b)]), q)
        grad_p = nt(spread(values[:, lanes_of(b)]), g)
        ps, ds = [], []
        for h in range(GROUP):
            n = GROUP * b + h
            p = jnp.exp(s[h * 16 : (h + 1) * 16] * scale_ref[n]) * columns[n : n + 1, :]
            ps.append(p)
            ds.append(
                scale_ref[n] * p * (grad_p[h * 16 : (h + 1) * 16] - columns[HEADS + n : HEADS + n + 1, :])
            )
        p, d = jnp.concatenate(ps, axis=0).astype(BF), jnp.concatenate(ds, axis=0).astype(BF)
        return fold(nn(d, q)), fold(nn(p, g))

    for t in near_peers:
        arrived(near_s.at[t], s_ns.at[0], r_ns.at[t])
        arrived(near_qg.at[t], s_nqg.at[0], r_nqg.at[t])
    columns = near_s[...].reshape(TOK, 128).T
    near_k, near_v = near_kv[mine, 0], near_kv[mine, 1]
    for b in range(GROUPS):
        k_part, v_part = key_side(near_k, near_v, near_rows(near_qg, 0), near_rows(near_qg, 1), columns, b)
        dk[:, lanes_of(b)] += unnear(k_part, b)
        dv[:, lanes_of(b)] += unnear(v_part, b)
    arrived(far_qg.at[other], s_cqg, r_cqg)
    arrived(far_s.at[other], s_cs, r_cs)
    columns = far_s[...].reshape(TOK, 128).T
    for b in range(GROUPS):
        k_part, v_part = key_side(far_k, far_v, far_rows_of(far_qg, 0), far_rows_of(far_qg, 1), columns, b)
        dk[:, lanes_of(b)] += unfar(k_part, b)
        dv[:, lanes_of(b)] += unfar(v_part, b)

    for i, (inv_ref, grad) in enumerate(((inv_q, dq), (inv_k, dk))):
        for b in range(GROUPS):
            inverse = inv_ref[:, lanes_of(b)]
            unit = qkv[:, lanes_of(GROUPS * i + b)].astype(F32) * inverse
            d = grad[:, lanes_of(b)]
            high, low = split(unit * d)
            along = nn(high, block_ref[...]) + nn(low, block_ref[...])
            dqkv_ref[:, lanes_of(GROUPS * i + b)] = (inverse * (d - unit * along)).astype(BF)
    dqkv_ref[:, 2 * WIDTH :] = dv[...].astype(BF)
    for copy in sent:
        copy.wait_send()


def weights(
    dqkv_ref, tok_ref, attn_ref, cot_ref, wqkv_ref, deal_ref,
    grad_tok_ref, qkv_out, out_out,
    dqkv_t, attn_t, part, total, core_send, core_recv, y_send, y_recv, z_send, z_recv, x_pieces,
    s_core, r_core, s_y, r_y, s_z, r_z, s_x, r_x,
):
    seq, core, z, y = place()
    x = lax.axis_index("dp")
    other = 1 - core
    partner = at(y, z, other)
    y_right, y_left = at(lax.rem(y + 1, NY), z, core), at(lax.rem(y + 3, NY), z, core)
    z_right, z_left = at(y, lax.rem(z + 1, NZ), core), at(y, lax.rem(z + NZ - 1, NZ), core)
    pair = seq - core
    owners = []
    for d in range(1, 2 * NX):
        to = lax.rem(core * NX + x + d, 2 * NX)
        owners.append((to, {"seq": pair + to // NX, "dp": lax.rem(to, NX)}))
    greet([partner_ for partner_ in (y_right, y_left, z_right, z_left)] + [device for _, device in owners])
    sent = []

    def send(src, dst, ssem, rsem, device):
        copy = remote(src, dst, ssem, rsem, device)
        copy.start()
        sent.append(copy)

    def arrived(ref, ssem, rsem):
        remote(ref, ref, ssem, rsem, {"seq": seq}).wait_recv()

    tok, cot = tok_ref[...], cot_ref[...]
    first = core == 0
    tok_mine = jnp.where(first, tok[:, :HALF], tok[:, HALF:])
    tok_other = jnp.where(first, tok[:, HALF:], tok[:, :HALF])
    cot_mine = jnp.where(first, cot[:, :HALF], cot[:, HALF:])
    cot_other = jnp.where(first, cot[:, HALF:], cot[:, :HALF])
    dqkv_t[...] = dqkv_ref[...].T
    attn_t[...] = attn_ref[...].T

    turns = (2, 1, 3, 0)
    for n, turn in enumerate(turns):
        p = lax.rem(y + turn, NY)
        q_rows = pl.ds(pl.multiple_of(p * QROWS, 64), QROWS)
        o_rows = pl.ds(pl.multiple_of(p * OROWS, 64), OROWS)
        core_send[n, :QROWS, :] = nn(dqkv_t[q_rows, :], tok_other).astype(BF)
        core_send[n, QROWS:, :] = nn(attn_t[o_rows, :], cot_other).astype(BF)
        send(core_send.at[n], core_recv.at[n], s_core.at[n], r_core.at[n], partner)
        part[n, :QROWS, :] = nn(dqkv_t[q_rows, :], tok_mine)
        part[n, QROWS:, :] = nn(attn_t[o_rows, :], cot_mine)

    grad_tok_ref[...] = nn(dqkv_ref[...], wqkv_ref[...]).astype(BF)

    a, b = slice(0, PIECE // 2), slice(PIECE // 2, PIECE)

    def both_cores(n):
        arrived(core_recv.at[n], s_core.at[n], r_core.at[n])
        part[n] += core_recv[n].astype(F32)

    def y_out(slot, value, device, into=None):
        y_send[slot] = value.astype(BF)
        send(y_send.at[slot], y_recv.at[slot], s_y.at[slot], r_y.at[slot], device)

    def y_in(slot):
        arrived(y_recv.at[slot], s_y.at[slot], r_y.at[slot])
        return y_recv[slot].astype(F32)

    both_cores(0)
    y_out(0, part[0, a, :], y_right)
    y_out(1, part[0, b, :], y_left)
    both_cores(1)
    y_out(2, part[1, b, :], y_right)
    both_cores(2)
    y_out(4, part[2, a, :], y_left)
    y_out(3, part[1, a, :] + y_in(0), y_right)
    y_out(5, part[2, b, :] + y_in(1), y_left)
    both_cores(3)
    total[b, :] = part[3, b, :] + y_in(2)
    total[a, :] = part[3, a, :] + y_in(4)
    total[a, :] += y_in(3)
    total[b, :] += y_in(5)

    def block(t):
        q_rows = pl.ds(pl.multiple_of(t * QZ, 8), QZ)
        o_rows = pl.ds(pl.multiple_of(QROWS + t * OZ, 8), OZ)
        return jnp.concatenate([total[q_rows, :], total[o_rows, :]], axis=0)

    half = ZROWS // 2
    slices = (slice(0, half), slice(half, ZROWS))

    def z_out(side, step, value, rows):
        z_send[side, step, rows, :] = value.astype(BF)
        send(
            z_send.at[side, step, rows], z_recv.at[side, step, rows], s_z.at[side, step], r_z.at[side, step],
            (z_right, z_left)[side],
        )

    def z_in(side, step, rows):
        arrived(z_recv.at[side, step, rows], s_z.at[side, step], r_z.at[side, step])
        return z_recv[side, step, rows, :].astype(F32)

    far = block(lax.rem(z + NZ // 2, NZ))
    for side in range(2):
        z_out(side, 0, far[slices[side]], slices[side])
    whole = slice(0, ZROWS)
    for step in range(1, NZ // 2):
        for side in range(2):
            away = NZ // 2 - step
            here = block(lax.rem(z + (away if side == 0 else NZ - away), NZ))
            if step == 1:
                came = z_in(side, 0, slices[side])
                if side == 0:
                    here = jnp.concatenate([here[:half] + came, here[half:]], axis=0)
                else:
                    here = jnp.concatenate([here[:half], here[half:] + came], axis=0)
            else:
                here = here + z_in(side, step - 1, whole)
            z_out(side, step, here, whole)
    here = block(z) + z_in(0, NZ // 2 - 1, whole) + z_in(1, NZ // 2 - 1, whole)

    dealt = nn(deal_ref[...], here.astype(BF)).astype(BF)
    slot = core * NX + x
    for to in range(2 * NX):
        x_pieces[0, to] = dealt[16 * to : 16 * (to + 1), :]
    x_pieces[1, slot] = x_pieces[0, slot]
    for n, (to, device) in enumerate(owners):
        send(x_pieces.at[0, to], x_pieces.at[1, slot], s_x.at[n], r_x.at[slot], device)
    for to, _ in owners:
        arrived(x_pieces.at[1, to], s_x.at[0], r_x.at[to])
    for side in range(2):
        share = sum(x_pieces[1, side * NX + t].astype(F32) for t in range(NX))
        qkv_out[:, side * HALF : (side + 1) * HALF] = share[:9]
        out_out[:, side * HALF : (side + 1) * HALF] = share[9:12]
    for copy in sent:
        copy.wait_send()


def constants():
    lane = np.arange(WIDTH)
    block = (lane[:LANES, None] // HEAD == lane[None, :LANES] // HEAD).astype(np.float32)
    compact = np.zeros((WIDTH, 256), np.float32)
    compact[np.arange(HEADS) * HEAD, np.arange(HEADS)] = 1
    compact[lane, 128 + HEADS + lane // HEAD] = 1
    order = np.zeros((NZ * PACK, NZ * PACK), np.float32)
    tiles = WIDTH // 128
    for t in range(4):
        for j in range(tiles):
            for s in range(NZ):
                for i in range(FAR):
                    order[(t * tiles + j) * 16 + s * FAR + i, s * PACK + (t * FAR + i) * tiles + j] = 1
    deal = np.zeros((2 * NX * 16, ZROWS), np.float32)
    for core in range(2):
        for x in range(NX):
            for i in range(9):
                deal[(core * NX + x) * 16 + i, (core * NX + x) * 9 + i] = 1
            for i in range(3):
                deal[(core * NX + x) * 16 + 9 + i, QZ + (core * NX + x) * 3 + i] = 1
    return [jnp.asarray(m, BF) for m in (block, compact, order, deal)]


def body(tokens, cotangent, qkv_weight, out_weight, logit_scale, near_offsets, far_offsets):
    inputs, incoming = tokens[0], cotangent[0]
    block, compact, order, deal = constants()
    smem = pl.BlockSpec(memory_space=pltpu.SMEM)
    vmem = pl.BlockSpec(memory_space=pltpu.VMEM)
    dma = pltpu.SemaphoreType.DMA
    wide_bf = pltpu.VMEM((TOK, WIDTH), BF)
    wide = pltpu.VMEM((TOK, WIDTH), F32)
    branch, attn, dqkv = pl.pallas_call(
        attention,
        out_shape=[
            jax.ShapeDtypeStruct((TOK, WIDTH), BF),
            jax.ShapeDtypeStruct((TOK, WIDTH), BF),
            jax.ShapeDtypeStruct((TOK, 3 * WIDTH), BF),
        ],
        in_specs=[smem] * 3 + [vmem] * 7,
        out_specs=[vmem] * 3,
        scratch_shapes=[
            pltpu.VMEM((TOK, 3 * WIDTH), BF), wide_bf, wide_bf, wide_bf, wide, wide,
            pltpu.VMEM((HEADS * TOK, 128), F32),
            pltpu.VMEM((GROUPS, GROUP * 16, 128), F32),
            pltpu.VMEM((GROUPS, GROUP * 16, 128), F32),
            wide, wide, wide, wide, wide,
            pltpu.VMEM((PACK, 128), F32),
            pltpu.VMEM((SPAN, 2, NEAR, WIDTH), BF),
            pltpu.VMEM((SPAN, 2, NEAR, WIDTH), BF),
            pltpu.VMEM((SPAN, NEAR, 128), F32),
            pltpu.VMEM((NZ, PACK, 128), BF),
            pltpu.VMEM((2, NY, 2, 16, WIDTH), BF),
            pltpu.VMEM((2, NY, 2, 16, WIDTH), BF),
            pltpu.VMEM((NZ, 16, 128), F32),
            pltpu.VMEM((2, NY, 16, 128), F32),
            dma((7,)), dma((8,)), dma((7,)), dma((8,)), dma((7,)), dma((8,)),
            dma((7,)), dma((8,)), dma((7,)), dma((8,)),
            dma((3,)), dma((4,)), dma((3,)), dma((4,)), dma((3,)), dma((4,)),
            dma, dma, dma, dma, dma, dma,
        ],
        compiler_params=pltpu.CompilerParams(
            collective_id=0, has_side_effects=True, vmem_limit_bytes=48 * 1024 * 1024
        ),
    )(logit_scale, near_offsets, far_offsets, inputs, incoming, qkv_weight, out_weight, block, compact, order)
    grad_inputs, qkv_share, out_share = pl.pallas_call(
        weights,
        out_shape=[
            jax.ShapeDtypeStruct((TOK, WIDTH), BF),
            jax.ShapeDtypeStruct((9, WIDTH), F32),
            jax.ShapeDtypeStruct((3, WIDTH), F32),
        ],
        in_specs=[vmem] * 6,
        out_specs=[vmem] * 3,
        scratch_shapes=[
            pltpu.VMEM((3 * WIDTH, TOK), BF),
            pltpu.VMEM((WIDTH, TOK), BF),
            pltpu.VMEM((NY, PIECE, HALF), F32),
            pltpu.VMEM((PIECE, HALF), F32),
            pltpu.VMEM((NY, PIECE, HALF), BF),
            pltpu.VMEM((NY, PIECE, HALF), BF),
            pltpu.VMEM((6, PIECE // 2, HALF), BF),
            pltpu.VMEM((6, PIECE // 2, HALF), BF),
            pltpu.VMEM((2, NZ // 2, ZROWS, HALF), BF),
            pltpu.VMEM((2, NZ // 2, ZROWS, HALF), BF),
            pltpu.VMEM((2, 2 * NX, 16, HALF), BF),
            dma((4,)), dma((4,)), dma((6,)), dma((6,)), dma((2, 4)), dma((2, 4)), dma((7,)), dma((8,)),
        ],
        compiler_params=pltpu.CompilerParams(
            collective_id=1, has_side_effects=True, vmem_limit_bytes=48 * 1024 * 1024
        ),
    )(dqkv, inputs, attn, incoming, qkv_weight, deal)
    return (branch[None], grad_inputs[None], qkv_share, out_share)


def solution(mesh):
    return jax.shard_map(
        body,
        mesh=mesh,
        in_specs=(P("dp", "seq", None), P("dp", "seq", None), P(), P(), P(), P(), P()),
        out_specs=(
            P("dp", "seq", None),
            P("dp", "seq", None),
            P(("seq", "dp"), None),
            P(("seq", "dp"), None),
        ),
        check_vma=False,
    )
```

```python
import jax
import jax.numpy as jnp
import numpy as np
from jax import lax
from jax.experimental import pallas as pl
from jax.experimental.pallas import tpu as pltpu
from jax.sharding import PartitionSpec as P

BF = jnp.bfloat16
F32 = jnp.float32
MESH = pl.DeviceIdType.MESH
EPS = 1e-06

NY, NZ, NX = 4, 8, 4
TOK = 128
WIDTH = 768
HEADS = 12
HEAD = 64
GROUP = 4
LANES = GROUP * HEAD
GROUPS = HEADS // GROUP
SPAN = 8
NEAR = TOK // SPAN
FAR = 2
PACK = 32
TILES = WIDTH // 128
OWNERS = 2 * NX
QROWS = 3 * WIDTH // NY
OROWS = WIDTH // NY
QOWN, OOWN = QROWS // OWNERS, OROWS // OWNERS
PIECE = QOWN + OOWN
EARLY = 176
LATE = 224


def nn(a, b):
    return lax.dot_general(a, b, (((1,), (0,)), ((), ())), preferred_element_type=F32)


def nt(a, b):
    return lax.dot_general(a, b, (((1,), (1,)), ((), ())), preferred_element_type=F32)


def tn(a, b):
    return lax.dot_general(a, b, (((0,), (0,)), ((), ())), preferred_element_type=F32)


def split(x):
    high = x.astype(BF)
    return high, (x - high.astype(F32)).astype(BF)


def iota(shape, dim):
    return lax.broadcasted_iota(jnp.int32, shape, dim)


def place():
    seq = lax.axis_index("seq")
    return seq, lax.rem(seq, 2), lax.rem(seq // 2, NZ), seq // (2 * NZ)


def at(y, z, core):
    return {"seq": (y * NZ + z) * 2 + core}


def remote(src, dst, send, recv, device):
    return pltpu.make_async_remote_copy(
        src_ref=src, dst_ref=dst, send_sem=send, recv_sem=recv, device_id=device, device_id_type=MESH
    )


def lanes_of(b):
    return slice(b * LANES, (b + 1) * LANES)


def layer(
    scale_ref, near_ref, far_ref, tok_hbm, cot_hbm, wqkv_hbm, wout_hbm,
    block_hbm, compact_hbm, order_hbm, perm_q_hbm, perm_o_hbm, deal_hbm,
    branch_ref, grad_tok_ref, qkv_out, out_out,
    wqkv_ref, wout_ref, block_ref, compact_ref, order_ref, perm_q, perm_o, deal_ref,
    toks, cots, qkv, qn, kn, gr, inv_q, inv_k, p_loc, p_near, p_far, num, den, dq, dk, dv, dqkv, pack,
    near_kv, near_qg, near_s, far_zkv, far_zqg, far_kv, far_qg, far_sz, far_s,
    attn_t, dqkv_t, stage, early_out, early_in, late_out, late_in, q_sum, o_sum, y_send, y_recv, z_send, z_recv,
    loads, sends, r_tok, r_cot, r_ftok, r_fcot, r_nkv, r_nqg, r_ns, r_zkv, r_zqg, r_sz, r_fkv, r_fqg, r_ckv, r_cqg,
    r_fs, r_early, r_late, r_y, r_z,
):
    seq, core, z, y = place()
    x = lax.axis_index("dp")
    mine = lax.rem(seq, SPAN)
    base = seq - mine
    other = 1 - core
    own = core * NX + x

    copies = []
    for n, (src, dst) in enumerate((
        (tok_hbm, toks.at[own]), (wqkv_hbm.at[WIDTH : 3 * WIDTH], wqkv_ref.at[WIDTH : 3 * WIDTH]),
        (block_hbm, block_ref), (cot_hbm, cots.at[own]), (wqkv_hbm.at[:WIDTH], wqkv_ref.at[:WIDTH]),
        (wout_hbm, wout_ref), (order_hbm, order_ref), (compact_hbm, compact_ref), (perm_q_hbm, perm_q),
        (perm_o_hbm, perm_o), (deal_hbm, deal_ref),
    )):
        copy = pltpu.make_async_copy(src, dst, loads.at[n])
        copy.start()
        copies.append(copy)

    z_peers = [lax.rem(z + d, NZ) for d in range(1, NZ)]
    y_peers = [lax.rem(y + d, NY) for d in range(1, NY)]
    x_peers = [lax.rem(x + d, NX) for d in range(1, NX)]
    near_peers = [lax.rem(mine + d, SPAN) for d in range(1, SPAN)]
    near_same = [2 * lax.rem(mine // 2 + d, SPAN // 2) + core for d in range(1, SPAN // 2)]
    near_other = [2 * lax.rem(mine // 2 + d, SPAN // 2) + other for d in range(SPAN // 2)]
    partner = at(y, z, other)
    pair = seq - core

    def owner(o):
        return {"seq": pair + o // NX, "dp": lax.rem(o, NX)}

    owners = [lax.rem(own + d, OWNERS) for d in range(1, OWNERS)]
    barrier = pltpu.get_barrier_semaphore()
    greeted = (
        [at(y, t, core) for t in z_peers]
        + [{"seq": base + t} for t in near_other]
        + [at(t, z, core) for t in y_peers]
        + [at(t, z, other) for t in y_peers]
        + [{"seq": seq, "dp": t} for t in x_peers]
        + [{"seq": pair + other, "dp": t} for t in x_peers]
    )
    for device in greeted:
        pl.semaphore_signal(barrier, inc=1, device_id=device, device_id_type=MESH)
    sent = []

    def send(src, dst, recv, device):
        copy = remote(src, dst, sends.at[len(sent)], recv, device)
        copy.start()
        sent.append(copy)

    def arrived(ref, recv):
        remote(ref, ref, sends.at[0], recv, {"seq": seq}).wait_recv()

    head_lane = iota((1, LANES), 1) // HEAD
    picks_f = [(head_lane == h).astype(F32) for h in range(GROUP)]
    picks = [m.astype(BF) for m in picks_f]

    def spread(x):
        return jnp.concatenate([x * m for m in picks], axis=0)

    def fold(x):
        rows = x.shape[0] // GROUP
        return sum(x[h * rows : (h + 1) * rows] * picks_f[h] for h in range(GROUP))

    wide_head = iota((1, WIDTH), 1) // HEAD
    slim_head = iota((1, 128), 1)
    slim_head = jnp.where(slim_head >= HEADS, slim_head - HEADS, slim_head)
    near_row, far_row = jnp.zeros((1, WIDTH), jnp.int32), jnp.zeros((1, WIDTH), jnp.int32)
    near_slim, far_slim = jnp.zeros((1, 128), jnp.int32), jnp.zeros((1, 128), jnp.int32)
    for h in range(HEADS):
        near_row = jnp.where(wide_head == h, near_ref[h], near_row)
        far_row = jnp.where(wide_head == h, far_ref[h], far_row)
        near_slim = jnp.where(slim_head == h, near_ref[h], near_slim)
        far_slim = jnp.where(slim_head == h, far_ref[h], far_slim)
    near_mask = ((iota((TOK, WIDTH), 0) & (SPAN - 1)) == near_row).astype(F32)
    far_mask = ((iota((TOK, WIDTH), 0) & (TOK // FAR - 1)) == far_row).astype(F32)
    near_bf, far_bf = near_mask.astype(BF), far_mask.astype(BF)
    near_slim = ((iota((TOK, 128), 0) & (SPAN - 1)) == near_slim).astype(F32).astype(BF)
    far_slim = ((iota((TOK, 128), 0) & (TOK // FAR - 1)) == far_slim).astype(F32).astype(BF)
    row, token = iota((NEAR, TOK), 0), iota((NEAR, TOK), 1)
    take_near = (token // SPAN == row).astype(F32).astype(BF)
    take_far = (token // (TOK // FAR) == row).astype(F32).astype(BF)
    take_far_z = ((row // FAR == z) & (token // (TOK // FAR) == (row & 1))).astype(F32).astype(BF)

    def unnear(x, b):
        return jnp.broadcast_to(x[:, None, :], (NEAR, SPAN, LANES)).reshape(TOK, LANES) * near_mask[:, lanes_of(b)]

    def unfar(x, b):
        rows = [jnp.broadcast_to(x[i : i + 1], (TOK // FAR, LANES)) for i in range(FAR)]
        return jnp.concatenate(rows, axis=0) * far_mask[:, lanes_of(b)]

    def norms(columns):
        wide = columns.astype(F32)
        high, low = split(wide * wide)
        inverse = lax.rsqrt(nn(high, block_ref[...]) + nn(low, block_ref[...]) + EPS)
        return inverse, wide * inverse

    far_rows = []

    def leave(pair_of, far_into, near_into):
        pack[2 * FAR * TILES :, :] = jnp.zeros((PACK - 2 * FAR * TILES, 128), F32)
        for i, x_ in enumerate(pair_of):
            picked = nn(take_far, x_ * far_bf)
            far_rows.append(picked.astype(BF))
            for r in range(FAR):
                for t in range(TILES):
                    at_row = (i * FAR + r) * TILES + t
                    pack[at_row : at_row + 1, :] = picked[r : r + 1, 128 * t : 128 * (t + 1)]
        far_into[z] = pack[...].astype(BF)
        for i, x_ in enumerate(pair_of):
            near_into[mine, i] = nn(take_near, x_ * near_bf).astype(BF)

    for n in range(3):
        copies[n].wait()
    tok = toks[own]
    for b in range(GROUPS, 3 * GROUPS):
        qkv[:, lanes_of(b)] = nt(tok, wqkv_ref[lanes_of(b), :]).astype(BF)
    for b in range(GROUPS):
        inverse, unit = norms(qkv[:, lanes_of(GROUPS + b)])
        inv_k[:, lanes_of(b)] = inverse
        kn[:, lanes_of(b)] = unit.astype(BF)
    pl.semaphore_wait(barrier, len(greeted))
    leave((kn[...], qkv[:, 2 * WIDTH :]), far_zkv, near_kv)
    for t in z_peers:
        send(far_zkv.at[z], far_zkv.at[z], r_zkv.at[z], at(y, t, core))
    for t in near_same:
        send(near_kv.at[mine], near_kv.at[mine], r_nkv.at[mine], {"seq": base + t})
    send(near_kv.at[mine], near_kv.at[mine], r_nkv.at[mine], partner)

    for n in range(3, 6):
        copies[n].wait()
    cot = cots[own]
    for b in range(GROUPS):
        qkv[:, lanes_of(b)] = nt(tok, wqkv_ref[lanes_of(b), :]).astype(BF)
        gr[:, lanes_of(b)] = nt(cot, wout_ref[lanes_of(b), :]).astype(BF)
        inverse, unit = norms(qkv[:, lanes_of(b)])
        inv_q[:, lanes_of(b)] = inverse
        qn[:, lanes_of(b)] = unit.astype(BF)
    leave((qn[...], gr[...]), far_zqg, near_qg)
    for t in z_peers:
        send(far_zqg.at[z], far_zqg.at[z], r_zqg.at[z], at(y, t, core))
    for t in near_same:
        send(near_qg.at[mine], near_qg.at[mine], r_nqg.at[mine], {"seq": base + t})
    send(near_qg.at[mine], near_qg.at[mine], r_nqg.at[mine], partner)
    for all_, recv, forward_recv in ((toks, r_tok, r_ftok), (cots, r_cot, r_fcot)):
        for t in x_peers:
            send(all_.at[own], all_.at[own], recv.at[x], {"seq": seq, "dp": t})
        send(all_.at[own], all_.at[own], forward_recv.at[x], partner)

    ones = spread(jnp.ones((TOK, LANES), BF))
    for b in range(GROUPS):
        s = nt(spread(qn[:, lanes_of(b)]), kn[:, lanes_of(b)])
        ps = []
        for h in range(GROUP):
            p = jnp.exp(s[h * TOK : (h + 1) * TOK] * scale_ref[GROUP * b + h])
            p_loc[(GROUP * b + h) * TOK : (GROUP * b + h + 1) * TOK, :] = p
            ps.append(p.astype(BF))
        ps = jnp.concatenate(ps, axis=1)
        num[:, lanes_of(b)] = nn(ps, spread(qkv[:, lanes_of(2 * GROUPS + b)]))
        den[:, lanes_of(b)] = nn(ps, ones)

    for n in range(6, 11):
        copies[n].wait()

    def along_y(packets, recv_z, into, recv):
        for t in z_peers:
            arrived(packets.at[t], recv_z.at[t])
        ordered = nn(order_ref[...], packets[...].reshape(NZ * PACK, 128)).astype(BF)
        for i in range(2):
            for t in range(TILES):
                first = (i * TILES + t) * 16
                into[core, y, i, :, 128 * t : 128 * (t + 1)] = ordered[first : first + 16, :]
        for t in y_peers:
            send(into.at[core, y], into.at[core, y], recv.at[y], at(t, z, core))

    def across(ref, recv):
        for t in near_same:
            arrived(ref.at[t], recv.at[t])
            send(ref.at[t], ref.at[t], recv.at[t], partner)

    def forward(queries, keys, values, p_ref):
        results = []
        for b in range(GROUPS):
            s = nt(spread(queries[:, lanes_of(b)]), keys(b))
            ps = []
            for h in range(GROUP):
                ps.append(jnp.exp(s[h * 16 : (h + 1) * 16] * scale_ref[GROUP * b + h]))
            p = jnp.concatenate(ps, axis=0)
            p_ref[b] = p
            total = jnp.broadcast_to(jnp.sum(p, axis=1, keepdims=True), (GROUP * 16, LANES))
            results.append((fold(nn(p.astype(BF), values(b))), fold(total)))
        return results

    def near_rows(ref, i):
        return lambda b: jnp.concatenate([ref[s, i, :, lanes_of(b)] for s in range(SPAN)], axis=0)

    def far_rows_of(ref, i):
        return lambda b: jnp.concatenate(
            [ref[s, t, i, :, lanes_of(b)] for s in range(2) for t in range(NY)], axis=0
        )

    along_y(far_zkv, r_zkv, far_kv, r_fkv)
    across(near_kv, r_nkv)
    along_y(far_zqg, r_zqg, far_qg, r_fqg)
    for t in near_other:
        arrived(near_kv.at[t], r_nkv.at[t])
    near_q, near_g = near_qg[mine, 0], near_qg[mine, 1]
    for b, (n_part, d_part) in enumerate(forward(near_q, near_rows(near_kv, 0), near_rows(near_kv, 1), p_near)):
        num[:, lanes_of(b)] += unnear(n_part, b)
        den[:, lanes_of(b)] += unnear(d_part, b)
    for t in y_peers:
        arrived(far_kv.at[core, t], r_fkv.at[t])
    send(far_kv.at[core], far_kv.at[core], r_ckv, partner)
    across(near_qg, r_nqg)
    arrived(far_kv.at[other], r_ckv)
    far_k, far_v, far_q, far_g = far_rows
    for b, (n_part, d_part) in enumerate(forward(far_q, far_rows_of(far_kv, 0), far_rows_of(far_kv, 1), p_far)):
        num[:, lanes_of(b)] += unfar(n_part, b)
        den[:, lanes_of(b)] += unfar(d_part, b)

    inverse = 1.0 / den[...]
    attn = (num[...] * inverse).astype(BF)
    high, low = split(inverse)
    slim = nn(high, compact_ref[:, :128]) + nn(low, compact_ref[:, :128])
    high, low = split(gr[...].astype(F32) * attn.astype(F32))
    slim = slim + nn(high, compact_ref[:, 128:]) + nn(low, compact_ref[:, 128:])
    high, low = split(slim)

    def take(selection, mask):
        return nn(selection, high * mask) + nn(selection, low * mask)

    far_sz[z] = take(take_far_z, far_slim)
    for t in z_peers:
        send(far_sz.at[z], far_sz.at[z], r_sz.at[z], at(y, t, core))
    near_slim_rows = take(take_near, near_slim)
    far_slim_rows = take(take_far, far_slim)
    near_s[mine] = near_slim_rows
    for t in near_peers:
        send(near_s.at[mine], near_s.at[mine], r_ns.at[mine], {"seq": base + t})
    for t in y_peers:
        arrived(far_qg.at[core, t], r_fqg.at[t])
    send(far_qg.at[core], far_qg.at[core], r_cqg, partner)

    for b in range(GROUPS):
        g = spread(gr[:, lanes_of(b)])
        grad_p = nt(g, qkv[:, lanes_of(2 * GROUPS + b)])
        ps, ds = [], []
        for h in range(GROUP):
            n = GROUP * b + h
            p = p_loc[n * TOK : (n + 1) * TOK, :] * slim[:, n : n + 1]
            d = scale_ref[n] * p * (grad_p[h * TOK : (h + 1) * TOK] - slim[:, HEADS + n : HEADS + n + 1])
            ps.append(p.astype(BF))
            ds.append(d.astype(BF))
        dq[:, lanes_of(b)] = nn(jnp.concatenate(ds, axis=1), spread(kn[:, lanes_of(b)]))
        dk[:, lanes_of(b)] = tn(jnp.concatenate(ds, axis=0), spread(qn[:, lanes_of(b)]))
        dv[:, lanes_of(b)] = tn(jnp.concatenate(ps, axis=0), g)

    def query_side(grads, keys, values, p_ref, slim_rows, b):
        grad_p = nt(spread(grads[:, lanes_of(b)]), values(b))
        ds = []
        for h in range(GROUP):
            n = GROUP * b + h
            p = p_ref[b, h * 16 : (h + 1) * 16, :] * slim_rows[:, n : n + 1]
            ds.append(
                scale_ref[n] * p * (grad_p[h * 16 : (h + 1) * 16] - slim_rows[:, HEADS + n : HEADS + n + 1])
            )
        return fold(nn(jnp.concatenate(ds, axis=0).astype(BF), keys(b)))

    for b in range(GROUPS):
        near_part = query_side(near_g, near_rows(near_kv, 0), near_rows(near_kv, 1), p_near, near_slim_rows, b)
        far_part = query_side(far_g, far_rows_of(far_kv, 0), far_rows_of(far_kv, 1), p_far, far_slim_rows, b)
        dq[:, lanes_of(b)] += unnear(near_part, b) + unfar(far_part, b)

    def unnormalize(inv_ref, grad, i):
        for b in range(GROUPS):
            inverse = inv_ref[:, lanes_of(b)]
            unit = qkv[:, lanes_of(GROUPS * i + b)].astype(F32) * inverse
            d = grad[:, lanes_of(b)]
            high, low = split(unit * d)
            along = nn(high, block_ref[...]) + nn(low, block_ref[...])
            dqkv[:, lanes_of(GROUPS * i + b)] = (inverse * (d - unit * along)).astype(BF)

    for t in z_peers:
        arrived(far_sz.at[t], r_sz.at[t])
    far_s[core, y] = jnp.sum(far_sz[...], axis=0)
    for t in y_peers:
        send(far_s.at[core, y], far_s.at[core, y], r_fs.at[core, y], at(t, z, core))
        send(far_s.at[core, y], far_s.at[core, y], r_fs.at[core, y], at(t, z, other))
    send(far_s.at[core, y], far_s.at[core, y], r_fs.at[core, y], partner)

    unnormalize(inv_q, dq, 0)
    attn_t[...] = attn.T
    dqkv_t[:WIDTH, :] = dqkv[:, :WIDTH].T
    for t in range(NY):
        dealt = nn(perm_o[...], attn_t[t * OROWS : (t + 1) * OROWS, :])
        for o in range(OWNERS):
            stage[o, t * OOWN : (t + 1) * OOWN, :] = dealt[o * OOWN : (o + 1) * OOWN]

    def deal_rows(t, first):
        dealt = nn(perm_q[...], dqkv_t[t * QROWS : (t + 1) * QROWS, :])
        for o in range(OWNERS):
            stage[o, first : first + QOWN, :] = dealt[o * QOWN : (o + 1) * QOWN]

    deal_rows(0, NY * OOWN)
    for o in range(OWNERS):
        stage[o, EARLY - 8 : EARLY, :] = jnp.zeros((8, 128), F32)
    early_out[...] = stage[:, :EARLY, :].astype(BF)
    for o in owners:
        send(early_out.at[o], early_in.at[own], r_early.at[own], owner(o))
    early_in[own] = early_out[own]
    branch_ref[...] = nn(attn, wout_ref[...]).astype(BF)

    for all_, recv, forward_recv in ((toks, r_tok, r_ftok), (cots, r_cot, r_fcot)):
        for t in x_peers:
            arrived(all_.at[core * NX + t], recv.at[t])
            send(all_.at[core * NX + t], all_.at[core * NX + t], forward_recv.at[t], partner)

    def key_side(keys, values, queries, grads, columns, b):
        q, g = queries(b), grads(b)
        s = nt(spread(keys[:, lanes_of(b)]), q)
        grad_p = nt(spread(values[:, lanes_of(b)]), g)
        ps, ds = [], []
        for h in range(GROUP):
            n = GROUP * b + h
            p = jnp.exp(s[h * 16 : (h + 1) * 16] * scale_ref[n]) * columns[n : n + 1, :]
            ps.append(p)
            ds.append(
                scale_ref[n] * p * (grad_p[h * 16 : (h + 1) * 16] - columns[HEADS + n : HEADS + n + 1, :])
            )
        p, d = jnp.concatenate(ps, axis=0).astype(BF), jnp.concatenate(ds, axis=0).astype(BF)
        return fold(nn(d, q)), fold(nn(p, g))

    for t in near_peers:
        arrived(near_s.at[t], r_ns.at[t])
    for t in near_other:
        arrived(near_qg.at[t], r_nqg.at[t])
    columns = near_s[...].reshape(TOK, 128).T
    near_k, near_v = near_kv[mine, 0], near_kv[mine, 1]
    for b in range(GROUPS):
        k_part, v_part = key_side(near_k, near_v, near_rows(near_qg, 0), near_rows(near_qg, 1), columns, b)
        dk[:, lanes_of(b)] += unnear(k_part, b)
        dv[:, lanes_of(b)] += unnear(v_part, b)

    for o in owners:
        arrived(early_in.at[o], r_early.at[o])
    for t in range(NX):
        arrived(toks.at[other * NX + t], r_ftok.at[t])
        arrived(cots.at[other * NX + t], r_fcot.at[t])

    def factors(ref, rows):
        return jnp.concatenate([ref[o, rows, :] for o in range(OWNERS)], axis=1)

    o_sum[...] = nn(factors(early_in, slice(0, NY * OOWN)), cots[...].reshape(OWNERS * TOK, WIDTH))
    tokens = toks[...].reshape(OWNERS * TOK, WIDTH)
    q_sum[: EARLY - NY * OOWN, :] = nn(factors(early_in, slice(NY * OOWN, EARLY)), tokens)

    arrived(far_qg.at[other], r_cqg)
    for t in y_peers:
        arrived(far_s.at[core, t], r_fs.at[core, t])
    for t in range(NY):
        arrived(far_s.at[other, t], r_fs.at[other, t])
    columns = far_s[...].reshape(TOK, 128).T
    for b in range(GROUPS):
        k_part, v_part = key_side(far_k, far_v, far_rows_of(far_qg, 0), far_rows_of(far_qg, 1), columns, b)
        dk[:, lanes_of(b)] += unfar(k_part, b)
        dv[:, lanes_of(b)] += unfar(v_part, b)

    unnormalize(inv_k, dk, 1)
    dqkv[:, 2 * WIDTH :] = dv[...].astype(BF)
    dqkv_t[WIDTH:, :] = dqkv[:, WIDTH:].T
    for t in range(1, NY):
        deal_rows(t, (t - 1) * QOWN)
    for o in range(OWNERS):
        stage[o, LATE - 8 : LATE, :] = jnp.zeros((8, 128), F32)
    late_out[...] = stage[...].astype(BF)
    for o in owners:
        send(late_out.at[o], late_in.at[own], r_late.at[own], owner(o))
    late_in[own] = late_out[own]
    grad_tok_ref[...] = nn(dqkv[...], wqkv_ref[...]).astype(BF)
    for o in owners:
        arrived(late_in.at[o], r_late.at[o])
    late = nn(factors(late_in, slice(0, LATE)), tokens)
    q_sum[QOWN:, :] = late[: (NY - 1) * QOWN]

    y_right, y_left = at(lax.rem(y + 1, NY), z, core), at(lax.rem(y + NY - 1, NY), z, core)
    a, b_ = slice(0, PIECE // 2), slice(PIECE // 2, PIECE)

    def piece(t):
        q_rows = pl.ds(pl.multiple_of(t * QOWN, 8), QOWN)
        o_rows = pl.ds(pl.multiple_of(t * OOWN, 8), OOWN)
        return jnp.concatenate([q_sum[q_rows, :], o_sum[o_rows, :]], axis=0)

    def y_out(slot, part, device):
        y_send[slot] = part.astype(BF)
        send(y_send.at[slot], y_recv.at[slot], r_y.at[slot], device)

    def y_in(slot):
        arrived(y_recv.at[slot], r_y.at[slot])
        return y_recv[slot].astype(F32)

    part = piece(lax.rem(y + 2, NY))
    y_out(0, part[a], y_right)
    y_out(1, part[b_], y_left)
    right_part, left_part = piece(lax.rem(y + 1, NY)), piece(lax.rem(y + NY - 1, NY))
    y_out(2, right_part[b_], y_right)
    y_out(4, left_part[a], y_left)
    y_out(3, right_part[a] + y_in(0), y_right)
    y_out(5, left_part[b_] + y_in(1), y_left)
    part = piece(y)
    part = jnp.concatenate([part[a] + y_in(4) + y_in(3), part[b_] + y_in(2) + y_in(5)], axis=0)

    dealt = nn(deal_ref[...], part.astype(BF)).astype(BF)
    for t in range(NZ):
        z_send[t] = dealt[16 * t : 16 * (t + 1), :]
    for t in z_peers:
        send(z_send.at[t], z_recv.at[z], r_z.at[z], at(y, t, core))
    z_recv[z] = z_send[z]
    for t in z_peers:
        arrived(z_recv.at[t], r_z.at[t])
    share = jnp.sum(z_recv[...].astype(F32), axis=0)
    qkv_out[...] = share[: QOWN // NZ]
    out_out[...] = share[QOWN // NZ : PIECE // NZ]
    for copy in sent:
        copy.wait_send()


def constants():
    lane = np.arange(WIDTH)
    block = (lane[:LANES, None] // HEAD == lane[None, :LANES] // HEAD).astype(np.float32)
    compact = np.zeros((WIDTH, 256), np.float32)
    compact[np.arange(HEADS) * HEAD, np.arange(HEADS)] = 1
    compact[lane, 128 + HEADS + lane // HEAD] = 1
    order = np.zeros((2 * TILES * 16, NZ * PACK), np.float32)
    for t in range(2):
        for j in range(TILES):
            for s in range(NZ):
                for i in range(FAR):
                    order[(t * TILES + j) * 16 + s * FAR + i, s * PACK + (t * FAR + i) * TILES + j] = 1

    def deal_out(each):
        index = np.arange(NZ * OWNERS * each).reshape(NZ, OWNERS, each).transpose(1, 0, 2).reshape(-1)
        return np.eye(index.size, dtype=np.float32)[index]

    deal = np.zeros((NZ * 16, PIECE), np.float32)
    for t in range(NZ):
        for i in range(9):
            deal[t * 16 + i, t * 9 + i] = 1
        for i in range(3):
            deal[t * 16 + 9 + i, QOWN + t * 3 + i] = 1
    return [jnp.asarray(m, BF) for m in (block, compact, order, deal_out(9), deal_out(3), deal)]


def body(tokens, cotangent, qkv_weight, out_weight, logit_scale, near_offsets, far_offsets):
    fixed = constants()
    smem = pl.BlockSpec(memory_space=pltpu.SMEM)
    hbm = pl.BlockSpec(memory_space=pltpu.HBM)
    vmem = pl.BlockSpec(memory_space=pltpu.VMEM)
    dma = pltpu.SemaphoreType.DMA
    wide_bf = pltpu.VMEM((TOK, WIDTH), BF)
    wide = pltpu.VMEM((TOK, WIDTH), F32)

    def held(*shape):
        return pltpu.VMEM(shape, BF)

    def held_f32(*shape):
        return pltpu.VMEM(shape, F32)

    branch, grad_inputs, qkv_share, out_share = pl.pallas_call(
        layer,
        out_shape=[
            jax.ShapeDtypeStruct((TOK, WIDTH), BF),
            jax.ShapeDtypeStruct((TOK, WIDTH), BF),
            jax.ShapeDtypeStruct((9, WIDTH), F32),
            jax.ShapeDtypeStruct((3, WIDTH), F32),
        ],
        in_specs=[smem] * 3 + [hbm] * 10,
        out_specs=[vmem] * 4,
        scratch_shapes=[
            held(3 * WIDTH, WIDTH), held(WIDTH, WIDTH), *[held(*m.shape) for m in fixed],
            held(OWNERS, TOK, WIDTH), held(OWNERS, TOK, WIDTH),
            held(TOK, 3 * WIDTH), wide_bf, wide_bf, wide_bf, wide, wide,
            held_f32(HEADS * TOK, 128), held_f32(GROUPS, GROUP * 16, 128), held_f32(GROUPS, GROUP * 16, 128),
            wide, wide, wide, wide, wide, held(TOK, 3 * WIDTH), held_f32(PACK, 128),
            held(SPAN, 2, NEAR, WIDTH), held(SPAN, 2, NEAR, WIDTH), held_f32(SPAN, NEAR, 128),
            held(NZ, PACK, 128), held(NZ, PACK, 128),
            held(2, NY, 2, 16, WIDTH), held(2, NY, 2, 16, WIDTH), held_f32(NZ, 16, 128), held_f32(2, NY, 16, 128),
            held(WIDTH, TOK), held(3 * WIDTH, TOK), held_f32(OWNERS, LATE, 128),
            held(OWNERS, EARLY, 128), held(OWNERS, EARLY, 128), held(OWNERS, LATE, 128), held(OWNERS, LATE, 128),
            held_f32(NY * QOWN, WIDTH), held_f32(NY * OOWN, WIDTH),
            held(6, PIECE // 2, WIDTH), held(6, PIECE // 2, WIDTH),
            held(NZ, 16, WIDTH), held(NZ, 16, WIDTH),
            dma((11,)), dma((112,)),
            dma((4,)), dma((4,)), dma((4,)), dma((4,)),
            dma((8,)), dma((8,)), dma((8,)), dma((8,)), dma((8,)), dma((8,)), dma((4,)), dma((4,)), dma, dma,
            dma((2, 4)), dma((8,)), dma((8,)), dma((6,)), dma((8,)),
        ],
        compiler_params=pltpu.CompilerParams(
            collective_id=0, has_side_effects=True, vmem_limit_bytes=56 * 1024 * 1024
        ),
    )(logit_scale, near_offsets, far_offsets, tokens[0], cotangent[0], qkv_weight, out_weight, *fixed)
    return (branch[None], grad_inputs[None], qkv_share, out_share)


def solution(mesh):
    return jax.shard_map(
        body,
        mesh=mesh,
        in_specs=(P("dp", "seq", None), P("dp", "seq", None), P(), P(), P(), P(), P()),
        out_specs=(
            P("dp", "seq", None),
            P("dp", "seq", None),
            P(("seq", "dp"), None),
            P(("seq", "dp"), None),
        ),
        check_vma=False,
    )
```

```python
import jax
import jax.numpy as jnp
import numpy as np
from jax import lax
from jax.experimental import pallas as pl
from jax.experimental.pallas import tpu as pltpu
from jax.sharding import PartitionSpec as P

BF = jnp.bfloat16
F32 = jnp.float32
MESH = pl.DeviceIdType.MESH
EPS = 1e-06

NY, NZ, NX = 4, 8, 4
TOK = 128
WIDTH = 768
HEADS = 12
HEAD = 64
GROUP = 4
LANES = GROUP * HEAD
GROUPS = HEADS // GROUP
SPAN = 8
NEAR = TOK // SPAN
FAR = 2
PACK = 32
TILES = WIDTH // 128
OWNERS = 2 * NX
QROWS = 3 * WIDTH // NY
OROWS = WIDTH // NY
QOWN, OOWN = QROWS // OWNERS, OROWS // OWNERS
PIECE = QOWN + OOWN
EARLY = 176
LATE = 224


def nn(a, b):
    return lax.dot_general(a, b, (((1,), (0,)), ((), ())), preferred_element_type=F32)


def nt(a, b):
    return lax.dot_general(a, b, (((1,), (1,)), ((), ())), preferred_element_type=F32)


def tn(a, b):
    return lax.dot_general(a, b, (((0,), (0,)), ((), ())), preferred_element_type=F32)


def split(x):
    high = x.astype(BF)
    return high, (x - high.astype(F32)).astype(BF)


def iota(shape, dim):
    return lax.broadcasted_iota(jnp.int32, shape, dim)


def place():
    seq = lax.axis_index("seq")
    return seq, lax.rem(seq, 2), lax.rem(seq // 2, NZ), seq // (2 * NZ)


def at(y, z, core):
    return {"seq": (y * NZ + z) * 2 + core}


def remote(src, dst, send, recv, device):
    return pltpu.make_async_remote_copy(
        src_ref=src, dst_ref=dst, send_sem=send, recv_sem=recv, device_id=device, device_id_type=MESH
    )


def lanes_of(b):
    return slice(b * LANES, (b + 1) * LANES)


def layer(
    scale_ref, near_ref, far_ref, tok_hbm, cot_hbm, wqkv_hbm, wout_hbm,
    block_hbm, compact_hbm, order_hbm, perm_q_hbm, perm_o_hbm, deal_hbm,
    branch_ref, grad_tok_ref, qkv_out, out_out,
    wqkv_ref, wout_ref, block_ref, compact_ref, order_ref, perm_q, perm_o, deal_ref,
    toks, cots, qkv, qn, kn, gr, inv_q, inv_k, p_loc, p_near, p_far, num, den, dq, dk, dv, dqkv, pack,
    near_kv, near_qg, near_s, far_zkv, far_zqg, far_kv, far_qg, far_sz, far_s,
    attn_t, dqkv_t, stage, early_out, early_in, late_out, late_in, q_sum, o_sum, y_send, y_recv, z_send, z_recv,
    loads, sends, r_tok, r_cot, r_ftok, r_fcot, r_nkv, r_nqg, r_ns, r_zkv, r_zqg, r_sz, r_fkv, r_fqg, r_ckv, r_cqg,
    r_fs, r_early, r_late, r_y, r_z,
):
    seq, core, z, y = place()
    x = lax.axis_index("dp")
    mine = lax.rem(seq, SPAN)
    base = seq - mine
    other = 1 - core
    own = core * NX + x

    loading = []

    def load(src, dst):
        copy = pltpu.make_async_copy(src, dst, loads.at[len(loading)])
        copy.start()
        loading.append(copy)

    def load_rows(src, dst, start, stop):
        for first in range(start, stop, LANES):
            load(src.at[first : first + LANES], dst.at[first : first + LANES])

    load(tok_hbm, toks.at[own])
    load(block_hbm, block_ref)
    load_rows(wqkv_hbm, wqkv_ref, WIDTH, 3 * WIDTH)
    load(cot_hbm, cots.at[own])
    load_rows(wqkv_hbm, wqkv_ref, 0, WIDTH)
    load_rows(wout_hbm, wout_ref, 0, WIDTH)

    z_peers = [lax.rem(z + d, NZ) for d in range(1, NZ)]
    y_peers = [lax.rem(y + d, NY) for d in range(1, NY)]
    x_peers = [lax.rem(x + d, NX) for d in range(1, NX)]
    near_peers = [lax.rem(mine + d, SPAN) for d in range(1, SPAN)]
    near_same = [2 * lax.rem(mine // 2 + d, SPAN // 2) + core for d in range(1, SPAN // 2)]
    near_other = [2 * lax.rem(mine // 2 + d, SPAN // 2) + other for d in range(SPAN // 2)]
    partner = at(y, z, other)
    pair = seq - core

    def owner(o):
        return {"seq": pair + o // NX, "dp": lax.rem(o, NX)}

    owners = [lax.rem(own + d, OWNERS) for d in range(1, OWNERS)]
    barrier = pltpu.get_barrier_semaphore()
    greeted = (
        [at(y, t, core) for t in z_peers]
        + [{"seq": base + t} for t in near_other]
        + [at(t, z, core) for t in y_peers]
        + [at(t, z, other) for t in y_peers]
        + [{"seq": seq, "dp": t} for t in x_peers]
        + [{"seq": pair + other, "dp": t} for t in x_peers]
    )
    for device in greeted:
        pl.semaphore_signal(barrier, inc=1, device_id=device, device_id_type=MESH)
    sent = []

    def send(src, dst, recv, device):
        copy = remote(src, dst, sends.at[len(sent)], recv, device)
        copy.start()
        sent.append(copy)

    def arrived(ref, recv):
        remote(ref, ref, sends.at[0], recv, {"seq": seq}).wait_recv()

    head_lane = iota((1, LANES), 1) // HEAD
    picks_f = [(head_lane == h).astype(F32) for h in range(GROUP)]
    picks = [m.astype(BF) for m in picks_f]

    def spread(x):
        return jnp.concatenate([x * m for m in picks], axis=0)

    def fold(x):
        rows = x.shape[0] // GROUP
        return sum(x[h * rows : (h + 1) * rows] * picks_f[h] for h in range(GROUP))

    wide_head = iota((1, WIDTH), 1) // HEAD
    slim_head = iota((1, 128), 1)
    slim_head = jnp.where(slim_head >= HEADS, slim_head - HEADS, slim_head)
    near_row, far_row = jnp.zeros((1, WIDTH), jnp.int32), jnp.zeros((1, WIDTH), jnp.int32)
    near_slim, far_slim = jnp.zeros((1, 128), jnp.int32), jnp.zeros((1, 128), jnp.int32)
    for h in range(HEADS):
        near_row = jnp.where(wide_head == h, near_ref[h], near_row)
        far_row = jnp.where(wide_head == h, far_ref[h], far_row)
        near_slim = jnp.where(slim_head == h, near_ref[h], near_slim)
        far_slim = jnp.where(slim_head == h, far_ref[h], far_slim)
    near_mask = ((iota((TOK, WIDTH), 0) & (SPAN - 1)) == near_row).astype(F32)
    far_mask = ((iota((TOK, WIDTH), 0) & (TOK // FAR - 1)) == far_row).astype(F32)
    near_bf, far_bf = near_mask.astype(BF), far_mask.astype(BF)
    near_slim = ((iota((TOK, 128), 0) & (SPAN - 1)) == near_slim).astype(F32).astype(BF)
    far_slim = ((iota((TOK, 128), 0) & (TOK // FAR - 1)) == far_slim).astype(F32).astype(BF)
    row, token = iota((NEAR, TOK), 0), iota((NEAR, TOK), 1)
    take_near = (token // SPAN == row).astype(F32).astype(BF)
    take_far = (token // (TOK // FAR) == row).astype(F32).astype(BF)
    take_far_z = ((row // FAR == z) & (token // (TOK // FAR) == (row & 1))).astype(F32).astype(BF)

    def unnear(x, b):
        return jnp.broadcast_to(x[:, None, :], (NEAR, SPAN, LANES)).reshape(TOK, LANES) * near_mask[:, lanes_of(b)]

    def unfar(x, b):
        rows = [jnp.broadcast_to(x[i : i + 1], (TOK // FAR, LANES)) for i in range(FAR)]
        return jnp.concatenate(rows, axis=0) * far_mask[:, lanes_of(b)]

    def norms(columns):
        wide = columns.astype(F32)
        high, low = split(wide * wide)
        inverse = lax.rsqrt(nn(high, block_ref[...]) + nn(low, block_ref[...]) + EPS)
        return inverse, wide * inverse

    far_rows = []

    def leave(pair_of, far_into, near_into):
        pack[2 * FAR * TILES :, :] = jnp.zeros((PACK - 2 * FAR * TILES, 128), F32)
        for i, x_ in enumerate(pair_of):
            picked = nn(take_far, x_ * far_bf)
            far_rows.append(picked.astype(BF))
            for r in range(FAR):
                for t in range(TILES):
                    at_row = (i * FAR + r) * TILES + t
                    pack[at_row : at_row + 1, :] = picked[r : r + 1, 128 * t : 128 * (t + 1)]
        far_into[z] = pack[...].astype(BF)
        for i, x_ in enumerate(pair_of):
            near_into[mine, i] = nn(take_near, x_ * near_bf).astype(BF)

    for copy in loading[:2]:
        copy.wait()
    tok = toks[own]
    for b in range(GROUPS, 3 * GROUPS):
        loading[2 + b - GROUPS].wait()
        qkv[:, lanes_of(b)] = nt(tok, wqkv_ref[lanes_of(b), :]).astype(BF)
    for b in range(GROUPS):
        inverse, unit = norms(qkv[:, lanes_of(GROUPS + b)])
        inv_k[:, lanes_of(b)] = inverse
        kn[:, lanes_of(b)] = unit.astype(BF)
    pl.semaphore_wait(barrier, len(greeted))
    leave((kn[...], qkv[:, 2 * WIDTH :]), far_zkv, near_kv)
    for t in z_peers:
        send(far_zkv.at[z], far_zkv.at[z], r_zkv.at[z], at(y, t, core))
    for t in near_same:
        send(near_kv.at[mine], near_kv.at[mine], r_nkv.at[mine], {"seq": base + t})
    send(near_kv.at[mine], near_kv.at[mine], r_nkv.at[mine], partner)

    first = len(loading)
    load(order_hbm, order_ref)
    load(compact_hbm, compact_ref)
    load(perm_q_hbm, perm_q)
    load(perm_o_hbm, perm_o)
    load(deal_hbm, deal_ref)
    for copy in loading[2 + 2 * GROUPS : first]:
        copy.wait()
    cot = cots[own]
    for b in range(GROUPS):
        qkv[:, lanes_of(b)] = nt(tok, wqkv_ref[lanes_of(b), :]).astype(BF)
        gr[:, lanes_of(b)] = nt(cot, wout_ref[lanes_of(b), :]).astype(BF)
        inverse, unit = norms(qkv[:, lanes_of(b)])
        inv_q[:, lanes_of(b)] = inverse
        qn[:, lanes_of(b)] = unit.astype(BF)
    leave((qn[...], gr[...]), far_zqg, near_qg)
    for all_, recv, forward_recv in ((toks, r_tok, r_ftok), (cots, r_cot, r_fcot)):
        for t in x_peers:
            send(all_.at[own], all_.at[own], recv.at[x], {"seq": seq, "dp": t})
        send(all_.at[own], all_.at[own], forward_recv.at[x], partner)

    ones = spread(jnp.ones((TOK, LANES), BF))
    for b in range(GROUPS):
        s = nt(spread(qn[:, lanes_of(b)]), kn[:, lanes_of(b)])
        ps = []
        for h in range(GROUP):
            p = jnp.exp(s[h * TOK : (h + 1) * TOK] * scale_ref[GROUP * b + h])
            p_loc[(GROUP * b + h) * TOK : (GROUP * b + h + 1) * TOK, :] = p
            ps.append(p.astype(BF))
        ps = jnp.concatenate(ps, axis=1)
        num[:, lanes_of(b)] = nn(ps, spread(qkv[:, lanes_of(2 * GROUPS + b)]))
        den[:, lanes_of(b)] = nn(ps, ones)

    for copy in loading[first:]:
        copy.wait()

    def along_y(packets, recv_z, into, recv):
        for t in z_peers:
            arrived(packets.at[t], recv_z.at[t])
        ordered = nn(order_ref[...], packets[...].reshape(NZ * PACK, 128)).astype(BF)
        for i in range(2):
            for t in range(TILES):
                first = (i * TILES + t) * 16
                into[core, y, i, :, 128 * t : 128 * (t + 1)] = ordered[first : first + 16, :]
        for t in y_peers:
            send(into.at[core, y], into.at[core, y], recv.at[y], at(t, z, core))

    def across(ref, recv):
        for t in near_same:
            arrived(ref.at[t], recv.at[t])
            send(ref.at[t], ref.at[t], recv.at[t], partner)

    def forward(queries, keys, values, p_ref):
        results = []
        for b in range(GROUPS):
            s = nt(spread(queries[:, lanes_of(b)]), keys(b))
            ps = []
            for h in range(GROUP):
                ps.append(jnp.exp(s[h * 16 : (h + 1) * 16] * scale_ref[GROUP * b + h]))
            p = jnp.concatenate(ps, axis=0)
            p_ref[b] = p
            total = jnp.broadcast_to(jnp.sum(p, axis=1, keepdims=True), (GROUP * 16, LANES))
            results.append((fold(nn(p.astype(BF), values(b))), fold(total)))
        return results

    def near_rows(ref, i):
        return lambda b: jnp.concatenate([ref[s, i, :, lanes_of(b)] for s in range(SPAN)], axis=0)

    def far_rows_of(ref, i):
        return lambda b: jnp.concatenate(
            [ref[s, t, i, :, lanes_of(b)] for s in range(2) for t in range(NY)], axis=0
        )

    along_y(far_zkv, r_zkv, far_kv, r_fkv)
    across(near_kv, r_nkv)
    for t in z_peers:
        send(far_zqg.at[z], far_zqg.at[z], r_zqg.at[z], at(y, t, core))
    for t in near_same:
        send(near_qg.at[mine], near_qg.at[mine], r_nqg.at[mine], {"seq": base + t})
    send(near_qg.at[mine], near_qg.at[mine], r_nqg.at[mine], partner)
    for t in near_other:
        arrived(near_kv.at[t], r_nkv.at[t])
    near_q, near_g = near_qg[mine, 0], near_qg[mine, 1]
    for b, (n_part, d_part) in enumerate(forward(near_q, near_rows(near_kv, 0), near_rows(near_kv, 1), p_near)):
        num[:, lanes_of(b)] += unnear(n_part, b)
        den[:, lanes_of(b)] += unnear(d_part, b)
    for t in y_peers:
        arrived(far_kv.at[core, t], r_fkv.at[t])
    send(far_kv.at[core], far_kv.at[core], r_ckv, partner)
    along_y(far_zqg, r_zqg, far_qg, r_fqg)
    arrived(far_kv.at[other], r_ckv)
    far_k, far_v, far_q, far_g = far_rows
    for b, (n_part, d_part) in enumerate(forward(far_q, far_rows_of(far_kv, 0), far_rows_of(far_kv, 1), p_far)):
        num[:, lanes_of(b)] += unfar(n_part, b)
        den[:, lanes_of(b)] += unfar(d_part, b)

    inverse = 1.0 / den[...]
    attn = (num[...] * inverse).astype(BF)
    high, low = split(inverse)
    slim = nn(high, compact_ref[:, :128]) + nn(low, compact_ref[:, :128])
    high, low = split(gr[...].astype(F32) * attn.astype(F32))
    slim = slim + nn(high, compact_ref[:, 128:]) + nn(low, compact_ref[:, 128:])
    high, low = split(slim)

    def take(selection, mask):
        return nn(selection, high * mask) + nn(selection, low * mask)

    far_sz[z] = take(take_far_z, far_slim)
    for t in z_peers:
        send(far_sz.at[z], far_sz.at[z], r_sz.at[z], at(y, t, core))
    near_slim_rows = take(take_near, near_slim)
    far_slim_rows = take(take_far, far_slim)
    near_s[mine] = near_slim_rows
    for t in near_peers:
        send(near_s.at[mine], near_s.at[mine], r_ns.at[mine], {"seq": base + t})
    across(near_qg, r_nqg)

    for b in range(GROUPS):
        g = spread(gr[:, lanes_of(b)])
        grad_p = nt(g, qkv[:, lanes_of(2 * GROUPS + b)])
        ps, ds = [], []
        for h in range(GROUP):
            n = GROUP * b + h
            p = p_loc[n * TOK : (n + 1) * TOK, :] * slim[:, n : n + 1]
            d = scale_ref[n] * p * (grad_p[h * TOK : (h + 1) * TOK] - slim[:, HEADS + n : HEADS + n + 1])
            ps.append(p.astype(BF))
            ds.append(d.astype(BF))
        dq[:, lanes_of(b)] = nn(jnp.concatenate(ds, axis=1), spread(kn[:, lanes_of(b)]))
        dk[:, lanes_of(b)] = tn(jnp.concatenate(ds, axis=0), spread(qn[:, lanes_of(b)]))
        dv[:, lanes_of(b)] = tn(jnp.concatenate(ps, axis=0), g)

    def query_side(grads, keys, values, p_ref, slim_rows, b):
        grad_p = nt(spread(grads[:, lanes_of(b)]), values(b))
        ds = []
        for h in range(GROUP):
            n = GROUP * b + h
            p = p_ref[b, h * 16 : (h + 1) * 16, :] * slim_rows[:, n : n + 1]
            ds.append(
                scale_ref[n] * p * (grad_p[h * 16 : (h + 1) * 16] - slim_rows[:, HEADS + n : HEADS + n + 1])
            )
        return fold(nn(jnp.concatenate(ds, axis=0).astype(BF), keys(b)))

    for b in range(GROUPS):
        near_part = query_side(near_g, near_rows(near_kv, 0), near_rows(near_kv, 1), p_near, near_slim_rows, b)
        far_part = query_side(far_g, far_rows_of(far_kv, 0), far_rows_of(far_kv, 1), p_far, far_slim_rows, b)
        dq[:, lanes_of(b)] += unnear(near_part, b) + unfar(far_part, b)

    def unnormalize(inv_ref, grad, i):
        for b in range(GROUPS):
            inverse = inv_ref[:, lanes_of(b)]
            unit = qkv[:, lanes_of(GROUPS * i + b)].astype(F32) * inverse
            d = grad[:, lanes_of(b)]
            high, low = split(unit * d)
            along = nn(high, block_ref[...]) + nn(low, block_ref[...])
            dqkv[:, lanes_of(GROUPS * i + b)] = (inverse * (d - unit * along)).astype(BF)

    for t in y_peers:
        arrived(far_qg.at[core, t], r_fqg.at[t])
    send(far_qg.at[core], far_qg.at[core], r_cqg, partner)

    for t in z_peers:
        arrived(far_sz.at[t], r_sz.at[t])
    far_s[core, y] = jnp.sum(far_sz[...], axis=0)
    for t in y_peers:
        send(far_s.at[core, y], far_s.at[core, y], r_fs.at[core, y], at(t, z, core))
        send(far_s.at[core, y], far_s.at[core, y], r_fs.at[core, y], at(t, z, other))
    send(far_s.at[core, y], far_s.at[core, y], r_fs.at[core, y], partner)

    unnormalize(inv_q, dq, 0)
    attn_t[...] = attn.T
    dqkv_t[:WIDTH, :] = dqkv[:, :WIDTH].T
    for t in range(NY):
        dealt = nn(perm_o[...], attn_t[t * OROWS : (t + 1) * OROWS, :])
        for o in range(OWNERS):
            stage[o, t * OOWN : (t + 1) * OOWN, :] = dealt[o * OOWN : (o + 1) * OOWN]

    def deal_rows(t, first):
        dealt = nn(perm_q[...], dqkv_t[t * QROWS : (t + 1) * QROWS, :])
        for o in range(OWNERS):
            stage[o, first : first + QOWN, :] = dealt[o * QOWN : (o + 1) * QOWN]

    deal_rows(0, NY * OOWN)
    for o in range(OWNERS):
        stage[o, EARLY - 8 : EARLY, :] = jnp.zeros((8, 128), F32)
    early_out[...] = stage[:, :EARLY, :].astype(BF)
    for o in owners:
        send(early_out.at[o], early_in.at[own], r_early.at[own], owner(o))
    early_in[own] = early_out[own]
    branch_ref[...] = nn(attn, wout_ref[...]).astype(BF)

    for all_, recv, forward_recv in ((toks, r_tok, r_ftok), (cots, r_cot, r_fcot)):
        for t in x_peers:
            arrived(all_.at[core * NX + t], recv.at[t])
            send(all_.at[core * NX + t], all_.at[core * NX + t], forward_recv.at[t], partner)

    def key_side(keys, values, queries, grads, columns, b):
        q, g = queries(b), grads(b)
        s = nt(spread(keys[:, lanes_of(b)]), q)
        grad_p = nt(spread(values[:, lanes_of(b)]), g)
        ps, ds = [], []
        for h in range(GROUP):
            n = GROUP * b + h
            p = jnp.exp(s[h * 16 : (h + 1) * 16] * scale_ref[n]) * columns[n : n + 1, :]
            ps.append(p)
            ds.append(
                scale_ref[n] * p * (grad_p[h * 16 : (h + 1) * 16] - columns[HEADS + n : HEADS + n + 1, :])
            )
        p, d = jnp.concatenate(ps, axis=0).astype(BF), jnp.concatenate(ds, axis=0).astype(BF)
        return fold(nn(d, q)), fold(nn(p, g))

    for t in near_peers:
        arrived(near_s.at[t], r_ns.at[t])
    for t in near_other:
        arrived(near_qg.at[t], r_nqg.at[t])
    columns = near_s[...].reshape(TOK, 128).T
    near_k, near_v = near_kv[mine, 0], near_kv[mine, 1]
    for b in range(GROUPS):
        k_part, v_part = key_side(near_k, near_v, near_rows(near_qg, 0), near_rows(near_qg, 1), columns, b)
        dk[:, lanes_of(b)] += unnear(k_part, b)
        dv[:, lanes_of(b)] += unnear(v_part, b)

    arrived(far_qg.at[other], r_cqg)
    for t in y_peers:
        arrived(far_s.at[core, t], r_fs.at[core, t])
    for t in range(NY):
        arrived(far_s.at[other, t], r_fs.at[other, t])
    columns = far_s[...].reshape(TOK, 128).T
    for b in range(GROUPS):
        k_part, v_part = key_side(far_k, far_v, far_rows_of(far_qg, 0), far_rows_of(far_qg, 1), columns, b)
        dk[:, lanes_of(b)] += unfar(k_part, b)
        dv[:, lanes_of(b)] += unfar(v_part, b)

    unnormalize(inv_k, dk, 1)
    dqkv[:, 2 * WIDTH :] = dv[...].astype(BF)
    dqkv_t[WIDTH:, :] = dqkv[:, WIDTH:].T
    for t in range(1, NY):
        deal_rows(t, (t - 1) * QOWN)
    for o in range(OWNERS):
        stage[o, LATE - 8 : LATE, :] = jnp.zeros((8, 128), F32)
    late_out[...] = stage[...].astype(BF)
    for o in owners:
        send(late_out.at[o], late_in.at[own], r_late.at[own], owner(o))
    late_in[own] = late_out[own]
    for o in owners:
        arrived(early_in.at[o], r_early.at[o])
    for t in range(NX):
        arrived(toks.at[other * NX + t], r_ftok.at[t])
        arrived(cots.at[other * NX + t], r_fcot.at[t])

    def factors(ref, rows):
        return jnp.concatenate([ref[o, rows, :] for o in range(OWNERS)], axis=1)

    o_sum[...] = nn(factors(early_in, slice(0, NY * OOWN)), cots[...].reshape(OWNERS * TOK, WIDTH))
    tokens = toks[...].reshape(OWNERS * TOK, WIDTH)
    q_sum[: EARLY - NY * OOWN, :] = nn(factors(early_in, slice(NY * OOWN, EARLY)), tokens)
    grad_tok_ref[...] = nn(dqkv[...], wqkv_ref[...]).astype(BF)
    for o in owners:
        arrived(late_in.at[o], r_late.at[o])
    late = nn(factors(late_in, slice(0, LATE)), tokens)
    q_sum[QOWN:, :] = late[: (NY - 1) * QOWN]

    y_right, y_left = at(lax.rem(y + 1, NY), z, core), at(lax.rem(y + NY - 1, NY), z, core)
    a, b_ = slice(0, PIECE // 2), slice(PIECE // 2, PIECE)

    def piece(t):
        q_rows = pl.ds(pl.multiple_of(t * QOWN, 8), QOWN)
        o_rows = pl.ds(pl.multiple_of(t * OOWN, 8), OOWN)
        return jnp.concatenate([q_sum[q_rows, :], o_sum[o_rows, :]], axis=0)

    def y_out(slot, part, device):
        y_send[slot] = part.astype(BF)
        send(y_send.at[slot], y_recv.at[slot], r_y.at[slot], device)

    def y_in(slot):
        arrived(y_recv.at[slot], r_y.at[slot])
        return y_recv[slot].astype(F32)

    part = piece(lax.rem(y + 2, NY))
    y_out(0, part[a], y_right)
    y_out(1, part[b_], y_left)
    right_part, left_part = piece(lax.rem(y + 1, NY)), piece(lax.rem(y + NY - 1, NY))
    y_out(2, right_part[b_], y_right)
    y_out(4, left_part[a], y_left)
    y_out(3, right_part[a] + y_in(0), y_right)
    y_out(5, left_part[b_] + y_in(1), y_left)
    part = piece(y)
    part = jnp.concatenate([part[a] + y_in(4) + y_in(3), part[b_] + y_in(2) + y_in(5)], axis=0)

    dealt = nn(deal_ref[...], part.astype(BF)).astype(BF)
    for t in range(NZ):
        z_send[t] = dealt[16 * t : 16 * (t + 1), :]
    for t in z_peers:
        send(z_send.at[t], z_recv.at[z], r_z.at[z], at(y, t, core))
    z_recv[z] = z_send[z]
    for t in z_peers:
        arrived(z_recv.at[t], r_z.at[t])
    share = jnp.sum(z_recv[...].astype(F32), axis=0)
    qkv_out[...] = share[: QOWN // NZ]
    out_out[...] = share[QOWN // NZ : PIECE // NZ]
    for copy in sent:
        copy.wait_send()


def finish(*refs):
    count = len(refs) // 2
    copies = [pltpu.make_async_copy(refs[n], refs[count + n], refs[-1].at[n]) for n in range(count)]
    for copy in copies:
        copy.start()
    for copy in copies:
        copy.wait()


def constants():
    lane = np.arange(WIDTH)
    block = (lane[:LANES, None] // HEAD == lane[None, :LANES] // HEAD).astype(np.float32)
    compact = np.zeros((WIDTH, 256), np.float32)
    compact[np.arange(HEADS) * HEAD, np.arange(HEADS)] = 1
    compact[lane, 128 + HEADS + lane // HEAD] = 1
    order = np.zeros((2 * TILES * 16, NZ * PACK), np.float32)
    for t in range(2):
        for j in range(TILES):
            for s in range(NZ):
                for i in range(FAR):
                    order[(t * TILES + j) * 16 + s * FAR + i, s * PACK + (t * FAR + i) * TILES + j] = 1

    def deal_out(each):
        index = np.arange(NZ * OWNERS * each).reshape(NZ, OWNERS, each).transpose(1, 0, 2).reshape(-1)
        return np.eye(index.size, dtype=np.float32)[index]

    deal = np.zeros((NZ * 16, PIECE), np.float32)
    for t in range(NZ):
        for i in range(9):
            deal[t * 16 + i, t * 9 + i] = 1
        for i in range(3):
            deal[t * 16 + 9 + i, QOWN + t * 3 + i] = 1
    return [jnp.asarray(m, BF) for m in (block, compact, order, deal_out(9), deal_out(3), deal)]


def body(tokens, cotangent, qkv_weight, out_weight, logit_scale, near_offsets, far_offsets):
    fixed = constants()
    smem = pl.BlockSpec(memory_space=pltpu.SMEM)
    hbm = pl.BlockSpec(memory_space=pltpu.HBM)
    vmem = pl.BlockSpec(memory_space=pltpu.VMEM)
    dma = pltpu.SemaphoreType.DMA
    wide_bf = pltpu.VMEM((TOK, WIDTH), BF)
    wide = pltpu.VMEM((TOK, WIDTH), F32)

    def held(*shape):
        return pltpu.VMEM(shape, BF)

    def held_f32(*shape):
        return pltpu.VMEM(shape, F32)

    results = [
        jax.ShapeDtypeStruct((TOK, WIDTH), BF),
        jax.ShapeDtypeStruct((TOK, WIDTH), BF),
        jax.ShapeDtypeStruct((9, WIDTH), F32),
        jax.ShapeDtypeStruct((3, WIDTH), F32),
    ]
    values = pl.pallas_call(
        layer,
        out_shape=results,
        in_specs=[smem] * 3 + [hbm] * 10,
        out_specs=[vmem] * 4,
        scratch_shapes=[
            held(3 * WIDTH, WIDTH), held(WIDTH, WIDTH), *[held(*m.shape) for m in fixed],
            held(OWNERS, TOK, WIDTH), held(OWNERS, TOK, WIDTH),
            held(TOK, 3 * WIDTH), wide_bf, wide_bf, wide_bf, wide, wide,
            held_f32(HEADS * TOK, 128), held_f32(GROUPS, GROUP * 16, 128), held_f32(GROUPS, GROUP * 16, 128),
            wide, wide, wide, wide, wide, held(TOK, 3 * WIDTH), held_f32(PACK, 128),
            held(SPAN, 2, NEAR, WIDTH), held(SPAN, 2, NEAR, WIDTH), held_f32(SPAN, NEAR, 128),
            held(NZ, PACK, 128), held(NZ, PACK, 128),
            held(2, NY, 2, 16, WIDTH), held(2, NY, 2, 16, WIDTH), held_f32(NZ, 16, 128), held_f32(2, NY, 16, 128),
            held(WIDTH, TOK), held(3 * WIDTH, TOK), held_f32(OWNERS, LATE, 128),
            held(OWNERS, EARLY, 128), held(OWNERS, EARLY, 128), held(OWNERS, LATE, 128), held(OWNERS, LATE, 128),
            held_f32(NY * QOWN, WIDTH), held_f32(NY * OOWN, WIDTH),
            held(6, PIECE // 2, WIDTH), held(6, PIECE // 2, WIDTH),
            held(NZ, 16, WIDTH), held(NZ, 16, WIDTH),
            dma((24,)), dma((112,)),
            dma((4,)), dma((4,)), dma((4,)), dma((4,)),
            dma((8,)), dma((8,)), dma((8,)), dma((8,)), dma((8,)), dma((8,)), dma((4,)), dma((4,)), dma, dma,
            dma((2, 4)), dma((8,)), dma((8,)), dma((6,)), dma((8,)),
        ],
        compiler_params=pltpu.CompilerParams(
            collective_id=0, has_side_effects=True, vmem_limit_bytes=56 * 1024 * 1024
        ),
    )(logit_scale, near_offsets, far_offsets, tokens[0], cotangent[0], qkv_weight, out_weight, *fixed)
    branch, grad_inputs, qkv_share, out_share = pl.pallas_call(
        finish,
        out_shape=results,
        in_specs=[pl.BlockSpec(memory_space=pl.ANY)] * 4,
        out_specs=[pl.BlockSpec(memory_space=pl.ANY)] * 4,
        scratch_shapes=[dma((4,))],
        compiler_params=pltpu.CompilerParams(vmem_limit_bytes=1024 * 1024),
    )(*values)
    return (branch[None], grad_inputs[None], qkv_share, out_share)


def solution(mesh):
    return jax.shard_map(
        body,
        mesh=mesh,
        in_specs=(P("dp", "seq", None), P("dp", "seq", None), P(), P(), P(), P(), P()),
        out_specs=(
            P("dp", "seq", None),
            P("dp", "seq", None),
            P(("seq", "dp"), None),
            P(("seq", "dp"), None),
        ),
        check_vma=False,
    )
```

```python
import jax
import jax.numpy as jnp
import numpy as np
from jax import lax
from jax.experimental import pallas as pl
from jax.experimental.pallas import tpu as pltpu
from jax.sharding import PartitionSpec as P

BF = jnp.bfloat16
F32 = jnp.float32
MESH = pl.DeviceIdType.MESH
EPS = 1e-06

NY, NZ, NX = 4, 8, 4
TOK = 128
WIDTH = 768
HEADS = 12
HEAD = 64
GROUP = 4
LANES = GROUP * HEAD
GROUPS = HEADS // GROUP
SPAN = 8
NEAR = TOK // SPAN
FAR = 2
PACK = 32
TILES = WIDTH // 128
OWNERS = 2 * NX
QROWS = 3 * WIDTH // NY
OROWS = WIDTH // NY
QOWN, OOWN = QROWS // OWNERS, OROWS // OWNERS
PIECE = QOWN + OOWN
EARLY = 176
LATE = 224


def nn(a, b):
    return lax.dot_general(a, b, (((1,), (0,)), ((), ())), preferred_element_type=F32)


def nt(a, b):
    return lax.dot_general(a, b, (((1,), (1,)), ((), ())), preferred_element_type=F32)


def tn(a, b):
    return lax.dot_general(a, b, (((0,), (0,)), ((), ())), preferred_element_type=F32)


def split(x):
    high = x.astype(BF)
    return high, (x - high.astype(F32)).astype(BF)


def iota(shape, dim):
    return lax.broadcasted_iota(jnp.int32, shape, dim)


def place():
    seq = lax.axis_index("seq")
    return seq, lax.rem(seq, 2), lax.rem(seq // 2, NZ), seq // (2 * NZ)


def at(y, z, core):
    return {"seq": (y * NZ + z) * 2 + core}


def remote(src, dst, send, recv, device):
    return pltpu.make_async_remote_copy(
        src_ref=src, dst_ref=dst, send_sem=send, recv_sem=recv, device_id=device, device_id_type=MESH
    )


def lanes_of(b):
    return slice(b * LANES, (b + 1) * LANES)


def layer(
    scale_ref, near_ref, far_ref, tok_hbm, cot_hbm, wqkv_hbm, wout_hbm,
    block_hbm, compact_hbm, order_hbm, perm_q_hbm, perm_o_hbm, deal_hbm,
    branch_ref, grad_tok_ref, qkv_out, out_out,
    wqkv_ref, wout_ref, block_ref, compact_ref, order_ref, perm_q, perm_o, deal_ref,
    toks, cots, qkv, qn, kn, gr, inv_q, inv_k, p_loc, p_near, p_far, num, den, dq, dk, dv, dqkv, pack,
    near_kv, near_qg, near_s, far_zkv, far_zqg, far_kv, far_qg, far_sz, far_s,
    attn_t, dqkv_t, stage, corr, chosen, early_out, early_in, late_out, late_in, q_sum, o_sum, y_send, y_recv, z_send, z_recv,
    loads, sends, r_tok, r_cot, r_ftok, r_fcot, r_nkv, r_nqg, r_ns, r_zkv, r_zqg, r_sz, r_fkv, r_fqg, r_ckv, r_cqg,
    r_fs, r_early, r_late, r_corr, r_y, r_z,
):
    seq, core, z, y = place()
    x = lax.axis_index("dp")
    mine = lax.rem(seq, SPAN)
    base = seq - mine
    other = 1 - core
    own = core * NX + x

    loading = []

    def load(src, dst):
        copy = pltpu.make_async_copy(src, dst, loads.at[len(loading)])
        copy.start()
        loading.append(copy)

    def load_rows(src, dst, start, stop):
        for first in range(start, stop, LANES):
            load(src.at[first : first + LANES], dst.at[first : first + LANES])

    load(tok_hbm, toks.at[own])
    load(block_hbm, block_ref)
    load_rows(wqkv_hbm, wqkv_ref, WIDTH, 3 * WIDTH)
    load(cot_hbm, cots.at[own])
    load_rows(wqkv_hbm, wqkv_ref, 0, WIDTH)
    load_rows(wout_hbm, wout_ref, 0, WIDTH)

    z_peers = [lax.rem(z + d, NZ) for d in range(1, NZ)]
    y_peers = [lax.rem(y + d, NY) for d in range(1, NY)]
    x_peers = [lax.rem(x + d, NX) for d in range(1, NX)]
    near_peers = [lax.rem(mine + d, SPAN) for d in range(1, SPAN)]
    near_same = [2 * lax.rem(mine // 2 + d, SPAN // 2) + core for d in range(1, SPAN // 2)]
    near_other = [2 * lax.rem(mine // 2 + d, SPAN // 2) + other for d in range(SPAN // 2)]
    partner = at(y, z, other)
    pair = seq - core

    def owner(o):
        return {"seq": pair + o // NX, "dp": lax.rem(o, NX)}

    owners = [lax.rem(own + d, OWNERS) for d in range(1, OWNERS)]
    barrier = pltpu.get_barrier_semaphore()
    greeted = (
        [at(y, t, core) for t in z_peers]
        + [{"seq": base + t} for t in near_other]
        + [at(t, z, core) for t in y_peers]
        + [at(t, z, other) for t in y_peers]
        + [{"seq": seq, "dp": t} for t in x_peers]
        + [{"seq": pair + other, "dp": t} for t in x_peers]
    )
    for device in greeted:
        pl.semaphore_signal(barrier, inc=1, device_id=device, device_id_type=MESH)
    sent = []

    def send(src, dst, recv, device):
        copy = remote(src, dst, sends.at[len(sent)], recv, device)
        copy.start()
        sent.append(copy)

    def arrived(ref, recv):
        remote(ref, ref, sends.at[0], recv, {"seq": seq}).wait_recv()

    head_lane = iota((1, LANES), 1) // HEAD
    picks_f = [(head_lane == h).astype(F32) for h in range(GROUP)]
    picks = [m.astype(BF) for m in picks_f]

    def spread(x):
        return jnp.concatenate([x * m for m in picks], axis=0)

    def fold(x):
        rows = x.shape[0] // GROUP
        return sum(x[h * rows : (h + 1) * rows] * picks_f[h] for h in range(GROUP))

    wide_head = iota((1, WIDTH), 1) // HEAD
    slim_head = iota((1, 128), 1)
    slim_head = jnp.where(slim_head >= HEADS, slim_head - HEADS, slim_head)
    near_row, far_row = jnp.zeros((1, WIDTH), jnp.int32), jnp.zeros((1, WIDTH), jnp.int32)
    near_slim, far_slim = jnp.zeros((1, 128), jnp.int32), jnp.zeros((1, 128), jnp.int32)
    for h in range(HEADS):
        near_row = jnp.where(wide_head == h, near_ref[h], near_row)
        far_row = jnp.where(wide_head == h, far_ref[h], far_row)
        near_slim = jnp.where(slim_head == h, near_ref[h], near_slim)
        far_slim = jnp.where(slim_head == h, far_ref[h], far_slim)
    near_mask = ((iota((TOK, WIDTH), 0) & (SPAN - 1)) == near_row).astype(F32)
    far_mask = ((iota((TOK, WIDTH), 0) & (TOK // FAR - 1)) == far_row).astype(F32)
    near_bf, far_bf = near_mask.astype(BF), far_mask.astype(BF)
    near_slim = ((iota((TOK, 128), 0) & (SPAN - 1)) == near_slim).astype(F32).astype(BF)
    far_slim = ((iota((TOK, 128), 0) & (TOK // FAR - 1)) == far_slim).astype(F32).astype(BF)
    row, token = iota((NEAR, TOK), 0), iota((NEAR, TOK), 1)
    take_near = (token // SPAN == row).astype(F32).astype(BF)
    take_far = (token // (TOK // FAR) == row).astype(F32).astype(BF)
    take_far_z = ((row // FAR == z) & (token // (TOK // FAR) == (row & 1))).astype(F32).astype(BF)

    def unnear(x, b):
        return jnp.broadcast_to(x[:, None, :], (NEAR, SPAN, LANES)).reshape(TOK, LANES) * near_mask[:, lanes_of(b)]

    def unfar(x, b):
        rows = [jnp.broadcast_to(x[i : i + 1], (TOK // FAR, LANES)) for i in range(FAR)]
        return jnp.concatenate(rows, axis=0) * far_mask[:, lanes_of(b)]

    def norms(columns):
        wide = columns.astype(F32)
        high, low = split(wide * wide)
        inverse = lax.rsqrt(nn(high, block_ref[...]) + nn(low, block_ref[...]) + EPS)
        return inverse, wide * inverse

    far_rows = []

    def packed(pair_of):
        pack[2 * FAR * TILES :, :] = jnp.zeros((PACK - 2 * FAR * TILES, 128), F32)
        for i, picked in enumerate(pair_of):
            for r in range(FAR):
                for t in range(TILES):
                    at_row = (i * FAR + r) * TILES + t
                    pack[at_row : at_row + 1, :] = picked[r : r + 1, 128 * t : 128 * (t + 1)]
        return pack[...].astype(BF)

    def leave(pair_of, far_into, near_into):
        picked = [nn(take_far, x_ * far_bf) for x_ in pair_of]
        far_rows.extend(x_.astype(BF) for x_ in picked)
        far_into[z] = packed(picked)
        for i, x_ in enumerate(pair_of):
            near_into[mine, i] = nn(take_near, x_ * near_bf).astype(BF)

    for copy in loading[:2]:
        copy.wait()
    tok = toks[own]
    for b in range(GROUPS, 3 * GROUPS):
        loading[2 + b - GROUPS].wait()
        qkv[:, lanes_of(b)] = nt(tok, wqkv_ref[lanes_of(b), :]).astype(BF)
    for b in range(GROUPS):
        inverse, unit = norms(qkv[:, lanes_of(GROUPS + b)])
        inv_k[:, lanes_of(b)] = inverse
        kn[:, lanes_of(b)] = unit.astype(BF)
    pl.semaphore_wait(barrier, len(greeted))
    leave((kn[...], qkv[:, 2 * WIDTH :]), far_zkv, near_kv)
    for t in z_peers:
        send(far_zkv.at[z], far_zkv.at[z], r_zkv.at[z], at(y, t, core))

    first = len(loading)
    load(order_hbm, order_ref)
    load(compact_hbm, compact_ref)
    load(perm_q_hbm, perm_q)
    load(perm_o_hbm, perm_o)
    load(deal_hbm, deal_ref)
    for copy in loading[2 + 2 * GROUPS : first]:
        copy.wait()
    cot = cots[own]
    for b in range(GROUPS):
        qkv[:, lanes_of(b)] = nt(tok, wqkv_ref[lanes_of(b), :]).astype(BF)
        gr[:, lanes_of(b)] = nt(cot, wout_ref[lanes_of(b), :]).astype(BF)
        inverse, unit = norms(qkv[:, lanes_of(b)])
        inv_q[:, lanes_of(b)] = inverse
        qn[:, lanes_of(b)] = unit.astype(BF)
    leave((qn[...], gr[...]), far_zqg, near_qg)
    for t in near_same:
        send(near_kv.at[mine], near_kv.at[mine], r_nkv.at[mine], {"seq": base + t})
    send(near_kv.at[mine], near_kv.at[mine], r_nkv.at[mine], partner)
    for all_, recv, forward_recv in ((toks, r_tok, r_ftok), (cots, r_cot, r_fcot)):
        for t in x_peers:
            send(all_.at[own], all_.at[own], recv.at[x], {"seq": seq, "dp": t})
        send(all_.at[own], all_.at[own], forward_recv.at[x], partner)

    ones = spread(jnp.ones((TOK, LANES), BF))
    for b in range(GROUPS):
        s = nt(spread(qn[:, lanes_of(b)]), kn[:, lanes_of(b)])
        ps = []
        for h in range(GROUP):
            p = jnp.exp(s[h * TOK : (h + 1) * TOK] * scale_ref[GROUP * b + h])
            p_loc[(GROUP * b + h) * TOK : (GROUP * b + h + 1) * TOK, :] = p
            ps.append(p.astype(BF))
        ps = jnp.concatenate(ps, axis=1)
        num[:, lanes_of(b)] = nn(ps, spread(qkv[:, lanes_of(2 * GROUPS + b)]))
        den[:, lanes_of(b)] = nn(ps, ones)

    for copy in loading[first:]:
        copy.wait()

    def along_y(packets, recv_z, into, recv):
        for t in z_peers:
            arrived(packets.at[t], recv_z.at[t])
        ordered = nn(order_ref[...], packets[...].reshape(NZ * PACK, 128)).astype(BF)
        for i in range(2):
            for t in range(TILES):
                first = (i * TILES + t) * 16
                into[core, y, i, :, 128 * t : 128 * (t + 1)] = ordered[first : first + 16, :]
        for t in y_peers:
            send(into.at[core, y], into.at[core, y], recv.at[y], at(t, z, core))

    def across(ref, recv):
        for t in near_same:
            arrived(ref.at[t], recv.at[t])
            send(ref.at[t], ref.at[t], recv.at[t], partner)

    def hand_over(ref, recv, recv_core):
        send(ref.at[core, y], ref.at[core, y], recv_core.at[y], partner)
        for t in y_peers:
            arrived(ref.at[core, t], recv.at[t])
            send(ref.at[core, t], ref.at[core, t], recv_core.at[t], partner)

    def forward(queries, keys, values, p_ref):
        results = []
        for b in range(GROUPS):
            s = nt(spread(queries[:, lanes_of(b)]), keys(b))
            ps = []
            for h in range(GROUP):
                ps.append(jnp.exp(s[h * 16 : (h + 1) * 16] * scale_ref[GROUP * b + h]))
            p = jnp.concatenate(ps, axis=0)
            p_ref[b] = p
            total = jnp.broadcast_to(jnp.sum(p, axis=1, keepdims=True), (GROUP * 16, LANES))
            results.append((fold(nn(p.astype(BF), values(b))), fold(total)))
        return results

    def near_rows(ref, i):
        return lambda b: jnp.concatenate([ref[s, i, :, lanes_of(b)] for s in range(SPAN)], axis=0)

    def far_rows_of(ref, i):
        return lambda b: jnp.concatenate(
            [ref[s, t, i, :, lanes_of(b)] for s in range(2) for t in range(NY)], axis=0
        )

    along_y(far_zkv, r_zkv, far_kv, r_fkv)
    across(near_kv, r_nkv)
    for t in z_peers:
        send(far_zqg.at[z], far_zqg.at[z], r_zqg.at[z], at(y, t, core))
    for t in near_same:
        send(near_qg.at[mine], near_qg.at[mine], r_nqg.at[mine], {"seq": base + t})
    send(near_qg.at[mine], near_qg.at[mine], r_nqg.at[mine], partner)
    for t in near_other:
        arrived(near_kv.at[t], r_nkv.at[t])
    near_q, near_g = near_qg[mine, 0], near_qg[mine, 1]
    for b, (n_part, d_part) in enumerate(forward(near_q, near_rows(near_kv, 0), near_rows(near_kv, 1), p_near)):
        num[:, lanes_of(b)] += unnear(n_part, b)
        den[:, lanes_of(b)] += unnear(d_part, b)
    hand_over(far_kv, r_fkv, r_ckv)
    along_y(far_zqg, r_zqg, far_qg, r_fqg)
    for t in range(NY):
        arrived(far_kv.at[other, t], r_ckv.at[t])
    far_k, far_v, far_q, far_g = far_rows
    for b, (n_part, d_part) in enumerate(forward(far_q, far_rows_of(far_kv, 0), far_rows_of(far_kv, 1), p_far)):
        num[:, lanes_of(b)] += unfar(n_part, b)
        den[:, lanes_of(b)] += unfar(d_part, b)

    inverse = 1.0 / den[...]
    attn = (num[...] * inverse).astype(BF)
    high, low = split(inverse)
    slim = nn(high, compact_ref[:, :128]) + nn(low, compact_ref[:, :128])
    high, low = split(gr[...].astype(F32) * attn.astype(F32))
    slim = slim + nn(high, compact_ref[:, 128:]) + nn(low, compact_ref[:, 128:])
    high, low = split(slim)

    def take(selection, mask):
        return nn(selection, high * mask) + nn(selection, low * mask)

    far_sz[z] = take(take_far_z, far_slim)
    for t in z_peers:
        send(far_sz.at[z], far_sz.at[z], r_sz.at[z], at(y, t, core))
    near_slim_rows = take(take_near, near_slim)
    far_slim_rows = take(take_far, far_slim)
    near_s[mine] = near_slim_rows
    for t in near_peers:
        send(near_s.at[mine], near_s.at[mine], r_ns.at[mine], {"seq": base + t})
    across(near_qg, r_nqg)

    for b in range(GROUPS):
        g = spread(gr[:, lanes_of(b)])
        grad_p = nt(g, qkv[:, lanes_of(2 * GROUPS + b)])
        ps, ds = [], []
        for h in range(GROUP):
            n = GROUP * b + h
            p = p_loc[n * TOK : (n + 1) * TOK, :] * slim[:, n : n + 1]
            d = scale_ref[n] * p * (grad_p[h * TOK : (h + 1) * TOK] - slim[:, HEADS + n : HEADS + n + 1])
            ps.append(p.astype(BF))
            ds.append(d.astype(BF))
        dq[:, lanes_of(b)] = nn(jnp.concatenate(ds, axis=1), spread(kn[:, lanes_of(b)]))
        dk[:, lanes_of(b)] = tn(jnp.concatenate(ds, axis=0), spread(qn[:, lanes_of(b)]))
        dv[:, lanes_of(b)] = tn(jnp.concatenate(ps, axis=0), g)

    def query_side(grads, keys, values, p_ref, slim_rows, b):
        grad_p = nt(spread(grads[:, lanes_of(b)]), values(b))
        ds = []
        for h in range(GROUP):
            n = GROUP * b + h
            p = p_ref[b, h * 16 : (h + 1) * 16, :] * slim_rows[:, n : n + 1]
            ds.append(
                scale_ref[n] * p * (grad_p[h * 16 : (h + 1) * 16] - slim_rows[:, HEADS + n : HEADS + n + 1])
            )
        return fold(nn(jnp.concatenate(ds, axis=0).astype(BF), keys(b)))

    for b in range(GROUPS):
        near_part = query_side(near_g, near_rows(near_kv, 0), near_rows(near_kv, 1), p_near, near_slim_rows, b)
        far_part = query_side(far_g, far_rows_of(far_kv, 0), far_rows_of(far_kv, 1), p_far, far_slim_rows, b)
        dq[:, lanes_of(b)] += unnear(near_part, b) + unfar(far_part, b)

    def through(inverse, unit, d):
        high, low = split(unit * d)
        along = nn(high, block_ref[...]) + nn(low, block_ref[...])
        return inverse * (d - unit * along)

    def unnormalize(inv_ref, grad, i):
        for b in range(GROUPS):
            inverse = inv_ref[:, lanes_of(b)]
            unit = qkv[:, lanes_of(GROUPS * i + b)].astype(F32) * inverse
            dqkv[:, lanes_of(GROUPS * i + b)] = through(inverse, unit, grad[:, lanes_of(b)]).astype(BF)

    hand_over(far_qg, r_fqg, r_cqg)

    for t in z_peers:
        arrived(far_sz.at[t], r_sz.at[t])
    far_s[core, y] = jnp.sum(far_sz[...], axis=0)
    for t in y_peers:
        send(far_s.at[core, y], far_s.at[core, y], r_fs.at[core, y], at(t, z, core))
        send(far_s.at[core, y], far_s.at[core, y], r_fs.at[core, y], at(t, z, other))
    send(far_s.at[core, y], far_s.at[core, y], r_fs.at[core, y], partner)

    unnormalize(inv_q, dq, 0)
    attn_t[...] = attn.T
    dqkv_t[:WIDTH, :] = dqkv[:, :WIDTH].T
    for t in range(NY):
        dealt = nn(perm_o[...], attn_t[t * OROWS : (t + 1) * OROWS, :])
        for o in range(OWNERS):
            stage[o, t * OOWN : (t + 1) * OOWN, :] = dealt[o * OOWN : (o + 1) * OOWN]

    def deal_rows(t, first):
        dealt = nn(perm_q[...], dqkv_t[t * QROWS : (t + 1) * QROWS, :])
        for o in range(OWNERS):
            stage[o, first : first + QOWN, :] = dealt[o * QOWN : (o + 1) * QOWN]

    deal_rows(0, NY * OOWN)
    for o in range(OWNERS):
        stage[o, EARLY - 8 : EARLY, :] = jnp.zeros((8, 128), F32)
    early_out[...] = stage[:, :EARLY, :].astype(BF)
    for o in owners:
        send(early_out.at[o], early_in.at[own], r_early.at[own], owner(o))
    early_in[own] = early_out[own]
    branch_ref[...] = nn(attn, wout_ref[...]).astype(BF)

    for all_, recv, forward_recv in ((toks, r_tok, r_ftok), (cots, r_cot, r_fcot)):
        for t in x_peers:
            arrived(all_.at[core * NX + t], recv.at[t])
            send(all_.at[core * NX + t], all_.at[core * NX + t], forward_recv.at[t], partner)

    def key_side(keys, values, queries, grads, columns, b):
        q, g = queries(b), grads(b)
        s = nt(spread(keys[:, lanes_of(b)]), q)
        grad_p = nt(spread(values[:, lanes_of(b)]), g)
        ps, ds = [], []
        for h in range(GROUP):
            n = GROUP * b + h
            p = jnp.exp(s[h * 16 : (h + 1) * 16] * scale_ref[n]) * columns[n : n + 1, :]
            ps.append(p)
            ds.append(
                scale_ref[n] * p * (grad_p[h * 16 : (h + 1) * 16] - columns[HEADS + n : HEADS + n + 1, :])
            )
        p, d = jnp.concatenate(ps, axis=0).astype(BF), jnp.concatenate(ds, axis=0).astype(BF)
        return fold(nn(d, q)), fold(nn(p, g))

    for t in near_peers:
        arrived(near_s.at[t], r_ns.at[t])
    for t in near_other:
        arrived(near_qg.at[t], r_nqg.at[t])
    columns = near_s[...].reshape(TOK, 128).T
    near_k, near_v = near_kv[mine, 0], near_kv[mine, 1]
    for b in range(GROUPS):
        k_part, v_part = key_side(near_k, near_v, near_rows(near_qg, 0), near_rows(near_qg, 1), columns, b)
        dk[:, lanes_of(b)] += unnear(k_part, b)
        dv[:, lanes_of(b)] += unnear(v_part, b)

    unnormalize(inv_k, dk, 1)
    dqkv[:, 2 * WIDTH :] = dv[...].astype(BF)
    dqkv_t[WIDTH:, :] = dqkv[:, WIDTH:].T
    for t in range(1, NY):
        deal_rows(t, (t - 1) * QOWN)
    for o in range(OWNERS):
        stage[o, LATE - 8 : LATE, :] = jnp.zeros((8, 128), F32)
    late_out[...] = stage[...].astype(BF)
    for o in owners:
        send(late_out.at[o], late_in.at[own], r_late.at[own], owner(o))
    late_in[own] = late_out[own]

    far_inverse, far_unit = [], []
    for b in range(GROUPS):
        high, low = split(inv_k[:, lanes_of(b)])
        mask = far_bf[:, lanes_of(b)]
        inverse = nn(take_far, high * mask) + nn(take_far, low * mask)
        far_inverse.append(inverse)
        far_unit.append(nn(take_far, qkv[:, lanes_of(GROUPS + b)] * mask) * inverse)
    n = iota((LATE, 1), 0)
    t = sum((n >= QOWN * i).astype(jnp.int32) for i in range(1, NY - 1))
    left = n - QOWN * t
    u = sum((left >= QOWN // NZ * i).astype(jnp.int32) for i in range(1, NZ))
    column = QROWS * (1 + t) + (QROWS // NZ) * u + (QOWN // NZ) * own + (left - QOWN // NZ * u) - WIDTH
    column = jnp.where(n < QOWN * (NY - 1), column, -1)
    chosen[...] = (iota((LATE, 2 * WIDTH), 1) == column).astype(F32).astype(BF)
    offsets = jnp.concatenate([far_row, far_row], axis=1).astype(F32).astype(BF)
    offsets = nt(chosen[...], jnp.broadcast_to(offsets, (16, 2 * WIDTH)))[:, :1]
    far_place = ((iota((LATE, 128), 1) & (TOK // FAR - 1)).astype(F32) == offsets).astype(F32)
    far_place = jnp.concatenate([far_place] * OWNERS, axis=1)
    spread_rows = (iota((16, OWNERS * TOK), 1) // (TOK // FAR) == iota((16, OWNERS * TOK), 0)).astype(F32).astype(BF)

    for t in range(NY):
        arrived(far_qg.at[other, t], r_cqg.at[t])
    for t in y_peers:
        arrived(far_s.at[core, t], r_fs.at[core, t])
    for t in range(NY):
        arrived(far_s.at[other, t], r_fs.at[other, t])
    columns = far_s[...].reshape(TOK, 128).T
    k_far, v_far = [], []
    for b in range(GROUPS):
        k_part, v_part = key_side(far_k, far_v, far_rows_of(far_qg, 0), far_rows_of(far_qg, 1), columns, b)
        k_far.append(through(far_inverse[b], far_unit[b], k_part))
        v_far.append(v_part)
    two_rows = [jnp.concatenate(parts, axis=1) for parts in (k_far, v_far)]
    corr[own] = packed(two_rows)
    for o in owners:
        send(corr.at[own], corr.at[own], r_corr.at[own], owner(o))

    for o in owners:
        arrived(early_in.at[o], r_early.at[o])
    for t in range(NX):
        arrived(toks.at[other * NX + t], r_ftok.at[t])
        arrived(cots.at[other * NX + t], r_fcot.at[t])

    def factors(ref, rows):
        return jnp.concatenate([ref[o, rows, :] for o in range(OWNERS)], axis=1)

    o_sum[...] = nn(factors(early_in, slice(0, NY * OOWN)), cots[...].reshape(OWNERS * TOK, WIDTH))
    tokens = toks[...].reshape(OWNERS * TOK, WIDTH)
    q_sum[: EARLY - NY * OOWN, :] = nn(factors(early_in, slice(NY * OOWN, EARLY)), tokens)

    for o in owners:
        arrived(late_in.at[o], r_late.at[o])
    for o in owners:
        arrived(corr.at[o], r_corr.at[o])
    ordered = nn(order_ref[...], corr[...].reshape(OWNERS * PACK, 128)).astype(BF)
    ordered = jnp.concatenate([ordered[16 * t : 16 * (t + 1)] for t in range(2 * TILES)], axis=1)
    added = nn(nt(chosen[...], ordered).astype(BF), spread_rows) * far_place
    late = nn((factors(late_in, slice(0, LATE)).astype(F32) + added).astype(BF), tokens)
    q_sum[QOWN:, :] = late[: (NY - 1) * QOWN]

    y_right, y_left = at(lax.rem(y + 1, NY), z, core), at(lax.rem(y + NY - 1, NY), z, core)
    a, b_ = slice(0, PIECE // 2), slice(PIECE // 2, PIECE)

    def piece(t):
        q_rows = pl.ds(pl.multiple_of(t * QOWN, 8), QOWN)
        o_rows = pl.ds(pl.multiple_of(t * OOWN, 8), OOWN)
        return jnp.concatenate([q_sum[q_rows, :], o_sum[o_rows, :]], axis=0)

    def y_out(slot, part, device):
        y_send[slot] = part.astype(BF)
        send(y_send.at[slot], y_recv.at[slot], r_y.at[slot], device)

    def y_in(slot):
        arrived(y_recv.at[slot], r_y.at[slot])
        return y_recv[slot].astype(F32)

    part = piece(lax.rem(y + 2, NY))
    y_out(0, part[a], y_right)
    y_out(1, part[b_], y_left)
    right_part, left_part = piece(lax.rem(y + 1, NY)), piece(lax.rem(y + NY - 1, NY))
    y_out(2, right_part[b_], y_right)
    y_out(4, left_part[a], y_left)
    for i, rows in enumerate(two_rows):
        for b in range(GROUPS):
            at_lanes = lanes_of(GROUPS * (1 + i) + b)
            dqkv[:, at_lanes] = (dqkv[:, at_lanes].astype(F32) + unfar(rows[:, lanes_of(b)], b)).astype(BF)
    grad_tok_ref[...] = nn(dqkv[...], wqkv_ref[...]).astype(BF)
    y_out(3, right_part[a] + y_in(0), y_right)
    y_out(5, left_part[b_] + y_in(1), y_left)
    part = piece(y)
    part = jnp.concatenate([part[a] + y_in(4) + y_in(3), part[b_] + y_in(2) + y_in(5)], axis=0)

    dealt = nn(deal_ref[...], part.astype(BF)).astype(BF)
    for t in range(NZ):
        z_send[t] = dealt[16 * t : 16 * (t + 1), :]
    for t in z_peers:
        send(z_send.at[t], z_recv.at[z], r_z.at[z], at(y, t, core))
    z_recv[z] = z_send[z]
    for t in z_peers:
        arrived(z_recv.at[t], r_z.at[t])
    share = jnp.sum(z_recv[...].astype(F32), axis=0)
    qkv_out[...] = share[: QOWN // NZ]
    out_out[...] = share[QOWN // NZ : PIECE // NZ]
    for copy in sent:
        copy.wait_send()


def finish(*refs):
    count = len(refs) // 2
    copies = [pltpu.make_async_copy(refs[n], refs[count + n], refs[-1].at[n]) for n in range(count)]
    for copy in copies:
        copy.start()
    for copy in copies:
        copy.wait()


def constants():
    lane = np.arange(WIDTH)
    block = (lane[:LANES, None] // HEAD == lane[None, :LANES] // HEAD).astype(np.float32)
    compact = np.zeros((WIDTH, 256), np.float32)
    compact[np.arange(HEADS) * HEAD, np.arange(HEADS)] = 1
    compact[lane, 128 + HEADS + lane // HEAD] = 1
    order = np.zeros((2 * TILES * 16, NZ * PACK), np.float32)
    for t in range(2):
        for j in range(TILES):
            for s in range(NZ):
                for i in range(FAR):
                    order[(t * TILES + j) * 16 + s * FAR + i, s * PACK + (t * FAR + i) * TILES + j] = 1

    def deal_out(each):
        index = np.arange(NZ * OWNERS * each).reshape(NZ, OWNERS, each).transpose(1, 0, 2).reshape(-1)
        return np.eye(index.size, dtype=np.float32)[index]

    deal = np.zeros((NZ * 16, PIECE), np.float32)
    for t in range(NZ):
        for i in range(9):
            deal[t * 16 + i, t * 9 + i] = 1
        for i in range(3):
            deal[t * 16 + 9 + i, QOWN + t * 3 + i] = 1
    return [jnp.asarray(m, BF) for m in (block, compact, order, deal_out(9), deal_out(3), deal)]


def body(tokens, cotangent, qkv_weight, out_weight, logit_scale, near_offsets, far_offsets):
    fixed = constants()
    smem = pl.BlockSpec(memory_space=pltpu.SMEM)
    hbm = pl.BlockSpec(memory_space=pltpu.HBM)
    vmem = pl.BlockSpec(memory_space=pltpu.VMEM)
    dma = pltpu.SemaphoreType.DMA
    wide_bf = pltpu.VMEM((TOK, WIDTH), BF)
    wide = pltpu.VMEM((TOK, WIDTH), F32)

    def held(*shape):
        return pltpu.VMEM(shape, BF)

    def held_f32(*shape):
        return pltpu.VMEM(shape, F32)

    results = [
        jax.ShapeDtypeStruct((TOK, WIDTH), BF),
        jax.ShapeDtypeStruct((TOK, WIDTH), BF),
        jax.ShapeDtypeStruct((9, WIDTH), F32),
        jax.ShapeDtypeStruct((3, WIDTH), F32),
    ]
    values = pl.pallas_call(
        layer,
        out_shape=results,
        in_specs=[smem] * 3 + [hbm] * 10,
        out_specs=[vmem] * 4,
        scratch_shapes=[
            held(3 * WIDTH, WIDTH), held(WIDTH, WIDTH), *[held(*m.shape) for m in fixed],
            held(OWNERS, TOK, WIDTH), held(OWNERS, TOK, WIDTH),
            held(TOK, 3 * WIDTH), wide_bf, wide_bf, wide_bf, wide, wide,
            held_f32(HEADS * TOK, 128), held_f32(GROUPS, GROUP * 16, 128), held_f32(GROUPS, GROUP * 16, 128),
            wide, wide, wide, wide, wide, held(TOK, 3 * WIDTH), held_f32(PACK, 128),
            held(SPAN, 2, NEAR, WIDTH), held(SPAN, 2, NEAR, WIDTH), held_f32(SPAN, NEAR, 128),
            held(NZ, PACK, 128), held(NZ, PACK, 128),
            held(2, NY, 2, 16, WIDTH), held(2, NY, 2, 16, WIDTH), held_f32(NZ, 16, 128), held_f32(2, NY, 16, 128),
            held(WIDTH, TOK), held(3 * WIDTH, TOK), held_f32(OWNERS, LATE, 128),
            held(OWNERS, PACK, 128), held(LATE, 2 * WIDTH),
            held(OWNERS, EARLY, 128), held(OWNERS, EARLY, 128), held(OWNERS, LATE, 128), held(OWNERS, LATE, 128),
            held_f32(NY * QOWN, WIDTH), held_f32(NY * OOWN, WIDTH),
            held(6, PIECE // 2, WIDTH), held(6, PIECE // 2, WIDTH),
            held(NZ, 16, WIDTH), held(NZ, 16, WIDTH),
            dma((24,)), dma((128,)),
            dma((4,)), dma((4,)), dma((4,)), dma((4,)),
            dma((8,)), dma((8,)), dma((8,)), dma((8,)), dma((8,)), dma((8,)), dma((4,)), dma((4,)), dma((4,)), dma((4,)),
            dma((2, 4)), dma((8,)), dma((8,)), dma((8,)), dma((6,)), dma((8,)),
        ],
        compiler_params=pltpu.CompilerParams(
            collective_id=0, has_side_effects=True, vmem_limit_bytes=56 * 1024 * 1024
        ),
    )(logit_scale, near_offsets, far_offsets, tokens[0], cotangent[0], qkv_weight, out_weight, *fixed)
    branch, grad_inputs, qkv_share, out_share = pl.pallas_call(
        finish,
        out_shape=results,
        in_specs=[pl.BlockSpec(memory_space=pl.ANY)] * 4,
        out_specs=[pl.BlockSpec(memory_space=pl.ANY)] * 4,
        scratch_shapes=[dma((4,))],
        compiler_params=pltpu.CompilerParams(vmem_limit_bytes=1024 * 1024),
    )(*values)
    return (branch[None], grad_inputs[None], qkv_share, out_share)


def solution(mesh):
    return jax.shard_map(
        body,
        mesh=mesh,
        in_specs=(P("dp", "seq", None), P("dp", "seq", None), P(), P(), P(), P(), P()),
        out_specs=(
            P("dp", "seq", None),
            P("dp", "seq", None),
            P(("seq", "dp"), None),
            P(("seq", "dp"), None),
        ),
        check_vma=False,
    )
```

```python
import jax
import jax.numpy as jnp
import numpy as np
from jax import lax
from jax.experimental import pallas as pl
from jax.experimental.pallas import tpu as pltpu
from jax.sharding import PartitionSpec as P

BF = jnp.bfloat16
F32 = jnp.float32
MESH = pl.DeviceIdType.MESH
EPS = 1e-06

NY, NZ, NX = 4, 8, 4
TOK = 128
WIDTH = 768
HEADS = 12
HEAD = 64
GROUP = 4
LANES = GROUP * HEAD
GROUPS = HEADS // GROUP
SPAN = 8
NEAR = TOK // SPAN
FAR = 2
PACK = 32
TILES = WIDTH // 128
OWNERS = 2 * NX
CUT = 512
REST = WIDTH - CUT
QROWS = 3 * WIDTH // NY
OROWS = WIDTH // NY
QOWN, OOWN = QROWS // OWNERS, OROWS // OWNERS
PIECE = QOWN + OOWN
EARLY = 176
LATE = 224


def nn(a, b):
    return lax.dot_general(a, b, (((1,), (0,)), ((), ())), preferred_element_type=F32)


def nt(a, b):
    return lax.dot_general(a, b, (((1,), (1,)), ((), ())), preferred_element_type=F32)


def tn(a, b):
    return lax.dot_general(a, b, (((0,), (0,)), ((), ())), preferred_element_type=F32)


def split(x):
    high = x.astype(BF)
    return high, (x - high.astype(F32)).astype(BF)


def iota(shape, dim):
    return lax.broadcasted_iota(jnp.int32, shape, dim)


def place():
    seq = lax.axis_index("seq")
    return seq, lax.rem(seq, 2), lax.rem(seq // 2, NZ), seq // (2 * NZ)


def at(y, z, core):
    return {"seq": (y * NZ + z) * 2 + core}


def remote(src, dst, send, recv, device):
    return pltpu.make_async_remote_copy(
        src_ref=src, dst_ref=dst, send_sem=send, recv_sem=recv, device_id=device, device_id_type=MESH
    )


def lanes_of(b):
    return slice(b * LANES, (b + 1) * LANES)


def layer(
    scale_ref, near_ref, far_ref, tok_hbm, cot_hbm, wqkv_hbm, wout_hbm,
    block_hbm, compact_hbm, order_hbm, perm_q_hbm, perm_o_hbm, deal_hbm, deal_b_hbm, deal_y_hbm,
    branch_ref, grad_tok_ref, qkv_out, out_out,
    wqkv_ref, wout_ref, block_ref, compact_ref, order_ref, perm_q, perm_o, deal_ref, deal_b_ref, deal_y_ref,
    toks, cots, qkv, qn, kn, gr, inv_q, inv_k, p_loc, p_near, p_far, num, den, dq, dk, dv, dqkv, pack,
    near_kv, near_qg, near_s, far_zkv, far_zqg, far_kv, far_qg, far_sz, far_s,
    attn_t, dqkv_t, stage, corr, chosen, early_out, early_in, late_out, late_in, q_sum, o_sum, b_part,
    a_y_send, a_y_recv, a_z_send, a_z_recv, b_z_send, b_z_recv, b_y_send, b_y_recv,
    loads, sends, r_tok, r_cot, r_ftok, r_fcot, r_nkv, r_nqg, r_ns, r_zkv, r_zqg, r_sz, r_fkv, r_fqg, r_ckv, r_cqg,
    r_fs, r_early, r_late, r_corr, r_ay, r_az, r_bz, r_by,
):
    seq, core, z, y = place()
    x = lax.axis_index("dp")
    mine = lax.rem(seq, SPAN)
    base = seq - mine
    other = 1 - core
    own = core * NX + x

    loading = []

    def load(src, dst):
        copy = pltpu.make_async_copy(src, dst, loads.at[len(loading)])
        copy.start()
        loading.append(copy)

    def load_rows(src, dst, start, stop):
        for first in range(start, stop, LANES):
            load(src.at[first : first + LANES], dst.at[first : first + LANES])

    load(tok_hbm, toks.at[own])
    load(block_hbm, block_ref)
    load_rows(wqkv_hbm, wqkv_ref, WIDTH, 3 * WIDTH)
    load(cot_hbm, cots.at[own])
    load_rows(wqkv_hbm, wqkv_ref, 0, WIDTH)
    load_rows(wout_hbm, wout_ref, 0, WIDTH)

    z_peers = [lax.rem(z + d, NZ) for d in range(1, NZ)]
    y_peers = [lax.rem(y + d, NY) for d in range(1, NY)]
    x_peers = [lax.rem(x + d, NX) for d in range(1, NX)]
    near_peers = [lax.rem(mine + d, SPAN) for d in range(1, SPAN)]
    near_same = [2 * lax.rem(mine // 2 + d, SPAN // 2) + core for d in range(1, SPAN // 2)]
    near_other = [2 * lax.rem(mine // 2 + d, SPAN // 2) + other for d in range(SPAN // 2)]
    partner = at(y, z, other)
    pair = seq - core

    def owner(o):
        return {"seq": pair + o // NX, "dp": lax.rem(o, NX)}

    owners = [lax.rem(own + d, OWNERS) for d in range(1, OWNERS)]
    barrier = pltpu.get_barrier_semaphore()
    greeted = (
        [at(y, t, core) for t in z_peers]
        + [{"seq": base + t} for t in near_other]
        + [at(t, z, core) for t in y_peers]
        + [at(t, z, other) for t in y_peers]
        + [{"seq": seq, "dp": t} for t in x_peers]
        + [{"seq": pair + other, "dp": t} for t in x_peers]
    )
    for device in greeted:
        pl.semaphore_signal(barrier, inc=1, device_id=device, device_id_type=MESH)
    sent = []

    def send(src, dst, recv, device):
        copy = remote(src, dst, sends.at[len(sent)], recv, device)
        copy.start()
        sent.append(copy)

    def arrived(ref, recv):
        remote(ref, ref, sends.at[0], recv, {"seq": seq}).wait_recv()

    head_lane = iota((1, LANES), 1) // HEAD
    picks_f = [(head_lane == h).astype(F32) for h in range(GROUP)]
    picks = [m.astype(BF) for m in picks_f]

    def spread(x):
        return jnp.concatenate([x * m for m in picks], axis=0)

    def fold(x):
        rows = x.shape[0] // GROUP
        return sum(x[h * rows : (h + 1) * rows] * picks_f[h] for h in range(GROUP))

    wide_head = iota((1, WIDTH), 1) // HEAD
    slim_head = iota((1, 128), 1)
    slim_head = jnp.where(slim_head >= HEADS, slim_head - HEADS, slim_head)
    near_row, far_row = jnp.zeros((1, WIDTH), jnp.int32), jnp.zeros((1, WIDTH), jnp.int32)
    near_slim, far_slim = jnp.zeros((1, 128), jnp.int32), jnp.zeros((1, 128), jnp.int32)
    for h in range(HEADS):
        near_row = jnp.where(wide_head == h, near_ref[h], near_row)
        far_row = jnp.where(wide_head == h, far_ref[h], far_row)
        near_slim = jnp.where(slim_head == h, near_ref[h], near_slim)
        far_slim = jnp.where(slim_head == h, far_ref[h], far_slim)
    near_mask = ((iota((TOK, WIDTH), 0) & (SPAN - 1)) == near_row).astype(F32)
    far_mask = ((iota((TOK, WIDTH), 0) & (TOK // FAR - 1)) == far_row).astype(F32)
    near_bf, far_bf = near_mask.astype(BF), far_mask.astype(BF)
    near_slim = ((iota((TOK, 128), 0) & (SPAN - 1)) == near_slim).astype(F32).astype(BF)
    far_slim = ((iota((TOK, 128), 0) & (TOK // FAR - 1)) == far_slim).astype(F32).astype(BF)
    row, token = iota((NEAR, TOK), 0), iota((NEAR, TOK), 1)
    take_near = (token // SPAN == row).astype(F32).astype(BF)
    take_far = (token // (TOK // FAR) == row).astype(F32).astype(BF)
    take_far_z = ((row // FAR == z) & (token // (TOK // FAR) == (row & 1))).astype(F32).astype(BF)

    def unnear(x, b):
        return jnp.broadcast_to(x[:, None, :], (NEAR, SPAN, LANES)).reshape(TOK, LANES) * near_mask[:, lanes_of(b)]

    def unfar(x, b):
        rows = [jnp.broadcast_to(x[i : i + 1], (TOK // FAR, LANES)) for i in range(FAR)]
        return jnp.concatenate(rows, axis=0) * far_mask[:, lanes_of(b)]

    def norms(columns):
        wide = columns.astype(F32)
        high, low = split(wide * wide)
        inverse = lax.rsqrt(nn(high, block_ref[...]) + nn(low, block_ref[...]) + EPS)
        return inverse, wide * inverse

    far_rows = []

    def packed(pair_of):
        pack[2 * FAR * TILES :, :] = jnp.zeros((PACK - 2 * FAR * TILES, 128), F32)
        for i, picked in enumerate(pair_of):
            for r in range(FAR):
                for t in range(TILES):
                    at_row = (i * FAR + r) * TILES + t
                    pack[at_row : at_row + 1, :] = picked[r : r + 1, 128 * t : 128 * (t + 1)]
        return pack[...].astype(BF)

    def leave(pair_of, far_into, near_into):
        picked = [nn(take_far, x_ * far_bf) for x_ in pair_of]
        far_rows.extend(x_.astype(BF) for x_ in picked)
        far_into[z] = packed(picked)
        for i, x_ in enumerate(pair_of):
            near_into[mine, i] = nn(take_near, x_ * near_bf).astype(BF)

    for copy in loading[:2]:
        copy.wait()
    tok = toks[own]
    for b in range(GROUPS, 3 * GROUPS):
        loading[2 + b - GROUPS].wait()
        qkv[:, lanes_of(b)] = nt(tok, wqkv_ref[lanes_of(b), :]).astype(BF)
    for b in range(GROUPS):
        inverse, unit = norms(qkv[:, lanes_of(GROUPS + b)])
        inv_k[:, lanes_of(b)] = inverse
        kn[:, lanes_of(b)] = unit.astype(BF)
    pl.semaphore_wait(barrier, len(greeted))
    leave((kn[...], qkv[:, 2 * WIDTH :]), far_zkv, near_kv)
    for t in z_peers:
        send(far_zkv.at[z], far_zkv.at[z], r_zkv.at[z], at(y, t, core))
    for t in near_same:
        send(near_kv.at[mine], near_kv.at[mine], r_nkv.at[mine], {"seq": base + t})
    send(near_kv.at[mine], near_kv.at[mine], r_nkv.at[mine], partner)

    first = len(loading)
    load(order_hbm, order_ref)
    load(compact_hbm, compact_ref)
    load(perm_q_hbm, perm_q)
    load(perm_o_hbm, perm_o)
    load(deal_hbm, deal_ref)
    load(deal_b_hbm, deal_b_ref)
    load(deal_y_hbm, deal_y_ref)
    for copy in loading[2 + 2 * GROUPS : first]:
        copy.wait()
    cot = cots[own]
    for b in range(GROUPS):
        qkv[:, lanes_of(b)] = nt(tok, wqkv_ref[lanes_of(b), :]).astype(BF)
        gr[:, lanes_of(b)] = nt(cot, wout_ref[lanes_of(b), :]).astype(BF)
        inverse, unit = norms(qkv[:, lanes_of(b)])
        inv_q[:, lanes_of(b)] = inverse
        qn[:, lanes_of(b)] = unit.astype(BF)
    leave((qn[...], gr[...]), far_zqg, near_qg)
    for t in z_peers:
        send(far_zqg.at[z], far_zqg.at[z], r_zqg.at[z], at(y, t, core))
    for all_, recv, forward_recv in ((toks, r_tok, r_ftok), (cots, r_cot, r_fcot)):
        for t in x_peers:
            send(all_.at[own], all_.at[own], recv.at[x], {"seq": seq, "dp": t})
        send(all_.at[own], all_.at[own], forward_recv.at[x], partner)

    ones = spread(jnp.ones((TOK, LANES), BF))
    for b in range(GROUPS):
        s = nt(spread(qn[:, lanes_of(b)]), kn[:, lanes_of(b)])
        ps = []
        for h in range(GROUP):
            p = jnp.exp(s[h * TOK : (h + 1) * TOK] * scale_ref[GROUP * b + h])
            p_loc[(GROUP * b + h) * TOK : (GROUP * b + h + 1) * TOK, :] = p
            ps.append(p.astype(BF))
        ps = jnp.concatenate(ps, axis=1)
        num[:, lanes_of(b)] = nn(ps, spread(qkv[:, lanes_of(2 * GROUPS + b)]))
        den[:, lanes_of(b)] = nn(ps, ones)

    for copy in loading[first:]:
        copy.wait()

    def along_y(packets, recv_z, into, recv):
        for t in z_peers:
            arrived(packets.at[t], recv_z.at[t])
        ordered = nn(order_ref[...], packets[...].reshape(NZ * PACK, 128)).astype(BF)
        for i in range(2):
            for t in range(TILES):
                first = (i * TILES + t) * 16
                into[core, y, i, :, 128 * t : 128 * (t + 1)] = ordered[first : first + 16, :]
        for t in y_peers:
            send(into.at[core, y], into.at[core, y], recv.at[y], at(t, z, core))

    def across(ref, recv):
        for t in near_same:
            arrived(ref.at[t], recv.at[t])
            send(ref.at[t], ref.at[t], recv.at[t], partner)

    def hand_over(ref, recv, recv_core):
        send(ref.at[core, y], ref.at[core, y], recv_core.at[y], partner)
        for t in y_peers:
            arrived(ref.at[core, t], recv.at[t])
            send(ref.at[core, t], ref.at[core, t], recv_core.at[t], partner)

    def forward(queries, keys, values, p_ref):
        results = []
        for b in range(GROUPS):
            s = nt(spread(queries[:, lanes_of(b)]), keys(b))
            ps = []
            for h in range(GROUP):
                ps.append(jnp.exp(s[h * 16 : (h + 1) * 16] * scale_ref[GROUP * b + h]))
            p = jnp.concatenate(ps, axis=0)
            p_ref[b] = p
            total = jnp.broadcast_to(jnp.sum(p, axis=1, keepdims=True), (GROUP * 16, LANES))
            results.append((fold(nn(p.astype(BF), values(b))), fold(total)))
        return results

    def near_rows(ref, i):
        return lambda b: jnp.concatenate([ref[s, i, :, lanes_of(b)] for s in range(SPAN)], axis=0)

    def far_rows_of(ref, i):
        return lambda b: jnp.concatenate(
            [ref[s, t, i, :, lanes_of(b)] for s in range(2) for t in range(NY)], axis=0
        )

    along_y(far_zkv, r_zkv, far_kv, r_fkv)
    across(near_kv, r_nkv)
    for t in near_same:
        send(near_qg.at[mine], near_qg.at[mine], r_nqg.at[mine], {"seq": base + t})
    send(near_qg.at[mine], near_qg.at[mine], r_nqg.at[mine], partner)
    for t in near_other:
        arrived(near_kv.at[t], r_nkv.at[t])
    near_q, near_g = near_qg[mine, 0], near_qg[mine, 1]
    for b, (n_part, d_part) in enumerate(forward(near_q, near_rows(near_kv, 0), near_rows(near_kv, 1), p_near)):
        num[:, lanes_of(b)] += unnear(n_part, b)
        den[:, lanes_of(b)] += unnear(d_part, b)
    hand_over(far_kv, r_fkv, r_ckv)
    for t in range(NY):
        arrived(far_kv.at[other, t], r_ckv.at[t])
    far_k, far_v, far_q, far_g = far_rows
    for b, (n_part, d_part) in enumerate(forward(far_q, far_rows_of(far_kv, 0), far_rows_of(far_kv, 1), p_far)):
        num[:, lanes_of(b)] += unfar(n_part, b)
        den[:, lanes_of(b)] += unfar(d_part, b)

    inverse = 1.0 / den[...]
    attn = (num[...] * inverse).astype(BF)
    high, low = split(inverse)
    slim = nn(high, compact_ref[:, :128]) + nn(low, compact_ref[:, :128])
    high, low = split(gr[...].astype(F32) * attn.astype(F32))
    slim = slim + nn(high, compact_ref[:, 128:]) + nn(low, compact_ref[:, 128:])
    high, low = split(slim)

    def take(selection, mask):
        first, second = nn(selection, high * mask), nn(selection, low * mask)
        return first + second, (first + pltpu.roll(second, 64, 1)).astype(BF)

    def joined(rows):
        columns = rows.astype(F32).reshape(TOK, 128).T
        return columns[:64] + columns[64:]

    far_sz[z] = take(take_far_z, far_slim)[1]
    for t in z_peers:
        send(far_sz.at[z], far_sz.at[z], r_sz.at[z], at(y, t, core))
    near_slim_rows, near_s[mine] = take(take_near, near_slim)
    far_slim_rows = take(take_far, far_slim)[0]
    for t in near_peers:
        send(near_s.at[mine], near_s.at[mine], r_ns.at[mine], {"seq": base + t})
    along_y(far_zqg, r_zqg, far_qg, r_fqg)

    for b in range(GROUPS):
        g = spread(gr[:, lanes_of(b)])
        grad_p = nt(g, qkv[:, lanes_of(2 * GROUPS + b)])
        ps, ds = [], []
        for h in range(GROUP):
            n = GROUP * b + h
            p = p_loc[n * TOK : (n + 1) * TOK, :] * slim[:, n : n + 1]
            d = scale_ref[n] * p * (grad_p[h * TOK : (h + 1) * TOK] - slim[:, HEADS + n : HEADS + n + 1])
            ps.append(p.astype(BF))
            ds.append(d.astype(BF))
        dq[:, lanes_of(b)] = nn(jnp.concatenate(ds, axis=1), spread(kn[:, lanes_of(b)]))
        dk[:, lanes_of(b)] = tn(jnp.concatenate(ds, axis=0), spread(qn[:, lanes_of(b)]))
        dv[:, lanes_of(b)] = tn(jnp.concatenate(ps, axis=0), g)

    def query_side(grads, keys, values, p_ref, slim_rows, b):
        grad_p = nt(spread(grads[:, lanes_of(b)]), values(b))
        ds = []
        for h in range(GROUP):
            n = GROUP * b + h
            p = p_ref[b, h * 16 : (h + 1) * 16, :] * slim_rows[:, n : n + 1]
            ds.append(
                scale_ref[n] * p * (grad_p[h * 16 : (h + 1) * 16] - slim_rows[:, HEADS + n : HEADS + n + 1])
            )
        return fold(nn(jnp.concatenate(ds, axis=0).astype(BF), keys(b)))

    for b in range(GROUPS):
        near_part = query_side(near_g, near_rows(near_kv, 0), near_rows(near_kv, 1), p_near, near_slim_rows, b)
        far_part = query_side(far_g, far_rows_of(far_kv, 0), far_rows_of(far_kv, 1), p_far, far_slim_rows, b)
        dq[:, lanes_of(b)] += unnear(near_part, b) + unfar(far_part, b)

    def through(inverse, unit, d):
        high, low = split(unit * d)
        along = nn(high, block_ref[...]) + nn(low, block_ref[...])
        return inverse * (d - unit * along)

    def unnormalize(inv_ref, grad, i):
        for b in range(GROUPS):
            inverse = inv_ref[:, lanes_of(b)]
            unit = qkv[:, lanes_of(GROUPS * i + b)].astype(F32) * inverse
            dqkv[:, lanes_of(GROUPS * i + b)] = through(inverse, unit, grad[:, lanes_of(b)]).astype(BF)

    unnormalize(inv_q, dq, 0)
    attn_t[...] = attn.T
    dqkv_t[:WIDTH, :] = dqkv[:, :WIDTH].T
    for t in range(NY):
        dealt = nn(perm_o[...], attn_t[t * OROWS : (t + 1) * OROWS, :])
        for o in range(OWNERS):
            stage[o, t * OOWN : (t + 1) * OOWN, :] = dealt[o * OOWN : (o + 1) * OOWN]

    def deal_rows(t, first):
        dealt = nn(perm_q[...], dqkv_t[t * QROWS : (t + 1) * QROWS, :])
        for o in range(OWNERS):
            stage[o, first : first + QOWN, :] = dealt[o * QOWN : (o + 1) * QOWN]

    deal_rows(0, NY * OOWN)
    for o in range(OWNERS):
        stage[o, EARLY - 8 : EARLY, :] = jnp.zeros((8, 128), F32)
    early_out[...] = stage[:, :EARLY, :].astype(BF)
    for o in owners:
        send(early_out.at[o], early_in.at[own], r_early.at[own], owner(o))
    early_in[own] = early_out[own]

    def key_side(keys, values, queries, grads, columns, b):
        q, g = queries(b), grads(b)
        s = nt(spread(keys[:, lanes_of(b)]), q)
        grad_p = nt(spread(values[:, lanes_of(b)]), g)
        ps, ds = [], []
        for h in range(GROUP):
            n = GROUP * b + h
            p = jnp.exp(s[h * 16 : (h + 1) * 16] * scale_ref[n]) * columns[n : n + 1, :]
            ps.append(p)
            ds.append(
                scale_ref[n] * p * (grad_p[h * 16 : (h + 1) * 16] - columns[HEADS + n : HEADS + n + 1, :])
            )
        p, d = jnp.concatenate(ps, axis=0).astype(BF), jnp.concatenate(ds, axis=0).astype(BF)
        return fold(nn(d, q)), fold(nn(p, g))

    across(near_qg, r_nqg)
    for t in near_peers:
        arrived(near_s.at[t], r_ns.at[t])
    for t in near_other:
        arrived(near_qg.at[t], r_nqg.at[t])
    columns = joined(near_s[...])
    near_k, near_v = near_kv[mine, 0], near_kv[mine, 1]
    for b in range(GROUPS):
        k_part, v_part = key_side(near_k, near_v, near_rows(near_qg, 0), near_rows(near_qg, 1), columns, b)
        dk[:, lanes_of(b)] += unnear(k_part, b)
        dv[:, lanes_of(b)] += unnear(v_part, b)

    for t in z_peers:
        arrived(far_sz.at[t], r_sz.at[t])
    far_s[core, y] = jnp.sum(far_sz[...].astype(F32), axis=0).astype(BF)
    for t in y_peers:
        send(far_s.at[core, y], far_s.at[core, y], r_fs.at[core, y], at(t, z, core))
        send(far_s.at[core, y], far_s.at[core, y], r_fs.at[core, y], at(t, z, other))
    send(far_s.at[core, y], far_s.at[core, y], r_fs.at[core, y], partner)

    unnormalize(inv_k, dk, 1)
    dqkv[:, 2 * WIDTH :] = dv[...].astype(BF)
    dqkv_t[WIDTH:, :] = dqkv[:, WIDTH:].T
    for t in range(1, NY):
        deal_rows(t, (t - 1) * QOWN)
    for o in range(OWNERS):
        stage[o, LATE - 8 : LATE, :] = jnp.zeros((8, 128), F32)
    late_out[...] = stage[...].astype(BF)
    for o in owners:
        send(late_out.at[o], late_in.at[own], r_late.at[own], owner(o))
    late_in[own] = late_out[own]

    hand_over(far_qg, r_fqg, r_cqg)
    branch_ref[...] = nn(attn, wout_ref[...]).astype(BF)
    for all_, recv, forward_recv in ((toks, r_tok, r_ftok), (cots, r_cot, r_fcot)):
        for t in x_peers:
            arrived(all_.at[core * NX + t], recv.at[t])
            send(all_.at[core * NX + t], all_.at[core * NX + t], forward_recv.at[t], partner)

    far_inverse, far_unit = [], []
    for b in range(GROUPS):
        high, low = split(inv_k[:, lanes_of(b)])
        mask = far_bf[:, lanes_of(b)]
        inverse = nn(take_far, high * mask) + nn(take_far, low * mask)
        far_inverse.append(inverse)
        far_unit.append(nn(take_far, qkv[:, lanes_of(GROUPS + b)] * mask) * inverse)
    n = iota((LATE, 1), 0)
    t = sum((n >= QOWN * i).astype(jnp.int32) for i in range(1, NY - 1))
    left = n - QOWN * t
    u = sum((left >= QOWN // NZ * i).astype(jnp.int32) for i in range(1, NZ))
    column = QROWS * (1 + t) + (QROWS // NZ) * u + (QOWN // NZ) * own + (left - QOWN // NZ * u) - WIDTH
    column = jnp.where(n < QOWN * (NY - 1), column, -1)
    chosen[...] = (iota((LATE, 2 * WIDTH), 1) == column).astype(F32).astype(BF)
    offsets = jnp.concatenate([far_row, far_row], axis=1).astype(F32).astype(BF)
    offsets = nt(chosen[...], jnp.broadcast_to(offsets, (16, 2 * WIDTH)))[:, :1]
    far_place = ((iota((LATE, 128), 1) & (TOK // FAR - 1)).astype(F32) == offsets).astype(F32)
    far_place = jnp.concatenate([far_place] * OWNERS, axis=1)
    spread_rows = (iota((16, OWNERS * TOK), 1) // (TOK // FAR) == iota((16, OWNERS * TOK), 0)).astype(F32).astype(BF)

    for t in range(NY):
        arrived(far_qg.at[other, t], r_cqg.at[t])
    for t in y_peers:
        arrived(far_s.at[core, t], r_fs.at[core, t])
    for t in range(NY):
        arrived(far_s.at[other, t], r_fs.at[other, t])
    columns = joined(far_s[...])
    k_far, v_far = [], []
    for b in range(GROUPS):
        k_part, v_part = key_side(far_k, far_v, far_rows_of(far_qg, 0), far_rows_of(far_qg, 1), columns, b)
        k_far.append(through(far_inverse[b], far_unit[b], k_part))
        v_far.append(v_part)
    two_rows = [jnp.concatenate(parts, axis=1) for parts in (k_far, v_far)]
    corr[own] = packed(two_rows)
    for o in owners:
        send(corr.at[own], corr.at[own], r_corr.at[own], owner(o))

    for o in owners:
        arrived(early_in.at[o], r_early.at[o])
    for t in range(NX):
        arrived(toks.at[other * NX + t], r_ftok.at[t])
        arrived(cots.at[other * NX + t], r_fcot.at[t])

    def factors(ref, rows):
        return jnp.concatenate([ref[o, rows, :] for o in range(OWNERS)], axis=1)

    o_sum[...] = nn(factors(early_in, slice(0, NY * OOWN)), cots[...].reshape(OWNERS * TOK, WIDTH))
    tokens = toks[...].reshape(OWNERS * TOK, WIDTH)
    q_sum[: EARLY - NY * OOWN, :] = nn(factors(early_in, slice(NY * OOWN, EARLY)), tokens)

    for o in owners:
        arrived(late_in.at[o], r_late.at[o])
    for o in owners:
        arrived(corr.at[o], r_corr.at[o])
    ordered = nn(order_ref[...], corr[...].reshape(OWNERS * PACK, 128)).astype(BF)
    ordered = jnp.concatenate([ordered[16 * t : 16 * (t + 1)] for t in range(2 * TILES)], axis=1)
    added = nn(nt(chosen[...], ordered).astype(BF), spread_rows) * far_place
    late = nn((factors(late_in, slice(0, LATE)).astype(F32) + added).astype(BF), tokens)
    q_sum[QOWN:, :] = late[: (NY - 1) * QOWN]

    left, right = slice(0, CUT), slice(CUT, WIDTH)
    for t in range(NY):
        yz_part = jnp.concatenate(
            [q_sum[t * QOWN : (t + 1) * QOWN, :], o_sum[t * OOWN : (t + 1) * OOWN, :]], axis=0
        ).astype(BF)
        a_y_send[t] = yz_part[:, left]
        b_part[t * PIECE : (t + 1) * PIECE, :] = yz_part[:, right]
    for t in y_peers:
        send(a_y_send.at[t], a_y_recv.at[y], r_ay.at[y], at(t, z, core))
    a_y_recv[y] = a_y_send[y]
    dealt = nn(deal_b_ref[...], b_part[...]).astype(BF)
    for t in range(NZ):
        b_z_send[t] = dealt[48 * t : 48 * (t + 1), :]
    for t in z_peers:
        send(b_z_send.at[t], b_z_recv.at[z], r_bz.at[z], at(y, t, core))
    b_z_recv[z] = b_z_send[z]

    for i, rows in enumerate(two_rows):
        for b in range(GROUPS):
            at_lanes = lanes_of(GROUPS * (1 + i) + b)
            dqkv[:, at_lanes] = (dqkv[:, at_lanes].astype(F32) + unfar(rows[:, lanes_of(b)], b)).astype(BF)
    grad_tok_ref[...] = nn(dqkv[...], wqkv_ref[...]).astype(BF)

    for t in y_peers:
        arrived(a_y_recv.at[t], r_ay.at[t])
    part = jnp.sum(a_y_recv[...].astype(F32), axis=0)
    dealt = nn(deal_ref[...], part.astype(BF)).astype(BF)
    for t in range(NZ):
        a_z_send[t] = dealt[16 * t : 16 * (t + 1), :]
    for t in z_peers:
        send(a_z_send.at[t], a_z_recv.at[z], r_az.at[z], at(y, t, core))
    a_z_recv[z] = a_z_send[z]
    for t in z_peers:
        arrived(b_z_recv.at[t], r_bz.at[t])
    part = jnp.sum(b_z_recv[...].astype(F32), axis=0)
    dealt = nn(deal_y_ref[...], part.astype(BF)).astype(BF)
    for t in range(NY):
        b_y_send[t] = dealt[16 * t : 16 * (t + 1), :]
    for t in y_peers:
        send(b_y_send.at[t], b_y_recv.at[y], r_by.at[y], at(t, z, core))
    b_y_recv[y] = b_y_send[y]
    for columns, ref, recv, peers in ((left, a_z_recv, r_az, z_peers), (right, b_y_recv, r_by, y_peers)):
        for t in peers:
            arrived(ref.at[t], recv.at[t])
        share = jnp.sum(ref[...].astype(F32), axis=0)
        qkv_out[:, columns] = share[: QOWN // NZ]
        out_out[:, columns] = share[QOWN // NZ : PIECE // NZ]
    for copy in sent:
        copy.wait_send()


def finish(*refs):
    sources, results, held, sems = refs[:4], refs[4:8], refs[8:12], refs[12]
    inward = [pltpu.make_async_copy(sources[n], held[n], sems.at[0, n]) for n in range(4)]
    outward = [pltpu.make_async_copy(held[n], results[n], sems.at[1, n]) for n in range(4)]
    for copy in inward:
        copy.start()
    for come, go in zip(inward, outward):
        come.wait()
        go.start()
    for copy in outward:
        copy.wait()


def constants():
    lane = np.arange(WIDTH)
    block = (lane[:LANES, None] // HEAD == lane[None, :LANES] // HEAD).astype(np.float32)
    compact = np.zeros((WIDTH, 256), np.float32)
    compact[np.arange(HEADS) * HEAD, np.arange(HEADS)] = 1
    compact[lane, 128 + HEADS + lane // HEAD] = 1
    order = np.zeros((2 * TILES * 16, NZ * PACK), np.float32)
    for t in range(2):
        for j in range(TILES):
            for s in range(NZ):
                for i in range(FAR):
                    order[(t * TILES + j) * 16 + s * FAR + i, s * PACK + (t * FAR + i) * TILES + j] = 1

    def deal_out(each):
        index = np.arange(NZ * OWNERS * each).reshape(NZ, OWNERS, each).transpose(1, 0, 2).reshape(-1)
        return np.eye(index.size, dtype=np.float32)[index]

    deal = np.zeros((NZ * 16, PIECE), np.float32)
    for t in range(NZ):
        for i in range(9):
            deal[t * 16 + i, t * 9 + i] = 1
        for i in range(3):
            deal[t * 16 + 9 + i, QOWN + t * 3 + i] = 1
    deal_b = np.zeros((NZ * 48, NY * PIECE), np.float32)
    deal_y = np.zeros((NY * 16, 48), np.float32)
    for s in range(NY):
        for i in range(12):
            deal_y[s * 16 + i, s * 12 + i] = 1
            for t in range(NZ):
                deal_b[t * 48 + s * 12 + i, s * PIECE + (t * 9 + i if i < 9 else QOWN + t * 3 + i - 9)] = 1
    return [jnp.asarray(m, BF) for m in (block, compact, order, deal_out(9), deal_out(3), deal, deal_b, deal_y)]


def body(tokens, cotangent, qkv_weight, out_weight, logit_scale, near_offsets, far_offsets):
    fixed = constants()
    smem = pl.BlockSpec(memory_space=pltpu.SMEM)
    hbm = pl.BlockSpec(memory_space=pltpu.HBM)
    vmem = pl.BlockSpec(memory_space=pltpu.VMEM)
    dma = pltpu.SemaphoreType.DMA
    wide_bf = pltpu.VMEM((TOK, WIDTH), BF)
    wide = pltpu.VMEM((TOK, WIDTH), F32)

    def held(*shape):
        return pltpu.VMEM(shape, BF)

    def held_f32(*shape):
        return pltpu.VMEM(shape, F32)

    results = [
        jax.ShapeDtypeStruct((TOK, WIDTH), BF),
        jax.ShapeDtypeStruct((TOK, WIDTH), BF),
        jax.ShapeDtypeStruct((9, WIDTH), F32),
        jax.ShapeDtypeStruct((3, WIDTH), F32),
    ]
    values = pl.pallas_call(
        layer,
        out_shape=results,
        in_specs=[smem] * 3 + [hbm] * (4 + len(fixed)),
        out_specs=[vmem] * 4,
        scratch_shapes=[
            held(3 * WIDTH, WIDTH), held(WIDTH, WIDTH), *[held(*m.shape) for m in fixed],
            held(OWNERS, TOK, WIDTH), held(OWNERS, TOK, WIDTH),
            held(TOK, 3 * WIDTH), wide_bf, wide_bf, wide_bf, wide, wide,
            held_f32(HEADS * TOK, 128), held_f32(GROUPS, GROUP * 16, 128), held_f32(GROUPS, GROUP * 16, 128),
            wide, wide, wide, wide, wide, held(TOK, 3 * WIDTH), held_f32(PACK, 128),
            held(SPAN, 2, NEAR, WIDTH), held(SPAN, 2, NEAR, WIDTH), held(SPAN, NEAR, 128),
            held(NZ, PACK, 128), held(NZ, PACK, 128),
            held(2, NY, 2, 16, WIDTH), held(2, NY, 2, 16, WIDTH), held(NZ, 16, 128), held(2, NY, 16, 128),
            held(WIDTH, TOK), held(3 * WIDTH, TOK), held_f32(OWNERS, LATE, 128),
            held(OWNERS, PACK, 128), held(LATE, 2 * WIDTH),
            held(OWNERS, EARLY, 128), held(OWNERS, EARLY, 128), held(OWNERS, LATE, 128), held(OWNERS, LATE, 128),
            held_f32(NY * QOWN, WIDTH), held_f32(NY * OOWN, WIDTH),
            held(NY * PIECE, REST),
            held(NY, PIECE, CUT), held(NY, PIECE, CUT), held(NZ, 16, CUT), held(NZ, 16, CUT),
            held(NZ, 48, REST), held(NZ, 48, REST), held(NY, 16, REST), held(NY, 16, REST),
            dma((24,)), dma((128,)),
            dma((4,)), dma((4,)), dma((4,)), dma((4,)),
            dma((8,)), dma((8,)), dma((8,)), dma((8,)), dma((8,)), dma((8,)), dma((4,)), dma((4,)), dma((4,)), dma((4,)),
            dma((2, 4)), dma((8,)), dma((8,)), dma((8,)), dma((4,)), dma((8,)), dma((8,)), dma((4,)),
        ],
        compiler_params=pltpu.CompilerParams(
            collective_id=0, has_side_effects=True, vmem_limit_bytes=56 * 1024 * 1024
        ),
    )(logit_scale, near_offsets, far_offsets, tokens[0], cotangent[0], qkv_weight, out_weight, *fixed)
    branch, grad_inputs, qkv_share, out_share = pl.pallas_call(
        finish,
        out_shape=results,
        in_specs=[pl.BlockSpec(memory_space=pl.ANY)] * 4,
        out_specs=[pl.BlockSpec(memory_space=pl.ANY)] * 4,
        scratch_shapes=[pltpu.VMEM(r.shape, r.dtype) for r in results] + [dma((2, 4))],
        compiler_params=pltpu.CompilerParams(vmem_limit_bytes=56 * 1024 * 1024),
    )(*values)
    return (branch[None], grad_inputs[None], qkv_share, out_share)


def solution(mesh):
    return jax.shard_map(
        body,
        mesh=mesh,
        in_specs=(P("dp", "seq", None), P("dp", "seq", None), P(), P(), P(), P(), P()),
        out_specs=(
            P("dp", "seq", None),
            P("dp", "seq", None),
            P(("seq", "dp"), None),
            P(("seq", "dp"), None),
        ),
        check_vma=False,
    )
```

```python
import jax
import jax.numpy as jnp
import numpy as np
from jax import lax
from jax.experimental import pallas as pl
from jax.experimental.pallas import tpu as pltpu
from jax.sharding import PartitionSpec as P

BF = jnp.bfloat16
F32 = jnp.float32
MESH = pl.DeviceIdType.MESH
EPS = 1e-06

NY, NZ, NX = 4, 8, 4
TOK = 128
WIDTH = 768
HEADS = 12
HEAD = 64
GROUP = 4
LANES = GROUP * HEAD
GROUPS = HEADS // GROUP
SPAN = 8
NEAR = TOK // SPAN
FAR = 2
PACK = 32
TILES = WIDTH // 128
OWNERS = 2 * NX
CUT = 512
REST = WIDTH - CUT
QROWS = 3 * WIDTH // NY
OROWS = WIDTH // NY
QOWN, OOWN = QROWS // OWNERS, OROWS // OWNERS
PIECE = QOWN + OOWN
EARLY = 176
LATE = 224


def nn(a, b):
    return lax.dot_general(a, b, (((1,), (0,)), ((), ())), preferred_element_type=F32)


def nt(a, b):
    return lax.dot_general(a, b, (((1,), (1,)), ((), ())), preferred_element_type=F32)


def tn(a, b):
    return lax.dot_general(a, b, (((0,), (0,)), ((), ())), preferred_element_type=F32)


def split(x):
    high = x.astype(BF)
    return high, (x - high.astype(F32)).astype(BF)


def iota(shape, dim):
    return lax.broadcasted_iota(jnp.int32, shape, dim)


def place():
    seq = lax.axis_index("seq")
    return seq, lax.rem(seq, 2), lax.rem(seq // 2, NZ), seq // (2 * NZ)


def at(y, z, core):
    return {"seq": (y * NZ + z) * 2 + core}


def remote(src, dst, send, recv, device):
    return pltpu.make_async_remote_copy(
        src_ref=src, dst_ref=dst, send_sem=send, recv_sem=recv, device_id=device, device_id_type=MESH
    )


def lanes_of(b):
    return slice(b * LANES, (b + 1) * LANES)


def layer(
    scale_hbm, near_hbm, far_hbm, tok_hbm, cot_hbm, wqkv_hbm, wout_hbm,
    block_hbm, compact_hbm, order_hbm, perm_q_hbm, perm_o_hbm, deal_hbm, deal_b_hbm, deal_y_hbm,
    branch_ref, grad_tok_ref, qkv_out, out_out,
    scale_ref, near_ref, far_ref, wqkv_ref, wout_ref, block_ref, compact_ref, order_ref, perm_q, perm_o, deal_ref, deal_b_ref, deal_y_ref,
    toks, cots, qkv, qn, kn, gr, inv_q, inv_k, p_loc, p_near, p_far, num, den, dq, dk, dv, dqkv, pack,
    near_kv, near_qg, near_s, far_zkv, far_zqg, far_kv, far_qg, far_sz, far_s,
    attn_t, dqkv_t, stage, corr, chosen, early_out, early_in, late_out, late_in, q_sum, o_sum, b_part,
    a_y_send, a_y_recv, a_z_send, a_z_recv, b_z_send, b_z_recv, b_y_send, b_y_recv,
    loads, sends, r_tok, r_cot, r_ftok, r_fcot, r_nkv, r_nqg, r_ns, r_zkv, r_zqg, r_sz, r_fkv, r_fqg, r_ckv, r_cqg,
    r_fs, r_early, r_late, r_corr, r_ay, r_az, r_bz, r_by,
):
    seq, core, z, y = place()
    x = lax.axis_index("dp")
    mine = lax.rem(seq, SPAN)
    base = seq - mine
    other = 1 - core
    own = core * NX + x

    loading = []

    def load(src, dst):
        copy = pltpu.make_async_copy(src, dst, loads.at[len(loading)])
        copy.start()
        loading.append(copy)

    load(near_hbm, near_ref)
    load(far_hbm, far_ref)
    load(scale_hbm, scale_ref)
    load(tok_hbm, toks.at[own])
    load(block_hbm, block_ref)
    load(wqkv_hbm.at[WIDTH : 3 * WIDTH], wqkv_ref.at[WIDTH : 3 * WIDTH])
    load(cot_hbm, cots.at[own])
    load(wqkv_hbm.at[:WIDTH], wqkv_ref.at[:WIDTH])
    load(wout_hbm, wout_ref)

    z_peers = [lax.rem(z + d, NZ) for d in (4, 3, 5, 2, 6, 1, 7)]
    y_peers = [lax.rem(y + d, NY) for d in (2, 1, 3)]
    x_peers = [lax.rem(x + d, NX) for d in (2, 1, 3)]
    near_peers = [lax.rem(mine + d, SPAN) for d in range(1, SPAN)]
    near_same = [2 * lax.rem(mine // 2 + d, SPAN // 2) + core for d in (2, 1, 3)]
    near_other = [2 * lax.rem(mine // 2 + d, SPAN // 2) + other for d in range(SPAN // 2)]
    partner = at(y, z, other)
    pair = seq - core

    def owner(o):
        return {"seq": pair + o // NX, "dp": lax.rem(o, NX)}

    owners = [lax.rem(own + d, OWNERS) for d in (2, 6, 1, 3, 5, 7, 4)]
    barrier = pltpu.get_barrier_semaphore()
    greeted = (
        [at(y, t, core) for t in z_peers]
        + [{"seq": base + t} for t in near_other]
        + [at(t, z, core) for t in y_peers]
        + [at(t, z, other) for t in y_peers]
        + [{"seq": seq, "dp": t} for t in x_peers]
        + [{"seq": pair + other, "dp": t} for t in x_peers]
    )
    for device in greeted:
        pl.semaphore_signal(barrier, inc=1, device_id=device, device_id_type=MESH)
    sent = []

    def send(src, dst, recv, device):
        copy = remote(src, dst, sends.at[len(sent)], recv, device)
        copy.start()
        sent.append(copy)

    def arrived(ref, recv):
        remote(ref, ref, sends.at[0], recv, {"seq": seq}).wait_recv()

    head_lane = iota((1, LANES), 1) // HEAD
    picks_f = [(head_lane == h).astype(F32) for h in range(GROUP)]
    picks = [m.astype(BF) for m in picks_f]

    def spread(x):
        return jnp.concatenate([x * m for m in picks], axis=0)

    def fold(x):
        rows = x.shape[0] // GROUP
        return sum(x[h * rows : (h + 1) * rows] * picks_f[h] for h in range(GROUP))

    for copy in loading[:3]:
        copy.wait()
    wide_head = iota((1, WIDTH), 1) // HEAD
    slim_head = iota((1, 128), 1)
    slim_head = jnp.where(slim_head >= HEADS, slim_head - HEADS, slim_head)
    near_row, far_row = jnp.zeros((1, WIDTH), jnp.int32), jnp.zeros((1, WIDTH), jnp.int32)
    near_slim, far_slim = jnp.zeros((1, 128), jnp.int32), jnp.zeros((1, 128), jnp.int32)
    for h in range(HEADS):
        near_row = jnp.where(wide_head == h, near_ref[h], near_row)
        far_row = jnp.where(wide_head == h, far_ref[h], far_row)
        near_slim = jnp.where(slim_head == h, near_ref[h], near_slim)
        far_slim = jnp.where(slim_head == h, far_ref[h], far_slim)
    near_mask = ((iota((TOK, WIDTH), 0) & (SPAN - 1)) == near_row).astype(F32)
    far_mask = ((iota((TOK, WIDTH), 0) & (TOK // FAR - 1)) == far_row).astype(F32)
    near_bf, far_bf = near_mask.astype(BF), far_mask.astype(BF)
    near_slim = ((iota((TOK, 128), 0) & (SPAN - 1)) == near_slim).astype(F32).astype(BF)
    far_slim = ((iota((TOK, 128), 0) & (TOK // FAR - 1)) == far_slim).astype(F32).astype(BF)
    row, token = iota((NEAR, TOK), 0), iota((NEAR, TOK), 1)
    take_near = (token // SPAN == row).astype(F32).astype(BF)
    take_far = (token // (TOK // FAR) == row).astype(F32).astype(BF)
    take_far_z = ((row // FAR == z) & (token // (TOK // FAR) == (row & 1))).astype(F32).astype(BF)

    def unnear(x, b):
        return jnp.broadcast_to(x[:, None, :], (NEAR, SPAN, LANES)).reshape(TOK, LANES) * near_mask[:, lanes_of(b)]

    def unfar(x, b):
        rows = [jnp.broadcast_to(x[i : i + 1], (TOK // FAR, LANES)) for i in range(FAR)]
        return jnp.concatenate(rows, axis=0) * far_mask[:, lanes_of(b)]

    def norms(columns):
        wide = columns.astype(F32)
        high, low = split(wide * wide)
        inverse = lax.rsqrt(nn(high, block_ref[...]) + nn(low, block_ref[...]) + EPS)
        return inverse, wide * inverse

    far_rows = []

    def packed(pair_of):
        pack[2 * FAR * TILES :, :] = jnp.zeros((PACK - 2 * FAR * TILES, 128), F32)
        for i, picked in enumerate(pair_of):
            for r in range(FAR):
                for t in range(TILES):
                    at_row = (i * FAR + r) * TILES + t
                    pack[at_row : at_row + 1, :] = picked[r : r + 1, 128 * t : 128 * (t + 1)]
        return pack[...].astype(BF)

    def leave(pair_of, far_into, near_into):
        picked = [nn(take_far, x_ * far_bf) for x_ in pair_of]
        far_rows.extend(x_.astype(BF) for x_ in picked)
        far_into[z] = packed(picked)
        for i, x_ in enumerate(pair_of):
            near_into[mine, i] = nn(take_near, x_ * near_bf).astype(BF)

    for copy in loading[3:6]:
        copy.wait()
    tok = toks[own]
    for b in range(GROUPS, 3 * GROUPS):
        qkv[:, lanes_of(b)] = nt(tok, wqkv_ref[lanes_of(b), :]).astype(BF)
    for b in range(GROUPS):
        inverse, unit = norms(qkv[:, lanes_of(GROUPS + b)])
        inv_k[:, lanes_of(b)] = inverse
        kn[:, lanes_of(b)] = unit.astype(BF)
    pl.semaphore_wait(barrier, len(greeted))
    leave((kn[...], qkv[:, 2 * WIDTH :]), far_zkv, near_kv)
    for t in z_peers:
        send(far_zkv.at[z], far_zkv.at[z], r_zkv.at[z], at(y, t, core))
    for t in near_same:
        send(near_kv.at[mine], near_kv.at[mine], r_nkv.at[mine], {"seq": base + t})
    send(near_kv.at[mine], near_kv.at[mine], r_nkv.at[mine], partner)

    first = len(loading)
    load(order_hbm, order_ref)
    load(compact_hbm, compact_ref)
    load(perm_q_hbm, perm_q)
    load(perm_o_hbm, perm_o)
    load(deal_hbm, deal_ref)
    load(deal_b_hbm, deal_b_ref)
    load(deal_y_hbm, deal_y_ref)
    for copy in loading[6:first]:
        copy.wait()
    cot = cots[own]
    for b in range(GROUPS):
        qkv[:, lanes_of(b)] = nt(tok, wqkv_ref[lanes_of(b), :]).astype(BF)
        gr[:, lanes_of(b)] = nt(cot, wout_ref[lanes_of(b), :]).astype(BF)
        inverse, unit = norms(qkv[:, lanes_of(b)])
        inv_q[:, lanes_of(b)] = inverse
        qn[:, lanes_of(b)] = unit.astype(BF)
    leave((qn[...], gr[...]), far_zqg, near_qg)
    for t in z_peers:
        send(far_zqg.at[z], far_zqg.at[z], r_zqg.at[z], at(y, t, core))
    for all_, recv, forward_recv in ((toks, r_tok, r_ftok), (cots, r_cot, r_fcot)):
        for t in x_peers:
            send(all_.at[own], all_.at[own], recv.at[x], {"seq": seq, "dp": t})
        send(all_.at[own], all_.at[own], forward_recv.at[x], partner)

    ones = spread(jnp.ones((TOK, LANES), BF))
    for b in range(GROUPS):
        s = nt(spread(qn[:, lanes_of(b)]), kn[:, lanes_of(b)])
        ps = []
        for h in range(GROUP):
            p = jnp.exp(s[h * TOK : (h + 1) * TOK] * scale_ref[GROUP * b + h])
            p_loc[(GROUP * b + h) * TOK : (GROUP * b + h + 1) * TOK, :] = p
            ps.append(p.astype(BF))
        ps = jnp.concatenate(ps, axis=1)
        num[:, lanes_of(b)] = nn(ps, spread(qkv[:, lanes_of(2 * GROUPS + b)]))
        den[:, lanes_of(b)] = nn(ps, ones)

    for copy in loading[first:]:
        copy.wait()

    def along_y(packets, recv_z, into, recv):
        for t in z_peers:
            arrived(packets.at[t], recv_z.at[t])
        ordered = nn(order_ref[...], packets[...].reshape(NZ * PACK, 128)).astype(BF)
        for i in range(2):
            for t in range(TILES):
                first = (i * TILES + t) * 16
                into[core, y, i, :, 128 * t : 128 * (t + 1)] = ordered[first : first + 16, :]
        for t in y_peers:
            send(into.at[core, y], into.at[core, y], recv.at[y], at(t, z, core))

    def across(ref, recv):
        for t in near_same:
            arrived(ref.at[t], recv.at[t])
            send(ref.at[t], ref.at[t], recv.at[t], partner)

    def hand_over(ref, recv, recv_core):
        send(ref.at[core, y], ref.at[core, y], recv_core.at[y], partner)
        for t in y_peers:
            arrived(ref.at[core, t], recv.at[t])
            send(ref.at[core, t], ref.at[core, t], recv_core.at[t], partner)

    def forward(queries, keys, values, p_ref):
        results = []
        for b in range(GROUPS):
            s = nt(spread(queries[:, lanes_of(b)]), keys(b))
            ps = []
            for h in range(GROUP):
                ps.append(jnp.exp(s[h * 16 : (h + 1) * 16] * scale_ref[GROUP * b + h]))
            p = jnp.concatenate(ps, axis=0)
            p_ref[b] = p
            total = jnp.broadcast_to(jnp.sum(p, axis=1, keepdims=True), (GROUP * 16, LANES))
            results.append((fold(nn(p.astype(BF), values(b))), fold(total)))
        return results

    def near_rows(ref, i):
        return lambda b: jnp.concatenate([ref[s, i, :, lanes_of(b)] for s in range(SPAN)], axis=0)

    def far_rows_of(ref, i):
        return lambda b: jnp.concatenate(
            [ref[s, t, i, :, lanes_of(b)] for s in range(2) for t in range(NY)], axis=0
        )

    along_y(far_zkv, r_zkv, far_kv, r_fkv)
    across(near_kv, r_nkv)
    for t in near_same:
        send(near_qg.at[mine], near_qg.at[mine], r_nqg.at[mine], {"seq": base + t})
    send(near_qg.at[mine], near_qg.at[mine], r_nqg.at[mine], partner)
    for t in near_other:
        arrived(near_kv.at[t], r_nkv.at[t])
    near_q, near_g = near_qg[mine, 0], near_qg[mine, 1]
    for b, (n_part, d_part) in enumerate(forward(near_q, near_rows(near_kv, 0), near_rows(near_kv, 1), p_near)):
        num[:, lanes_of(b)] += unnear(n_part, b)
        den[:, lanes_of(b)] += unnear(d_part, b)
    hand_over(far_kv, r_fkv, r_ckv)
    for t in range(NY):
        arrived(far_kv.at[other, t], r_ckv.at[t])
    far_k, far_v, far_q, far_g = far_rows
    for b, (n_part, d_part) in enumerate(forward(far_q, far_rows_of(far_kv, 0), far_rows_of(far_kv, 1), p_far)):
        num[:, lanes_of(b)] += unfar(n_part, b)
        den[:, lanes_of(b)] += unfar(d_part, b)

    inverse = 1.0 / den[...]
    attn = (num[...] * inverse).astype(BF)
    high, low = split(inverse)
    slim = nn(high, compact_ref[:, :128]) + nn(low, compact_ref[:, :128])
    high, low = split(gr[...].astype(F32) * attn.astype(F32))
    slim = slim + nn(high, compact_ref[:, 128:]) + nn(low, compact_ref[:, 128:])
    high, low = split(slim)

    def take(selection, mask):
        first, second = nn(selection, high * mask), nn(selection, low * mask)
        return first + second, (first + pltpu.roll(second, 64, 1)).astype(BF)

    def joined(rows):
        columns = rows.astype(F32).reshape(TOK, 128).T
        return columns[:64] + columns[64:]

    far_sz[z] = take(take_far_z, far_slim)[1]
    for t in z_peers:
        send(far_sz.at[z], far_sz.at[z], r_sz.at[z], at(y, t, core))
    near_slim_rows, near_s[mine] = take(take_near, near_slim)
    far_slim_rows = take(take_far, far_slim)[0]
    for t in near_peers:
        send(near_s.at[mine], near_s.at[mine], r_ns.at[mine], {"seq": base + t})
    along_y(far_zqg, r_zqg, far_qg, r_fqg)

    for b in range(GROUPS):
        g = spread(gr[:, lanes_of(b)])
        grad_p = nt(g, qkv[:, lanes_of(2 * GROUPS + b)])
        ps, ds = [], []
        for h in range(GROUP):
            n = GROUP * b + h
            p = p_loc[n * TOK : (n + 1) * TOK, :] * slim[:, n : n + 1]
            d = scale_ref[n] * p * (grad_p[h * TOK : (h + 1) * TOK] - slim[:, HEADS + n : HEADS + n + 1])
            ps.append(p.astype(BF))
            ds.append(d.astype(BF))
        dq[:, lanes_of(b)] = nn(jnp.concatenate(ds, axis=1), spread(kn[:, lanes_of(b)]))
        dk[:, lanes_of(b)] = tn(jnp.concatenate(ds, axis=0), spread(qn[:, lanes_of(b)]))
        dv[:, lanes_of(b)] = tn(jnp.concatenate(ps, axis=0), g)

    def query_side(grads, keys, values, p_ref, slim_rows, b):
        grad_p = nt(spread(grads[:, lanes_of(b)]), values(b))
        ds = []
        for h in range(GROUP):
            n = GROUP * b + h
            p = p_ref[b, h * 16 : (h + 1) * 16, :] * slim_rows[:, n : n + 1]
            ds.append(
                scale_ref[n] * p * (grad_p[h * 16 : (h + 1) * 16] - slim_rows[:, HEADS + n : HEADS + n + 1])
            )
        return fold(nn(jnp.concatenate(ds, axis=0).astype(BF), keys(b)))

    for b in range(GROUPS):
        near_part = query_side(near_g, near_rows(near_kv, 0), near_rows(near_kv, 1), p_near, near_slim_rows, b)
        far_part = query_side(far_g, far_rows_of(far_kv, 0), far_rows_of(far_kv, 1), p_far, far_slim_rows, b)
        dq[:, lanes_of(b)] += unnear(near_part, b) + unfar(far_part, b)

    def through(inverse, unit, d):
        high, low = split(unit * d)
        along = nn(high, block_ref[...]) + nn(low, block_ref[...])
        return inverse * (d - unit * along)

    def unnormalize(inv_ref, grad, i):
        for b in range(GROUPS):
            inverse = inv_ref[:, lanes_of(b)]
            unit = qkv[:, lanes_of(GROUPS * i + b)].astype(F32) * inverse
            dqkv[:, lanes_of(GROUPS * i + b)] = through(inverse, unit, grad[:, lanes_of(b)]).astype(BF)

    unnormalize(inv_q, dq, 0)
    attn_t[...] = attn.T
    dqkv_t[:WIDTH, :] = dqkv[:, :WIDTH].T
    for t in range(NY):
        dealt = nn(perm_o[...], attn_t[t * OROWS : (t + 1) * OROWS, :])
        for o in range(OWNERS):
            stage[o, t * OOWN : (t + 1) * OOWN, :] = dealt[o * OOWN : (o + 1) * OOWN]

    def deal_rows(t, first):
        dealt = nn(perm_q[...], dqkv_t[t * QROWS : (t + 1) * QROWS, :])
        for o in range(OWNERS):
            stage[o, first : first + QOWN, :] = dealt[o * QOWN : (o + 1) * QOWN]

    deal_rows(0, NY * OOWN)
    for o in range(OWNERS):
        stage[o, EARLY - 8 : EARLY, :] = jnp.zeros((8, 128), F32)
    early_out[...] = stage[:, :EARLY, :].astype(BF)
    for o in owners:
        send(early_out.at[o], early_in.at[own], r_early.at[own], owner(o))
    early_in[own] = early_out[own]

    def key_side(keys, values, queries, grads, columns, b):
        q, g = queries(b), grads(b)
        s = nt(spread(keys[:, lanes_of(b)]), q)
        grad_p = nt(spread(values[:, lanes_of(b)]), g)
        ps, ds = [], []
        for h in range(GROUP):
            n = GROUP * b + h
            p = jnp.exp(s[h * 16 : (h + 1) * 16] * scale_ref[n]) * columns[n : n + 1, :]
            ps.append(p)
            ds.append(
                scale_ref[n] * p * (grad_p[h * 16 : (h + 1) * 16] - columns[HEADS + n : HEADS + n + 1, :])
            )
        p, d = jnp.concatenate(ps, axis=0).astype(BF), jnp.concatenate(ds, axis=0).astype(BF)
        return fold(nn(d, q)), fold(nn(p, g))

    across(near_qg, r_nqg)
    for t in near_peers:
        arrived(near_s.at[t], r_ns.at[t])
    for t in near_other:
        arrived(near_qg.at[t], r_nqg.at[t])
    columns = joined(near_s[...])
    near_k, near_v = near_kv[mine, 0], near_kv[mine, 1]
    for b in range(GROUPS):
        k_part, v_part = key_side(near_k, near_v, near_rows(near_qg, 0), near_rows(near_qg, 1), columns, b)
        dk[:, lanes_of(b)] += unnear(k_part, b)
        dv[:, lanes_of(b)] += unnear(v_part, b)

    for t in z_peers:
        arrived(far_sz.at[t], r_sz.at[t])
    far_s[core, y] = jnp.sum(far_sz[...].astype(F32), axis=0).astype(BF)
    for t in y_peers:
        send(far_s.at[core, y], far_s.at[core, y], r_fs.at[core, y], at(t, z, core))
        send(far_s.at[core, y], far_s.at[core, y], r_fs.at[core, y], at(t, z, other))
    send(far_s.at[core, y], far_s.at[core, y], r_fs.at[core, y], partner)

    unnormalize(inv_k, dk, 1)
    dqkv[:, 2 * WIDTH :] = dv[...].astype(BF)
    dqkv_t[WIDTH:, :] = dqkv[:, WIDTH:].T
    for t in range(1, NY):
        deal_rows(t, (t - 1) * QOWN)
    for o in range(OWNERS):
        stage[o, LATE - 8 : LATE, :] = jnp.zeros((8, 128), F32)
    late_out[...] = stage[...].astype(BF)
    for o in owners:
        send(late_out.at[o], late_in.at[own], r_late.at[own], owner(o))
    late_in[own] = late_out[own]

    hand_over(far_qg, r_fqg, r_cqg)
    branch_ref[...] = nn(attn, wout_ref[...]).astype(BF)
    for all_, recv, forward_recv in ((toks, r_tok, r_ftok), (cots, r_cot, r_fcot)):
        for t in x_peers:
            arrived(all_.at[core * NX + t], recv.at[t])
            send(all_.at[core * NX + t], all_.at[core * NX + t], forward_recv.at[t], partner)

    far_inverse, far_unit = [], []
    for b in range(GROUPS):
        high, low = split(inv_k[:, lanes_of(b)])
        mask = far_bf[:, lanes_of(b)]
        inverse = nn(take_far, high * mask) + nn(take_far, low * mask)
        far_inverse.append(inverse)
        far_unit.append(nn(take_far, qkv[:, lanes_of(GROUPS + b)] * mask) * inverse)
    n = iota((LATE, 1), 0)
    t = sum((n >= QOWN * i).astype(jnp.int32) for i in range(1, NY - 1))
    left = n - QOWN * t
    u = sum((left >= QOWN // NZ * i).astype(jnp.int32) for i in range(1, NZ))
    column = QROWS * (1 + t) + (QROWS // NZ) * u + (QOWN // NZ) * own + (left - QOWN // NZ * u) - WIDTH
    column = jnp.where(n < QOWN * (NY - 1), column, -1)
    chosen[...] = (iota((LATE, 2 * WIDTH), 1) == column).astype(F32).astype(BF)
    offsets = jnp.concatenate([far_row, far_row], axis=1).astype(F32).astype(BF)
    offsets = nt(chosen[...], jnp.broadcast_to(offsets, (16, 2 * WIDTH)))[:, :1]
    far_place = ((iota((LATE, 128), 1) & (TOK // FAR - 1)).astype(F32) == offsets).astype(F32)
    far_place = jnp.concatenate([far_place] * OWNERS, axis=1)
    spread_rows = (iota((16, OWNERS * TOK), 1) // (TOK // FAR) == iota((16, OWNERS * TOK), 0)).astype(F32).astype(BF)

    for t in range(NY):
        arrived(far_qg.at[other, t], r_cqg.at[t])
    for t in y_peers:
        arrived(far_s.at[core, t], r_fs.at[core, t])
    for t in range(NY):
        arrived(far_s.at[other, t], r_fs.at[other, t])
    columns = joined(far_s[...])
    k_far, v_far = [], []
    for b in range(GROUPS):
        k_part, v_part = key_side(far_k, far_v, far_rows_of(far_qg, 0), far_rows_of(far_qg, 1), columns, b)
        k_far.append(through(far_inverse[b], far_unit[b], k_part))
        v_far.append(v_part)
    two_rows = [jnp.concatenate(parts, axis=1) for parts in (k_far, v_far)]
    corr[own] = packed(two_rows)
    for o in owners:
        send(corr.at[own], corr.at[own], r_corr.at[own], owner(o))

    for o in owners:
        arrived(early_in.at[o], r_early.at[o])
    for t in range(NX):
        arrived(toks.at[other * NX + t], r_ftok.at[t])
        arrived(cots.at[other * NX + t], r_fcot.at[t])

    def factors(ref, rows):
        return jnp.concatenate([ref[o, rows, :] for o in range(OWNERS)], axis=1)

    o_sum[...] = nn(factors(early_in, slice(0, NY * OOWN)), cots[...].reshape(OWNERS * TOK, WIDTH))
    tokens = toks[...].reshape(OWNERS * TOK, WIDTH)
    q_sum[: EARLY - NY * OOWN, :] = nn(factors(early_in, slice(NY * OOWN, EARLY)), tokens)

    for o in owners:
        arrived(late_in.at[o], r_late.at[o])
    for o in owners:
        arrived(corr.at[o], r_corr.at[o])
    ordered = nn(order_ref[...], corr[...].reshape(OWNERS * PACK, 128)).astype(BF)
    ordered = jnp.concatenate([ordered[16 * t : 16 * (t + 1)] for t in range(2 * TILES)], axis=1)
    added = nn(nt(chosen[...], ordered).astype(BF), spread_rows) * far_place
    late = nn((factors(late_in, slice(0, LATE)).astype(F32) + added).astype(BF), tokens)
    q_sum[QOWN:, :] = late[: (NY - 1) * QOWN]

    left, right = slice(0, CUT), slice(CUT, WIDTH)
    for t in range(NY):
        yz_part = jnp.concatenate(
            [q_sum[t * QOWN : (t + 1) * QOWN, :], o_sum[t * OOWN : (t + 1) * OOWN, :]], axis=0
        ).astype(BF)
        a_y_send[t] = yz_part[:, left]
        b_part[t * PIECE : (t + 1) * PIECE, :] = yz_part[:, right]
    for t in y_peers:
        send(a_y_send.at[t], a_y_recv.at[y], r_ay.at[y], at(t, z, core))
    a_y_recv[y] = a_y_send[y]
    dealt = nn(deal_b_ref[...], b_part[...]).astype(BF)
    for t in range(NZ):
        b_z_send[t] = dealt[48 * t : 48 * (t + 1), :]
    for t in z_peers:
        send(b_z_send.at[t], b_z_recv.at[z], r_bz.at[z], at(y, t, core))
    b_z_recv[z] = b_z_send[z]

    for i, rows in enumerate(two_rows):
        for b in range(GROUPS):
            at_lanes = lanes_of(GROUPS * (1 + i) + b)
            dqkv[:, at_lanes] = (dqkv[:, at_lanes].astype(F32) + unfar(rows[:, lanes_of(b)], b)).astype(BF)
    grad_tok_ref[...] = nn(dqkv[...], wqkv_ref[...]).astype(BF)

    for t in y_peers:
        arrived(a_y_recv.at[t], r_ay.at[t])
    part = jnp.sum(a_y_recv[...].astype(F32), axis=0)
    dealt = nn(deal_ref[...], part.astype(BF)).astype(BF)
    for t in range(NZ):
        a_z_send[t] = dealt[16 * t : 16 * (t + 1), :]
    for t in z_peers:
        send(a_z_send.at[t], a_z_recv.at[z], r_az.at[z], at(y, t, core))
    a_z_recv[z] = a_z_send[z]
    for t in z_peers:
        arrived(b_z_recv.at[t], r_bz.at[t])
    part = jnp.sum(b_z_recv[...].astype(F32), axis=0)
    dealt = nn(deal_y_ref[...], part.astype(BF)).astype(BF)
    for t in range(NY):
        b_y_send[t] = dealt[16 * t : 16 * (t + 1), :]
    for t in y_peers:
        send(b_y_send.at[t], b_y_recv.at[y], r_by.at[y], at(t, z, core))
    b_y_recv[y] = b_y_send[y]
    for columns, ref, recv, peers in ((left, a_z_recv, r_az, z_peers), (right, b_y_recv, r_by, y_peers)):
        for t in peers:
            arrived(ref.at[t], recv.at[t])
        share = jnp.sum(ref[...].astype(F32), axis=0)
        qkv_out[:, columns] = share[: QOWN // NZ]
        out_out[:, columns] = share[QOWN // NZ : PIECE // NZ]
    for copy in sent:
        copy.wait_send()


def finish(*refs):
    sources, results, held, sems = refs[:4], refs[4:8], refs[8:12], refs[12]
    inward = [pltpu.make_async_copy(sources[n], held[n], sems.at[0, n]) for n in range(4)]
    outward = [pltpu.make_async_copy(held[n], results[n], sems.at[1, n]) for n in range(4)]
    for copy in inward:
        copy.start()
    for come, go in zip(inward, outward):
        come.wait()
        go.start()
    for copy in outward:
        copy.wait()


def constants():
    lane = np.arange(WIDTH)
    block = (lane[:LANES, None] // HEAD == lane[None, :LANES] // HEAD).astype(np.float32)
    compact = np.zeros((WIDTH, 256), np.float32)
    compact[np.arange(HEADS) * HEAD, np.arange(HEADS)] = 1
    compact[lane, 128 + HEADS + lane // HEAD] = 1
    order = np.zeros((2 * TILES * 16, NZ * PACK), np.float32)
    for t in range(2):
        for j in range(TILES):
            for s in range(NZ):
                for i in range(FAR):
                    order[(t * TILES + j) * 16 + s * FAR + i, s * PACK + (t * FAR + i) * TILES + j] = 1

    def deal_out(each):
        index = np.arange(NZ * OWNERS * each).reshape(NZ, OWNERS, each).transpose(1, 0, 2).reshape(-1)
        return np.eye(index.size, dtype=np.float32)[index]

    deal = np.zeros((NZ * 16, PIECE), np.float32)
    for t in range(NZ):
        for i in range(9):
            deal[t * 16 + i, t * 9 + i] = 1
        for i in range(3):
            deal[t * 16 + 9 + i, QOWN + t * 3 + i] = 1
    deal_b = np.zeros((NZ * 48, NY * PIECE), np.float32)
    deal_y = np.zeros((NY * 16, 48), np.float32)
    for s in range(NY):
        for i in range(12):
            deal_y[s * 16 + i, s * 12 + i] = 1
            for t in range(NZ):
                deal_b[t * 48 + s * 12 + i, s * PIECE + (t * 9 + i if i < 9 else QOWN + t * 3 + i - 9)] = 1
    return [jnp.asarray(m, BF) for m in (block, compact, order, deal_out(9), deal_out(3), deal, deal_b, deal_y)]


def body(tokens, cotangent, qkv_weight, out_weight, logit_scale, near_offsets, far_offsets):
    fixed = constants()
    hbm = pl.BlockSpec(memory_space=pltpu.HBM)
    vmem = pl.BlockSpec(memory_space=pltpu.VMEM)
    dma = pltpu.SemaphoreType.DMA
    wide_bf = pltpu.VMEM((TOK, WIDTH), BF)
    wide = pltpu.VMEM((TOK, WIDTH), F32)

    def held(*shape):
        return pltpu.VMEM(shape, BF)

    def held_f32(*shape):
        return pltpu.VMEM(shape, F32)

    results = [
        jax.ShapeDtypeStruct((TOK, WIDTH), BF),
        jax.ShapeDtypeStruct((TOK, WIDTH), BF),
        jax.ShapeDtypeStruct((9, WIDTH), F32),
        jax.ShapeDtypeStruct((3, WIDTH), F32),
    ]
    values = pl.pallas_call(
        layer,
        out_shape=results,
        in_specs=[hbm] * (7 + len(fixed)),
        out_specs=[vmem] * 4,
        scratch_shapes=[
            pltpu.SMEM((HEADS,), F32), pltpu.SMEM((HEADS,), jnp.int32), pltpu.SMEM((HEADS,), jnp.int32),
            held(3 * WIDTH, WIDTH), held(WIDTH, WIDTH), *[held(*m.shape) for m in fixed],
            held(OWNERS, TOK, WIDTH), held(OWNERS, TOK, WIDTH),
            held(TOK, 3 * WIDTH), wide_bf, wide_bf, wide_bf, wide, wide,
            held_f32(HEADS * TOK, 128), held_f32(GROUPS, GROUP * 16, 128), held_f32(GROUPS, GROUP * 16, 128),
            wide, wide, wide, wide, wide, held(TOK, 3 * WIDTH), held_f32(PACK, 128),
            held(SPAN, 2, NEAR, WIDTH), held(SPAN, 2, NEAR, WIDTH), held(SPAN, NEAR, 128),
            held(NZ, PACK, 128), held(NZ, PACK, 128),
            held(2, NY, 2, 16, WIDTH), held(2, NY, 2, 16, WIDTH), held(NZ, 16, 128), held(2, NY, 16, 128),
            held(WIDTH, TOK), held(3 * WIDTH, TOK), held_f32(OWNERS, LATE, 128),
            held(OWNERS, PACK, 128), held(LATE, 2 * WIDTH),
            held(OWNERS, EARLY, 128), held(OWNERS, EARLY, 128), held(OWNERS, LATE, 128), held(OWNERS, LATE, 128),
            held_f32(NY * QOWN, WIDTH), held_f32(NY * OOWN, WIDTH),
            held(NY * PIECE, REST),
            held(NY, PIECE, CUT), held(NY, PIECE, CUT), held(NZ, 16, CUT), held(NZ, 16, CUT),
            held(NZ, 48, REST), held(NZ, 48, REST), held(NY, 16, REST), held(NY, 16, REST),
            dma((24,)), dma((128,)),
            dma((4,)), dma((4,)), dma((4,)), dma((4,)),
            dma((8,)), dma((8,)), dma((8,)), dma((8,)), dma((8,)), dma((8,)), dma((4,)), dma((4,)), dma((4,)), dma((4,)),
            dma((2, 4)), dma((8,)), dma((8,)), dma((8,)), dma((4,)), dma((8,)), dma((8,)), dma((4,)),
        ],
        compiler_params=pltpu.CompilerParams(
            collective_id=0, has_side_effects=True, vmem_limit_bytes=56 * 1024 * 1024
        ),
    )(logit_scale, near_offsets, far_offsets, tokens[0], cotangent[0], qkv_weight, out_weight, *fixed)
    branch, grad_inputs, qkv_share, out_share = pl.pallas_call(
        finish,
        out_shape=results,
        in_specs=[pl.BlockSpec(memory_space=pl.ANY)] * 4,
        out_specs=[pl.BlockSpec(memory_space=pl.ANY)] * 4,
        scratch_shapes=[pltpu.VMEM(r.shape, r.dtype) for r in results] + [dma((2, 4))],
        compiler_params=pltpu.CompilerParams(vmem_limit_bytes=56 * 1024 * 1024),
    )(*values)
    return (branch[None], grad_inputs[None], qkv_share, out_share)


def solution(mesh):
    return jax.shard_map(
        body,
        mesh=mesh,
        in_specs=(P("dp", "seq", None), P("dp", "seq", None), P(), P(), P(), P(), P()),
        out_specs=(
            P("dp", "seq", None),
            P("dp", "seq", None),
            P(("seq", "dp"), None),
            P(("seq", "dp"), None),
        ),
        check_vma=False,
    )
```

```python
import jax
import jax.numpy as jnp
import numpy as np
from jax import lax
from jax.experimental import pallas as pl
from jax.experimental.pallas import tpu as pltpu
from jax.sharding import PartitionSpec as P

BF = jnp.bfloat16
F32 = jnp.float32
MESH = pl.DeviceIdType.MESH
EPS = 1e-06

NY, NZ, NX = 4, 8, 4
TOK = 128
WIDTH = 768
HEADS = 12
HEAD = 64
GROUP = 4
LANES = GROUP * HEAD
GROUPS = HEADS // GROUP
SPAN = 8
NEAR = TOK // SPAN
FAR = 2
PACK = 32
TILES = WIDTH // 128
OWNERS = 2 * NX
CUT = 512
REST = WIDTH - CUT
QROWS = 3 * WIDTH // NY
OROWS = WIDTH // NY
QOWN, OOWN = QROWS // OWNERS, OROWS // OWNERS
PIECE = QOWN + OOWN
EARLY = 176
LATE = 224


def nn(a, b):
    return lax.dot_general(a, b, (((1,), (0,)), ((), ())), preferred_element_type=F32)


def nt(a, b):
    return lax.dot_general(a, b, (((1,), (1,)), ((), ())), preferred_element_type=F32)


def tn(a, b):
    return lax.dot_general(a, b, (((0,), (0,)), ((), ())), preferred_element_type=F32)


def split(x):
    high = x.astype(BF)
    return high, (x - high.astype(F32)).astype(BF)


def iota(shape, dim):
    return lax.broadcasted_iota(jnp.int32, shape, dim)


def place():
    seq = lax.axis_index("seq")
    return seq, lax.rem(seq, 2), lax.rem(seq // 2, NZ), seq // (2 * NZ)


def at(y, z, core):
    return {"seq": (y * NZ + z) * 2 + core}


def remote(src, dst, send, recv, device):
    return pltpu.make_async_remote_copy(
        src_ref=src, dst_ref=dst, send_sem=send, recv_sem=recv, device_id=device, device_id_type=MESH
    )


def lanes_of(b):
    return slice(b * LANES, (b + 1) * LANES)


def layer(
    scale_hbm, near_hbm, far_hbm, tok_hbm, cot_hbm, wqkv_hbm, wout_hbm,
    block_hbm, compact_hbm, order_hbm, perm_q_hbm, perm_o_hbm, deal_hbm, deal_b_hbm, deal_y_hbm,
    branch_ref, grad_tok_ref, qkv_out, out_out,
    scale_ref, near_ref, far_ref, wqkv_ref, wout_ref, block_ref, compact_ref, order_ref, perm_q, perm_o, deal_ref, deal_b_ref, deal_y_ref,
    toks, cots, qkv, qn, kn, gr, inv_q, inv_k, p_loc, p_near, p_far, num, den, dq, dk, dv, dqkv, pack,
    near_kv, near_qg, near_s, far_zkv, far_zqg, far_kv, far_qg, far_sz, far_s,
    attn_t, dqkv_t, stage, corr, chosen, early_out, early_in, late_out, late_in, q_sum, o_sum, b_part,
    a_y_send, a_y_recv, a_z_send, a_z_recv, b_z_send, b_z_recv, b_y_send, b_y_recv,
    loads, sends, r_tok, r_cot, r_ftok, r_fcot, r_nkv, r_nqg, r_ns, r_zkv, r_zqg, r_sz, r_fkv, r_fqg, r_ckv, r_cqg,
    r_fs, r_early, r_late, r_corr, r_ay, r_az, r_bz, r_by,
):
    seq, core, z, y = place()
    x = lax.axis_index("dp")
    mine = lax.rem(seq, SPAN)
    base = seq - mine
    other = 1 - core
    own = core * NX + x

    loading = []

    def load(src, dst):
        copy = pltpu.make_async_copy(src, dst, loads.at[len(loading)])
        copy.start()
        loading.append(copy)

    load(near_hbm, near_ref)
    load(far_hbm, far_ref)
    load(scale_hbm, scale_ref)
    load(tok_hbm, toks.at[own])
    load(block_hbm, block_ref)
    load(wqkv_hbm.at[WIDTH : 3 * WIDTH], wqkv_ref.at[WIDTH : 3 * WIDTH])
    load(cot_hbm, cots.at[own])
    load(wqkv_hbm.at[:WIDTH], wqkv_ref.at[:WIDTH])
    load(wout_hbm, wout_ref)

    z_peers = [lax.rem(z + d, NZ) for d in (4, 3, 5, 2, 6, 1, 7)]
    y_peers = [lax.rem(y + d, NY) for d in (2, 1, 3)]
    x_peers = [lax.rem(x + d, NX) for d in (2, 1, 3)]
    near_peers = [lax.rem(mine + d, SPAN) for d in range(1, SPAN)]
    near_same = [2 * lax.rem(mine // 2 + d, SPAN // 2) + core for d in (2, 1, 3)]
    near_other = [2 * lax.rem(mine // 2 + d, SPAN // 2) + other for d in range(SPAN // 2)]
    partner = at(y, z, other)
    pair = seq - core

    def owner(o):
        return {"seq": pair + o // NX, "dp": lax.rem(o, NX)}

    owners = [lax.rem(own + d, OWNERS) for d in (2, 6, 1, 3, 5, 7, 4)]
    barrier = pltpu.get_barrier_semaphore()
    greeted = (
        [at(y, t, core) for t in z_peers]
        + [{"seq": base + t} for t in near_other]
        + [at(t, z, core) for t in y_peers]
        + [at(t, z, other) for t in y_peers]
        + [{"seq": seq, "dp": t} for t in x_peers]
        + [{"seq": pair + other, "dp": t} for t in x_peers]
    )
    for device in greeted:
        pl.semaphore_signal(barrier, inc=1, device_id=device, device_id_type=MESH)
    sent = []

    def send(src, dst, recv, device):
        copy = remote(src, dst, sends.at[len(sent)], recv, device)
        copy.start()
        sent.append(copy)

    def arrived(ref, recv):
        remote(ref, ref, sends.at[0], recv, {"seq": seq}).wait_recv()

    head_lane = iota((1, LANES), 1) // HEAD
    picks_f = [(head_lane == h).astype(F32) for h in range(GROUP)]
    picks = [m.astype(BF) for m in picks_f]

    def spread(x):
        return jnp.concatenate([x * m for m in picks], axis=0)

    def fold(x):
        rows = x.shape[0] // GROUP
        return sum(x[h * rows : (h + 1) * rows] * picks_f[h] for h in range(GROUP))

    for copy in loading[:3]:
        copy.wait()
    wide_head = iota((1, WIDTH), 1) // HEAD
    slim_head = iota((1, 128), 1)
    slim_head = jnp.where(slim_head >= HEADS, slim_head - HEADS, slim_head)
    near_row, far_row = jnp.zeros((1, WIDTH), jnp.int32), jnp.zeros((1, WIDTH), jnp.int32)
    near_slim, far_slim = jnp.zeros((1, 128), jnp.int32), jnp.zeros((1, 128), jnp.int32)
    for h in range(HEADS):
        near_row = jnp.where(wide_head == h, near_ref[h], near_row)
        far_row = jnp.where(wide_head == h, far_ref[h], far_row)
        near_slim = jnp.where(slim_head == h, near_ref[h], near_slim)
        far_slim = jnp.where(slim_head == h, far_ref[h], far_slim)
    near_mask = ((iota((TOK, WIDTH), 0) & (SPAN - 1)) == near_row).astype(F32)
    far_mask = ((iota((TOK, WIDTH), 0) & (TOK // FAR - 1)) == far_row).astype(F32)
    near_bf, far_bf = near_mask.astype(BF), far_mask.astype(BF)
    near_slim = ((iota((TOK, 128), 0) & (SPAN - 1)) == near_slim).astype(F32).astype(BF)
    far_slim = ((iota((TOK, 128), 0) & (TOK // FAR - 1)) == far_slim).astype(F32).astype(BF)
    row, token = iota((NEAR, TOK), 0), iota((NEAR, TOK), 1)
    take_near = (token // SPAN == row).astype(F32).astype(BF)
    take_far = (token // (TOK // FAR) == row).astype(F32).astype(BF)
    take_far_z = ((row // FAR == z) & (token // (TOK // FAR) == (row & 1))).astype(F32).astype(BF)

    def unnear(x, b):
        return jnp.broadcast_to(x[:, None, :], (NEAR, SPAN, LANES)).reshape(TOK, LANES) * near_mask[:, lanes_of(b)]

    def unfar(x, b):
        rows = [jnp.broadcast_to(x[i : i + 1], (TOK // FAR, LANES)) for i in range(FAR)]
        return jnp.concatenate(rows, axis=0) * far_mask[:, lanes_of(b)]

    def norms(columns):
        wide = columns.astype(F32)
        high, low = split(wide * wide)
        inverse = lax.rsqrt(nn(high, block_ref[...]) + nn(low, block_ref[...]) + EPS)
        return inverse, wide * inverse

    far_rows = []

    def packed(pair_of):
        pack[2 * FAR * TILES :, :] = jnp.zeros((PACK - 2 * FAR * TILES, 128), F32)
        for i, picked in enumerate(pair_of):
            for r in range(FAR):
                for t in range(TILES):
                    at_row = (i * FAR + r) * TILES + t
                    pack[at_row : at_row + 1, :] = picked[r : r + 1, 128 * t : 128 * (t + 1)]
        return pack[...].astype(BF)

    def leave(pair_of, far_into, near_into):
        picked = [nn(take_far, x_ * far_bf) for x_ in pair_of]
        far_rows.extend(x_.astype(BF) for x_ in picked)
        far_into[z] = packed(picked)
        for i, x_ in enumerate(pair_of):
            near_into[mine, i] = nn(take_near, x_ * near_bf).astype(BF)

    for copy in loading[3:6]:
        copy.wait()
    tok = toks[own]
    for b in range(GROUPS, 3 * GROUPS):
        qkv[:, lanes_of(b)] = nt(tok, wqkv_ref[lanes_of(b), :]).astype(BF)
    for b in range(GROUPS):
        inverse, unit = norms(qkv[:, lanes_of(GROUPS + b)])
        inv_k[:, lanes_of(b)] = inverse
        kn[:, lanes_of(b)] = unit.astype(BF)
    pl.semaphore_wait(barrier, len(greeted))
    leave((kn[...], qkv[:, 2 * WIDTH :]), far_zkv, near_kv)
    for t in z_peers:
        send(far_zkv.at[z], far_zkv.at[z], r_zkv.at[z], at(y, t, core))
    for t in near_same:
        send(near_kv.at[mine], near_kv.at[mine], r_nkv.at[mine], {"seq": base + t})
    send(near_kv.at[mine], near_kv.at[mine], r_nkv.at[mine], partner)

    def over_x(ref, recv, forward_recv):
        for t in x_peers:
            send(ref.at[own], ref.at[own], recv.at[x], {"seq": seq, "dp": t})
        send(ref.at[own], ref.at[own], forward_recv.at[x], partner)

    over_x(toks, r_tok, r_ftok)

    first = len(loading)
    load(order_hbm, order_ref)
    load(compact_hbm, compact_ref)
    load(perm_q_hbm, perm_q)
    load(perm_o_hbm, perm_o)
    load(deal_hbm, deal_ref)
    load(deal_b_hbm, deal_b_ref)
    load(deal_y_hbm, deal_y_ref)
    for copy in loading[6:first]:
        copy.wait()
    cot = cots[own]
    for b in range(GROUPS):
        qkv[:, lanes_of(b)] = nt(tok, wqkv_ref[lanes_of(b), :]).astype(BF)
        gr[:, lanes_of(b)] = nt(cot, wout_ref[lanes_of(b), :]).astype(BF)
        inverse, unit = norms(qkv[:, lanes_of(b)])
        inv_q[:, lanes_of(b)] = inverse
        qn[:, lanes_of(b)] = unit.astype(BF)
    leave((qn[...], gr[...]), far_zqg, near_qg)
    over_x(cots, r_cot, r_fcot)

    ones = spread(jnp.ones((TOK, LANES), BF))
    for b in range(GROUPS):
        s = nt(spread(qn[:, lanes_of(b)]), kn[:, lanes_of(b)])
        ps = []
        for h in range(GROUP):
            p = jnp.exp(s[h * TOK : (h + 1) * TOK] * scale_ref[GROUP * b + h])
            p_loc[(GROUP * b + h) * TOK : (GROUP * b + h + 1) * TOK, :] = p
            ps.append(p.astype(BF))
        ps = jnp.concatenate(ps, axis=1)
        num[:, lanes_of(b)] = nn(ps, spread(qkv[:, lanes_of(2 * GROUPS + b)]))
        den[:, lanes_of(b)] = nn(ps, ones)

    for copy in loading[first:]:
        copy.wait()

    def along_y(packets, recv_z, into, recv):
        for t in z_peers:
            arrived(packets.at[t], recv_z.at[t])
        ordered = nn(order_ref[...], packets[...].reshape(NZ * PACK, 128)).astype(BF)
        for i in range(2):
            for t in range(TILES):
                first = (i * TILES + t) * 16
                into[core, y, i, :, 128 * t : 128 * (t + 1)] = ordered[first : first + 16, :]
        for t in y_peers:
            send(into.at[core, y], into.at[core, y], recv.at[y], at(t, z, core))

    def across(ref, recv):
        for t in near_same:
            arrived(ref.at[t], recv.at[t])
            send(ref.at[t], ref.at[t], recv.at[t], partner)

    def hand_over(ref, recv, recv_core):
        send(ref.at[core, y], ref.at[core, y], recv_core.at[y], partner)
        for t in y_peers:
            arrived(ref.at[core, t], recv.at[t])
            send(ref.at[core, t], ref.at[core, t], recv_core.at[t], partner)

    def forward(queries, keys, values, p_ref):
        results = []
        for b in range(GROUPS):
            s = nt(spread(queries[:, lanes_of(b)]), keys(b))
            ps = []
            for h in range(GROUP):
                ps.append(jnp.exp(s[h * 16 : (h + 1) * 16] * scale_ref[GROUP * b + h]))
            p = jnp.concatenate(ps, axis=0)
            p_ref[b] = p
            total = jnp.broadcast_to(jnp.sum(p, axis=1, keepdims=True), (GROUP * 16, LANES))
            results.append((fold(nn(p.astype(BF), values(b))), fold(total)))
        return results

    def near_rows(ref, i):
        return lambda b: jnp.concatenate([ref[s, i, :, lanes_of(b)] for s in range(SPAN)], axis=0)

    def far_rows_of(ref, i):
        return lambda b: jnp.concatenate(
            [ref[s, t, i, :, lanes_of(b)] for s in range(2) for t in range(NY)], axis=0
        )

    along_y(far_zkv, r_zkv, far_kv, r_fkv)
    across(near_kv, r_nkv)
    for t in z_peers:
        send(far_zqg.at[z], far_zqg.at[z], r_zqg.at[z], at(y, t, core))
    for t in near_same:
        send(near_qg.at[mine], near_qg.at[mine], r_nqg.at[mine], {"seq": base + t})
    send(near_qg.at[mine], near_qg.at[mine], r_nqg.at[mine], partner)
    for t in near_other:
        arrived(near_kv.at[t], r_nkv.at[t])
    near_q, near_g = near_qg[mine, 0], near_qg[mine, 1]
    for b, (n_part, d_part) in enumerate(forward(near_q, near_rows(near_kv, 0), near_rows(near_kv, 1), p_near)):
        num[:, lanes_of(b)] += unnear(n_part, b)
        den[:, lanes_of(b)] += unnear(d_part, b)
    hand_over(far_kv, r_fkv, r_ckv)
    for t in range(NY):
        arrived(far_kv.at[other, t], r_ckv.at[t])
    far_k, far_v, far_q, far_g = far_rows
    for b, (n_part, d_part) in enumerate(forward(far_q, far_rows_of(far_kv, 0), far_rows_of(far_kv, 1), p_far)):
        num[:, lanes_of(b)] += unfar(n_part, b)
        den[:, lanes_of(b)] += unfar(d_part, b)

    inverse = 1.0 / den[...]
    attn = (num[...] * inverse).astype(BF)
    high, low = split(inverse)
    slim = nn(high, compact_ref[:, :128]) + nn(low, compact_ref[:, :128])
    high, low = split(gr[...].astype(F32) * attn.astype(F32))
    slim = slim + nn(high, compact_ref[:, 128:]) + nn(low, compact_ref[:, 128:])
    high, low = split(slim)

    def take(selection, mask):
        first, second = nn(selection, high * mask), nn(selection, low * mask)
        return first + second, (first + pltpu.roll(second, 64, 1)).astype(BF)

    def joined(rows):
        columns = rows.astype(F32).reshape(TOK, 128).T
        return columns[:64] + columns[64:]

    far_sz[z] = take(take_far_z, far_slim)[1]
    for t in z_peers:
        send(far_sz.at[z], far_sz.at[z], r_sz.at[z], at(y, t, core))
    near_slim_rows, near_s[mine] = take(take_near, near_slim)
    far_slim_rows = take(take_far, far_slim)[0]
    for t in near_peers:
        send(near_s.at[mine], near_s.at[mine], r_ns.at[mine], {"seq": base + t})
    along_y(far_zqg, r_zqg, far_qg, r_fqg)

    for b in range(GROUPS):
        g = spread(gr[:, lanes_of(b)])
        grad_p = nt(g, qkv[:, lanes_of(2 * GROUPS + b)])
        ps, ds = [], []
        for h in range(GROUP):
            n = GROUP * b + h
            p = p_loc[n * TOK : (n + 1) * TOK, :] * slim[:, n : n + 1]
            d = scale_ref[n] * p * (grad_p[h * TOK : (h + 1) * TOK] - slim[:, HEADS + n : HEADS + n + 1])
            ps.append(p.astype(BF))
            ds.append(d.astype(BF))
        dq[:, lanes_of(b)] = nn(jnp.concatenate(ds, axis=1), spread(kn[:, lanes_of(b)]))
        dk[:, lanes_of(b)] = tn(jnp.concatenate(ds, axis=0), spread(qn[:, lanes_of(b)]))
        dv[:, lanes_of(b)] = tn(jnp.concatenate(ps, axis=0), g)

    def query_side(grads, keys, values, p_ref, slim_rows, b):
        grad_p = nt(spread(grads[:, lanes_of(b)]), values(b))
        ds = []
        for h in range(GROUP):
            n = GROUP * b + h
            p = p_ref[b, h * 16 : (h + 1) * 16, :] * slim_rows[:, n : n + 1]
            ds.append(
                scale_ref[n] * p * (grad_p[h * 16 : (h + 1) * 16] - slim_rows[:, HEADS + n : HEADS + n + 1])
            )
        return fold(nn(jnp.concatenate(ds, axis=0).astype(BF), keys(b)))

    for b in range(GROUPS):
        near_part = query_side(near_g, near_rows(near_kv, 0), near_rows(near_kv, 1), p_near, near_slim_rows, b)
        far_part = query_side(far_g, far_rows_of(far_kv, 0), far_rows_of(far_kv, 1), p_far, far_slim_rows, b)
        dq[:, lanes_of(b)] += unnear(near_part, b) + unfar(far_part, b)

    def through(inverse, unit, d):
        high, low = split(unit * d)
        along = nn(high, block_ref[...]) + nn(low, block_ref[...])
        return inverse * (d - unit * along)

    def unnormalize(inv_ref, grad, i):
        for b in range(GROUPS):
            inverse = inv_ref[:, lanes_of(b)]
            unit = qkv[:, lanes_of(GROUPS * i + b)].astype(F32) * inverse
            dqkv[:, lanes_of(GROUPS * i + b)] = through(inverse, unit, grad[:, lanes_of(b)]).astype(BF)

    unnormalize(inv_q, dq, 0)
    attn_t[...] = attn.T
    dqkv_t[:WIDTH, :] = dqkv[:, :WIDTH].T
    for t in range(NY):
        dealt = nn(perm_o[...], attn_t[t * OROWS : (t + 1) * OROWS, :])
        for o in range(OWNERS):
            stage[o, t * OOWN : (t + 1) * OOWN, :] = dealt[o * OOWN : (o + 1) * OOWN]

    def deal_rows(t, first):
        dealt = nn(perm_q[...], dqkv_t[t * QROWS : (t + 1) * QROWS, :])
        for o in range(OWNERS):
            stage[o, first : first + QOWN, :] = dealt[o * QOWN : (o + 1) * QOWN]

    deal_rows(0, NY * OOWN)
    for o in range(OWNERS):
        stage[o, EARLY - 8 : EARLY, :] = jnp.zeros((8, 128), F32)
    early_out[...] = stage[:, :EARLY, :].astype(BF)
    for o in owners:
        send(early_out.at[o], early_in.at[own], r_early.at[own], owner(o))
    early_in[own] = early_out[own]

    def key_side(keys, values, queries, grads, columns, b):
        q, g = queries(b), grads(b)
        s = nt(spread(keys[:, lanes_of(b)]), q)
        grad_p = nt(spread(values[:, lanes_of(b)]), g)
        ps, ds = [], []
        for h in range(GROUP):
            n = GROUP * b + h
            p = jnp.exp(s[h * 16 : (h + 1) * 16] * scale_ref[n]) * columns[n : n + 1, :]
            ps.append(p)
            ds.append(
                scale_ref[n] * p * (grad_p[h * 16 : (h + 1) * 16] - columns[HEADS + n : HEADS + n + 1, :])
            )
        p, d = jnp.concatenate(ps, axis=0).astype(BF), jnp.concatenate(ds, axis=0).astype(BF)
        return fold(nn(d, q)), fold(nn(p, g))

    across(near_qg, r_nqg)
    for t in near_peers:
        arrived(near_s.at[t], r_ns.at[t])
    for t in near_other:
        arrived(near_qg.at[t], r_nqg.at[t])
    columns = joined(near_s[...])
    near_k, near_v = near_kv[mine, 0], near_kv[mine, 1]
    for b in range(GROUPS):
        k_part, v_part = key_side(near_k, near_v, near_rows(near_qg, 0), near_rows(near_qg, 1), columns, b)
        dk[:, lanes_of(b)] += unnear(k_part, b)
        dv[:, lanes_of(b)] += unnear(v_part, b)

    for t in z_peers:
        arrived(far_sz.at[t], r_sz.at[t])
    far_s[core, y] = jnp.sum(far_sz[...].astype(F32), axis=0).astype(BF)
    for t in y_peers:
        send(far_s.at[core, y], far_s.at[core, y], r_fs.at[core, y], at(t, z, core))
        send(far_s.at[core, y], far_s.at[core, y], r_fs.at[core, y], at(t, z, other))
    send(far_s.at[core, y], far_s.at[core, y], r_fs.at[core, y], partner)

    unnormalize(inv_k, dk, 1)
    dqkv[:, 2 * WIDTH :] = dv[...].astype(BF)
    dqkv_t[WIDTH:, :] = dqkv[:, WIDTH:].T
    for t in range(1, NY):
        deal_rows(t, (t - 1) * QOWN)
    for o in range(OWNERS):
        stage[o, LATE - 8 : LATE, :] = jnp.zeros((8, 128), F32)
    late_out[...] = stage[...].astype(BF)
    for o in owners:
        send(late_out.at[o], late_in.at[own], r_late.at[own], owner(o))
    late_in[own] = late_out[own]

    hand_over(far_qg, r_fqg, r_cqg)
    branch_ref[...] = nn(attn, wout_ref[...]).astype(BF)
    for all_, recv, forward_recv in ((toks, r_tok, r_ftok), (cots, r_cot, r_fcot)):
        for t in x_peers:
            arrived(all_.at[core * NX + t], recv.at[t])
            send(all_.at[core * NX + t], all_.at[core * NX + t], forward_recv.at[t], partner)

    far_inverse, far_unit = [], []
    for b in range(GROUPS):
        high, low = split(inv_k[:, lanes_of(b)])
        mask = far_bf[:, lanes_of(b)]
        inverse = nn(take_far, high * mask) + nn(take_far, low * mask)
        far_inverse.append(inverse)
        far_unit.append(nn(take_far, qkv[:, lanes_of(GROUPS + b)] * mask) * inverse)
    n = iota((LATE, 1), 0)
    t = sum((n >= QOWN * i).astype(jnp.int32) for i in range(1, NY - 1))
    left = n - QOWN * t
    u = sum((left >= QOWN // NZ * i).astype(jnp.int32) for i in range(1, NZ))
    column = QROWS * (1 + t) + (QROWS // NZ) * u + (QOWN // NZ) * own + (left - QOWN // NZ * u) - WIDTH
    column = jnp.where(n < QOWN * (NY - 1), column, -1)
    chosen[...] = (iota((LATE, 2 * WIDTH), 1) == column).astype(F32).astype(BF)
    offsets = jnp.concatenate([far_row, far_row], axis=1).astype(F32).astype(BF)
    offsets = nt(chosen[...], jnp.broadcast_to(offsets, (16, 2 * WIDTH)))[:, :1]
    far_place = ((iota((LATE, 128), 1) & (TOK // FAR - 1)).astype(F32) == offsets).astype(F32)
    far_place = jnp.concatenate([far_place] * OWNERS, axis=1)
    spread_rows = (iota((16, OWNERS * TOK), 1) // (TOK // FAR) == iota((16, OWNERS * TOK), 0)).astype(F32).astype(BF)

    for t in range(NY):
        arrived(far_qg.at[other, t], r_cqg.at[t])
    for t in y_peers:
        arrived(far_s.at[core, t], r_fs.at[core, t])
    for t in range(NY):
        arrived(far_s.at[other, t], r_fs.at[other, t])
    columns = joined(far_s[...])
    k_far, v_far = [], []
    for b in range(GROUPS):
        k_part, v_part = key_side(far_k, far_v, far_rows_of(far_qg, 0), far_rows_of(far_qg, 1), columns, b)
        k_far.append(through(far_inverse[b], far_unit[b], k_part))
        v_far.append(v_part)
    two_rows = [jnp.concatenate(parts, axis=1) for parts in (k_far, v_far)]
    corr[own] = packed(two_rows)
    for o in owners:
        send(corr.at[own], corr.at[own], r_corr.at[own], owner(o))

    for o in owners:
        arrived(early_in.at[o], r_early.at[o])
    for t in range(NX):
        arrived(toks.at[other * NX + t], r_ftok.at[t])
        arrived(cots.at[other * NX + t], r_fcot.at[t])

    def factors(ref, rows):
        return jnp.concatenate([ref[o, rows, :] for o in range(OWNERS)], axis=1)

    o_sum[...] = nn(factors(early_in, slice(0, NY * OOWN)), cots[...].reshape(OWNERS * TOK, WIDTH))
    tokens = toks[...].reshape(OWNERS * TOK, WIDTH)
    q_sum[: EARLY - NY * OOWN, :] = nn(factors(early_in, slice(NY * OOWN, EARLY)), tokens)

    for o in owners:
        arrived(late_in.at[o], r_late.at[o])
    for o in owners:
        arrived(corr.at[o], r_corr.at[o])
    ordered = nn(order_ref[...], corr[...].reshape(OWNERS * PACK, 128)).astype(BF)
    ordered = jnp.concatenate([ordered[16 * t : 16 * (t + 1)] for t in range(2 * TILES)], axis=1)
    added = nn(nt(chosen[...], ordered).astype(BF), spread_rows) * far_place
    late = nn((factors(late_in, slice(0, LATE)).astype(F32) + added).astype(BF), tokens)
    q_sum[QOWN:, :] = late[: (NY - 1) * QOWN]

    left, right = slice(0, CUT), slice(CUT, WIDTH)
    for t in range(NY):
        yz_part = jnp.concatenate(
            [q_sum[t * QOWN : (t + 1) * QOWN, :], o_sum[t * OOWN : (t + 1) * OOWN, :]], axis=0
        ).astype(BF)
        a_y_send[t] = yz_part[:, left]
        b_part[t * PIECE : (t + 1) * PIECE, :] = yz_part[:, right]
    for t in y_peers:
        send(a_y_send.at[t], a_y_recv.at[y], r_ay.at[y], at(t, z, core))
    a_y_recv[y] = a_y_send[y]
    dealt = nn(deal_b_ref[...], b_part[...]).astype(BF)
    for t in range(NZ):
        b_z_send[t] = dealt[48 * t : 48 * (t + 1), :]
    for t in z_peers:
        send(b_z_send.at[t], b_z_recv.at[z], r_bz.at[z], at(y, t, core))
    b_z_recv[z] = b_z_send[z]

    for i, rows in enumerate(two_rows):
        for b in range(GROUPS):
            at_lanes = lanes_of(GROUPS * (1 + i) + b)
            dqkv[:, at_lanes] = (dqkv[:, at_lanes].astype(F32) + unfar(rows[:, lanes_of(b)], b)).astype(BF)
    grad_tok_ref[...] = nn(dqkv[...], wqkv_ref[...]).astype(BF)

    for t in y_peers:
        arrived(a_y_recv.at[t], r_ay.at[t])
    part = jnp.sum(a_y_recv[...].astype(F32), axis=0)
    dealt = nn(deal_ref[...], part.astype(BF)).astype(BF)
    for t in range(NZ):
        a_z_send[t] = dealt[16 * t : 16 * (t + 1), :]
    for t in z_peers:
        send(a_z_send.at[t], a_z_recv.at[z], r_az.at[z], at(y, t, core))
    a_z_recv[z] = a_z_send[z]
    for t in z_peers:
        arrived(b_z_recv.at[t], r_bz.at[t])
    part = jnp.sum(b_z_recv[...].astype(F32), axis=0)
    dealt = nn(deal_y_ref[...], part.astype(BF)).astype(BF)
    for t in range(NY):
        b_y_send[t] = dealt[16 * t : 16 * (t + 1), :]
    for t in y_peers:
        send(b_y_send.at[t], b_y_recv.at[y], r_by.at[y], at(t, z, core))
    b_y_recv[y] = b_y_send[y]
    for columns, ref, recv, peers in ((left, a_z_recv, r_az, z_peers), (right, b_y_recv, r_by, y_peers)):
        for t in peers:
            arrived(ref.at[t], recv.at[t])
        share = jnp.sum(ref[...].astype(F32), axis=0)
        qkv_out[:, columns] = share[: QOWN // NZ]
        out_out[:, columns] = share[QOWN // NZ : PIECE // NZ]
    for copy in sent:
        copy.wait_send()


def finish(*refs):
    sources, results, held, sems = refs[:4], refs[4:8], refs[8:12], refs[12]
    inward = [pltpu.make_async_copy(sources[n], held[n], sems.at[0, n]) for n in range(4)]
    outward = [pltpu.make_async_copy(held[n], results[n], sems.at[1, n]) for n in range(4)]
    for copy in inward:
        copy.start()
    for come, go in zip(inward, outward):
        come.wait()
        go.start()
    for copy in outward:
        copy.wait()


def constants():
    lane = np.arange(WIDTH)
    block = (lane[:LANES, None] // HEAD == lane[None, :LANES] // HEAD).astype(np.float32)
    compact = np.zeros((WIDTH, 256), np.float32)
    compact[np.arange(HEADS) * HEAD, np.arange(HEADS)] = 1
    compact[lane, 128 + HEADS + lane // HEAD] = 1
    order = np.zeros((2 * TILES * 16, NZ * PACK), np.float32)
    for t in range(2):
        for j in range(TILES):
            for s in range(NZ):
                for i in range(FAR):
                    order[(t * TILES + j) * 16 + s * FAR + i, s * PACK + (t * FAR + i) * TILES + j] = 1

    def deal_out(each):
        index = np.arange(NZ * OWNERS * each).reshape(NZ, OWNERS, each).transpose(1, 0, 2).reshape(-1)
        return np.eye(index.size, dtype=np.float32)[index]

    deal = np.zeros((NZ * 16, PIECE), np.float32)
    for t in range(NZ):
        for i in range(9):
            deal[t * 16 + i, t * 9 + i] = 1
        for i in range(3):
            deal[t * 16 + 9 + i, QOWN + t * 3 + i] = 1
    deal_b = np.zeros((NZ * 48, NY * PIECE), np.float32)
    deal_y = np.zeros((NY * 16, 48), np.float32)
    for s in range(NY):
        for i in range(12):
            deal_y[s * 16 + i, s * 12 + i] = 1
            for t in range(NZ):
                deal_b[t * 48 + s * 12 + i, s * PIECE + (t * 9 + i if i < 9 else QOWN + t * 3 + i - 9)] = 1
    return [jnp.asarray(m, BF) for m in (block, compact, order, deal_out(9), deal_out(3), deal, deal_b, deal_y)]


def body(tokens, cotangent, qkv_weight, out_weight, logit_scale, near_offsets, far_offsets):
    fixed = constants()
    hbm = pl.BlockSpec(memory_space=pltpu.HBM)
    vmem = pl.BlockSpec(memory_space=pltpu.VMEM)
    dma = pltpu.SemaphoreType.DMA
    wide_bf = pltpu.VMEM((TOK, WIDTH), BF)
    wide = pltpu.VMEM((TOK, WIDTH), F32)

    def held(*shape):
        return pltpu.VMEM(shape, BF)

    def held_f32(*shape):
        return pltpu.VMEM(shape, F32)

    results = [
        jax.ShapeDtypeStruct((TOK, WIDTH), BF),
        jax.ShapeDtypeStruct((TOK, WIDTH), BF),
        jax.ShapeDtypeStruct((9, WIDTH), F32),
        jax.ShapeDtypeStruct((3, WIDTH), F32),
    ]
    values = pl.pallas_call(
        layer,
        out_shape=results,
        in_specs=[hbm] * (7 + len(fixed)),
        out_specs=[vmem] * 4,
        scratch_shapes=[
            pltpu.SMEM((HEADS,), F32), pltpu.SMEM((HEADS,), jnp.int32), pltpu.SMEM((HEADS,), jnp.int32),
            held(3 * WIDTH, WIDTH), held(WIDTH, WIDTH), *[held(*m.shape) for m in fixed],
            held(OWNERS, TOK, WIDTH), held(OWNERS, TOK, WIDTH),
            held(TOK, 3 * WIDTH), wide_bf, wide_bf, wide_bf, wide, wide,
            held_f32(HEADS * TOK, 128), held_f32(GROUPS, GROUP * 16, 128), held_f32(GROUPS, GROUP * 16, 128),
            wide, wide, wide, wide, wide, held(TOK, 3 * WIDTH), held_f32(PACK, 128),
            held(SPAN, 2, NEAR, WIDTH), held(SPAN, 2, NEAR, WIDTH), held(SPAN, NEAR, 128),
            held(NZ, PACK, 128), held(NZ, PACK, 128),
            held(2, NY, 2, 16, WIDTH), held(2, NY, 2, 16, WIDTH), held(NZ, 16, 128), held(2, NY, 16, 128),
            held(WIDTH, TOK), held(3 * WIDTH, TOK), held_f32(OWNERS, LATE, 128),
            held(OWNERS, PACK, 128), held(LATE, 2 * WIDTH),
            held(OWNERS, EARLY, 128), held(OWNERS, EARLY, 128), held(OWNERS, LATE, 128), held(OWNERS, LATE, 128),
            held_f32(NY * QOWN, WIDTH), held_f32(NY * OOWN, WIDTH),
            held(NY * PIECE, REST),
            held(NY, PIECE, CUT), held(NY, PIECE, CUT), held(NZ, 16, CUT), held(NZ, 16, CUT),
            held(NZ, 48, REST), held(NZ, 48, REST), held(NY, 16, REST), held(NY, 16, REST),
            dma((24,)), dma((128,)),
            dma((4,)), dma((4,)), dma((4,)), dma((4,)),
            dma((8,)), dma((8,)), dma((8,)), dma((8,)), dma((8,)), dma((8,)), dma((4,)), dma((4,)), dma((4,)), dma((4,)),
            dma((2, 4)), dma((8,)), dma((8,)), dma((8,)), dma((4,)), dma((8,)), dma((8,)), dma((4,)),
        ],
        compiler_params=pltpu.CompilerParams(
            collective_id=0, has_side_effects=True, vmem_limit_bytes=56 * 1024 * 1024
        ),
    )(logit_scale, near_offsets, far_offsets, tokens[0], cotangent[0], qkv_weight, out_weight, *fixed)
    branch, grad_inputs, qkv_share, out_share = pl.pallas_call(
        finish,
        out_shape=results,
        in_specs=[pl.BlockSpec(memory_space=pl.ANY)] * 4,
        out_specs=[pl.BlockSpec(memory_space=pl.ANY)] * 4,
        scratch_shapes=[pltpu.VMEM(r.shape, r.dtype) for r in results] + [dma((2, 4))],
        compiler_params=pltpu.CompilerParams(vmem_limit_bytes=56 * 1024 * 1024),
    )(*values)
    return (branch[None], grad_inputs[None], qkv_share, out_share)


def solution(mesh):
    return jax.shard_map(
        body,
        mesh=mesh,
        in_specs=(P("dp", "seq", None), P("dp", "seq", None), P(), P(), P(), P(), P()),
        out_specs=(
            P("dp", "seq", None),
            P("dp", "seq", None),
            P(("seq", "dp"), None),
            P(("seq", "dp"), None),
        ),
        check_vma=False,
    )
```
